32 devices in a mesh: dp: 8 (over y, x, core), cp: 4 (over z).
Axes of the slice: x: 2, y: 2, z: 4, core: 2. Of those that a mesh axis runs over, the one named last changes fastest.
Arguments:
- block_input: bfloat16 [16, 1024, 1024], P('dp', 'cp'), may hold values from -6 to 6
- mixer_gain: bfloat16 [1024], P(('dp', 'cp')), may hold values from 0.5 to 1.5
- qkv_weight: bfloat16 [1024, 3072], P(('dp', 'cp')), may hold values from -0.1875 to 0.1875
- conv_taps: bfloat16 [4, 3072], P(None, ('dp', 'cp')), may hold values from -3 to 3
- beta_weight: bfloat16 [1024, 8], P(('dp', 'cp')), may hold values from -0.1875 to 0.1875
- out_gain: bfloat16 [128], replicated, may hold values from 0.5 to 1.5
- proj_weight: bfloat16 [1024, 1024], P(('dp', 'cp')), may hold values from -0.1875 to 0.1875
- ffn_gain: bfloat16 [1024], P(('dp', 'cp')), may hold values from 0.5 to 1.5
- gate_up: bfloat16 [1024, 5632], P(('dp', 'cp')), may hold values from -0.1875 to 0.1875
- down_weight: bfloat16 [2816, 1024], P(('dp', 'cp')), may hold values from -0.109375 to 0.109375
- cotangent: bfloat16 [16, 1024, 1024], P('dp', 'cp'), may hold values from -6 to 6
Outputs:
- block_output: bfloat16 [16, 1024, 1024], P('dp', 'cp')
- grad_input: float32 [16, 1024, 1024], P('dp', 'cp')
- grad_mixer: float32 [1024], P(('dp', 'cp'))
- grad_qkv: float32 [1024, 3072], P(('dp', 'cp'))
- grad_conv: float32 [4, 3072], P(None, ('dp', 'cp'))
- grad_beta: float32 [1024, 8], P(('dp', 'cp'))
- grad_out: float32 [128], replicated
- grad_proj: float32 [1024, 1024], P(('dp', 'cp'))
- grad_ffn: float32 [1024], P(('dp', 'cp'))
- grad_gateup: float32 [1024, 5632], P(('dp', 'cp'))
- grad_down: float32 [2816, 1024], P(('dp', 'cp'))
- rms_values: float32 [3], replicated
The draws below stay inside these ranges and needn't reach their ends.
All inputs are finite; a program needn't handle non-finite values.
Results may differ from the reference program's by a relative error of at most 0.018.
Values may be sent and summed in bfloat16 or wider, within the bound.
No kernel may reach another device: no remote copies, remote signals or barrier semaphores. Data moves between devices by JAX's collectives and lax.ppermute only.
A program may use at most 192 MiB of HBM per device.

```python
import jax
import jax.numpy as jnp
from jax import lax

D = 1024
HEADS = 8
HEAD_DIM = 128
KW = 4
FF = 2816
GROUP = 64
SEQS = 16
LEN = 1024


def shard_levels(stream_key, extent, cuts, low, high):
    def one(dim, parts):
        heights = jax.random.uniform(jax.random.fold_in(jax.random.fold_in(stream_key, 6), dim), (parts,), jnp.float32, low / len(cuts), high / len(cuts))
        return jnp.repeat(jnp.exp(heights), extent[dim] // parts).reshape((-1,) + (1,) * (len(extent) - dim - 1))

    level = one(*cuts[0])
    for cut in cuts[1:]:
        level = level * one(*cut)
    return level


def noise(rng, dims, scale, most, cuts=(), kind=jnp.bfloat16):
    level = shard_levels(rng, dims, cuts, -0.22, 0.18) if cuts else 1.0
    values = jax.random.normal(rng, dims, jnp.float32) * scale * level
    return jnp.minimum(jnp.maximum(values, -most), most).astype(kind)


def setup_inputs(seed: int = 0) -> dict:
    arg_keys = jax.random.split(jax.random.key(seed), 12)
    block_input = noise(arg_keys[0], (SEQS, LEN, D), 1.0, 6.0, ((0, 8), (1, 4)))
    mixer_gain = jnp.clip(1.0 + 0.1 * jax.random.normal(arg_keys[1], (D,), jnp.float32), 0.5, 1.5).astype(jnp.bfloat16)
    qkv_weight = noise(arg_keys[2], (D, 3 * D), D ** -0.5, 0.1875, ((0, 32),))
    conv_taps = noise(arg_keys[3], (KW, 3 * D), KW ** -0.5, 3.0, ((1, 32),))
    beta_weight = noise(arg_keys[4], (D, HEADS), D ** -0.5, 0.1875, ((0, 32),))
    out_gain = jnp.clip(1.0 + 0.1 * jax.random.normal(arg_keys[5], (HEAD_DIM,), jnp.float32), 0.5, 1.5).astype(jnp.bfloat16)
    proj_weight = noise(arg_keys[6], (D, D), D ** -0.5, 0.1875, ((0, 32),))
    ffn_gain = jnp.clip(1.0 + 0.1 * jax.random.normal(arg_keys[7], (D,), jnp.float32), 0.5, 1.5).astype(jnp.bfloat16)
    gate_up = noise(arg_keys[8], (D, 2 * FF), D ** -0.5, 0.1875, ((0, 32),))
    down_weight = noise(arg_keys[9], (FF, D), FF ** -0.5, 0.109375, ((0, 32),))
    cotangent = noise(arg_keys[10], (SEQS, LEN, D), 1.0, 6.0, ((0, 8), (1, 4)))
    return dict(block_input=block_input, mixer_gain=mixer_gain, qkv_weight=qkv_weight, conv_taps=conv_taps, beta_weight=beta_weight, out_gain=out_gain, proj_weight=proj_weight, ffn_gain=ffn_gain, gate_up=gate_up, down_weight=down_weight, cotangent=cotangent)


@jax.custom_vjp
def low(v):
    return lax.optimization_barrier(v.astype(jnp.bfloat16)).astype(jnp.float32)

@jax.custom_vjp
def low_back(v):
    return v

def low_keep(v):
    return (low(v), None)

def low_pass(kept, grad):
    return (grad,)

def back_keep(v):
    return (v, None)

def back_low(kept, grad):
    return (low(grad),)
low.defvjp(low_keep, low_pass)
low_back.defvjp(back_keep, back_low)
norm_eps = 1e-05
unit_eps = 1e-06

def matmul_high(left, right):
    return jnp.dot(left.astype(jnp.float32), right.astype(jnp.float32), precision=lax.Precision.HIGHEST, preferred_element_type=jnp.float32)

def rms_norm(rows, gain):
    return rows * lax.rsqrt(lax.optimization_barrier(jnp.mean(rows * rows, axis=-1, keepdims=True)) + norm_eps) * gain

def mixer_inputs(extended, taps):
    width = taps.shape[0]
    count = extended.shape[-2] - width + 1
    conv = taps[0] * extended[..., 0:count, :]
    for lag in range(1, width):
        conv = conv + taps[lag] * extended[..., lag:lag + count, :]
    active = jax.nn.silu(conv)
    model = active.shape[-1] // 3
    shape = active.shape[:-1] + (HEADS, model // HEADS)
    query = active[..., :model].reshape(shape)
    keys = active[..., model:2 * model].reshape(shape)
    values = active[..., 2 * model:].reshape(shape)
    depth = shape[-1]
    query = query * lax.rsqrt(lax.optimization_barrier(jnp.sum(query * query, axis=-1, keepdims=True)) + unit_eps) * depth ** (-0.5)
    keys = keys * lax.rsqrt(lax.optimization_barrier(jnp.sum(keys * keys, axis=-1, keepdims=True)) + unit_eps)
    return (query, keys, values)

def group_system(key_heads, rate_heads):
    size = key_heads.shape[1]
    strict = jnp.tril(jnp.ones((size, size), jnp.float32), -1)
    inner = jnp.einsum('hcd,hed->hce', key_heads, key_heads, precision=lax.Precision.HIGHEST)
    return jnp.eye(size, dtype=jnp.float32) + strict * (rate_heads[:, :, None] * inner)

def group_step(state, query, keys, values, rates):
    query_heads = jnp.swapaxes(query, 0, 1)
    key_heads = jnp.swapaxes(keys, 0, 1)
    value_heads = jnp.swapaxes(values, 0, 1)
    rate_heads = jnp.swapaxes(rates, 0, 1)
    size = key_heads.shape[1]
    system = group_system(key_heads, rate_heads)
    recalled = jnp.einsum('hcd,hde->hce', key_heads, state, precision=lax.Precision.HIGHEST)
    errors = jax.scipy.linalg.solve_triangular(system, rate_heads[:, :, None] * (value_heads - recalled), lower=True)
    causal = jnp.tril(jnp.ones((size, size), jnp.float32), 0)
    scores = jnp.einsum('hcd,hed->hce', query_heads, key_heads, precision=lax.Precision.HIGHEST) * causal
    output = jnp.einsum('hcd,hde->hce', query_heads, state, precision=lax.Precision.HIGHEST)
    output = output + jnp.einsum('hce,hef->hcf', scores, errors, precision=lax.Precision.HIGHEST)
    state = state + jnp.einsum('hcd,hce->hde', key_heads, errors, precision=lax.Precision.HIGHEST)
    return (state, jnp.swapaxes(output, 0, 1))

def delta_rule(state, query, keys, values, rates, block):
    count = query.shape[0] // block

    def split(array):
        return array.reshape((count, block) + array.shape[1:])

    def advance(carry, items):
        return group_step(carry, items[0], items[1], items[2], items[3])
    final, outputs = lax.scan(jax.checkpoint(advance), state, (split(query), split(keys), split(values), split(rates)))
    return (outputs.reshape(query.shape), final)

def block_forward(rows, gain_one, w_qkv, taps, w_beta, gain_out, w_proj, gain_two, w_gateup, w_down):
    normed_one = low(rms_norm(rows, gain_one))
    projected = low_back(low(matmul_high(normed_one, w_qkv)))
    pad_rows = jnp.zeros((taps.shape[0] - 1, projected.shape[1]), jnp.float32)
    extended = jnp.concatenate([pad_rows, projected], axis=0)
    query, keys, values = mixer_inputs(extended, taps)
    rates = jax.nn.sigmoid(matmul_high(normed_one, w_beta))
    depth = query.shape[-1]
    start = jnp.zeros((HEADS, depth, depth), jnp.float32)
    mixed, final = delta_rule(start, low(query), low(keys), low(values), rates, GROUP)
    normed_mix = rms_norm(mixed, gain_out)
    mixed_low = low_back(low(normed_mix.reshape(rows.shape)))
    attn = matmul_high(mixed_low, w_proj)
    middle = rows + attn
    normed_two = low(rms_norm(middle, gain_two))
    gates = low_back(matmul_high(normed_two, w_gateup))
    hidden = low(jax.nn.silu(gates[:, :FF]) * gates[:, FF:])
    ffn_out = matmul_high(hidden, w_down)
    return (middle + ffn_out, (attn, ffn_out))

def reference(block_input, mixer_gain, qkv_weight, conv_taps, beta_weight, out_gain, proj_weight, ffn_gain, gate_up, down_weight, cotangent):
    params = tuple((weight.astype(jnp.float32) for weight in (mixer_gain, qkv_weight, conv_taps, beta_weight, out_gain, proj_weight, ffn_gain, gate_up, down_weight)))

    def per_sequence(carry, items):
        totals, squares = carry
        sequence, upstream = items
        result, pullback, extras = jax.vjp(block_forward, sequence, *params, has_aux=True)
        grads = pullback(upstream)
        totals = tuple((total + grad for total, grad in zip(totals, grads[1:])))
        attn, ffn_out = extras
        squares = squares + jnp.stack([jnp.sum(result * result), jnp.sum(attn * attn), jnp.sum(ffn_out * ffn_out)])
        return ((totals, squares), (result.astype(jnp.bfloat16), grads[0]))
    start = (tuple((jnp.zeros_like(weight) for weight in params)), jnp.zeros((3,), jnp.float32))
    (totals, squares), (outputs, input_grads) = lax.scan(per_sequence, start, (block_input.astype(jnp.float32), cotangent.astype(jnp.float32)))
    rms_values = jnp.sqrt(squares / (SEQS * LEN * D))
    return (outputs, input_grads, totals[0], totals[1], totals[2], totals[3], totals[4], totals[5], totals[6], totals[7], totals[8], rms_values)
```

```python
import functools

import jax
import jax.numpy as jnp
from jax import lax
from jax.experimental import pallas as pl
from jax.experimental.pallas import tpu as pltpu
from jax.sharding import PartitionSpec as P

HEADS = 8
PAIR = 4

norm_eps = 1e-05
unit_eps = 1e-06
F32 = jnp.float32
BF16 = jnp.bfloat16


def halves(value):
    high = value.astype(BF16)
    return high, (value - high.astype(F32)).astype(BF16)


NN = (((1,), (0,)), ((), ()))
NT = (((1,), (1,)), ((), ()))
TN = (((0,), (0,)), ((), ()))


def mul(left, right, dims):
    return lax.dot_general(left, right, dims, preferred_element_type=F32)


def mul_split(left, right, dims):
    return (
        mul(left[0], right[0], dims) + mul(left[0], right[1], dims) + mul(left[1], right[0], dims)
    )


def mul_high(left, right, dims):
    left = (left,) if left.dtype == BF16 else halves(left)
    right = (right,) if right.dtype == BF16 else halves(right)
    total = mul(left[0], right[0], dims)
    if len(right) == 2:
        total = total + mul(left[0], right[1], dims)
    if len(left) == 2:
        total = total + mul(left[1], right[0], dims)
    return total


def shifted_down(rows, before, by):
    if by == 0:
        return rows
    rolled = pltpu.roll(rows, by, 0)
    top = pltpu.roll(before, by, 0)
    index = lax.broadcasted_iota(jnp.int32, before.shape, 0)
    first = jnp.where(index < by, top, rolled[: before.shape[0]])
    return jnp.concatenate([first, rolled[before.shape[0] :]], axis=0)


def shifted_up(rows, by):
    if by == 0:
        return rows
    count = rows.shape[0]
    index = lax.broadcasted_iota(jnp.int32, rows.shape, 0)
    return jnp.where(index < count - by, pltpu.roll(rows, count - by, 0), 0.0)


def conv_parts(rows, before, taps):
    width = taps.shape[0]
    conv = None
    for lag in range(width):
        term = taps[lag : lag + 1] * shifted_down(rows, before, width - 1 - lag)
        conv = term if conv is None else conv + term
    return conv


def unit_scale(active):
    return lax.rsqrt(jnp.sum(active * active, axis=-1, keepdims=True) + unit_eps)


def column_of(rates, head):
    index = lax.broadcasted_iota(jnp.int32, rates.shape, 1)
    return jnp.sum(jnp.where(index == head, rates, 0.0), axis=1, keepdims=True)


def row_of(rates, head):
    index = lax.broadcasted_iota(jnp.int32, rates.shape, 0)
    return jnp.sum(jnp.where(index == head, rates, 0.0), axis=0, keepdims=True)


def forward_kernel(
    q_ref, k_ref, v_ref, qb_ref, kb_ref, vb_ref, qt_ref, kt_ref, vt_ref, rates_ref, flipped_ref,
    inverse_ref, updates_ref, weights_ref, reach_ref, mixed_ref, transfer_ref, offset_ref,
):
    depth = transfer_ref.shape[-1]
    size = q_ref.shape[1]
    first = pl.program_id(1) * PAIR
    row = lax.broadcasted_iota(jnp.int32, (size, size), 0)
    col = lax.broadcasted_iota(jnp.int32, (size, size), 1)
    apart = row ^ col
    strict = row > col
    lower = row >= col
    eye = jnp.where(row == col, 1.0, 0.0)
    small_row = lax.broadcasted_iota(jnp.int32, (depth, depth), 0)
    small_col = lax.broadcasted_iota(jnp.int32, (depth, depth), 1)
    small_eye = jnp.where(small_row == small_col, 1.0, 0.0)
    systems, inverses, queries, keys, values, across = [], [], [], [], [], []
    for h in range(PAIR):
        lanes = slice(h * depth, (h + 1) * depth)

        def active(ref, before, taps):
            conv = conv_parts(
                ref[0, :, lanes].astype(F32),
                before[0, :, lanes].astype(F32),
                taps[:, lanes].astype(F32),
            )
            return conv * jax.nn.sigmoid(conv)

        q = active(q_ref, qb_ref, qt_ref)
        k = active(k_ref, kb_ref, kt_ref)
        v = active(v_ref, vb_ref, vt_ref)
        q = (q * unit_scale(q) * depth ** (-0.5)).astype(BF16)
        k = (k * unit_scale(k)).astype(BF16)
        queries.append(q)
        keys.append(k)
        values.append(v.astype(BF16))
        column = column_of(rates_ref[0], first + h)
        across.append(row_of(flipped_ref[0], first + h))
        system = jnp.where(strict, column * mul(k, k, NT), 0.0)
        systems.append(system)
        inverses.append(eye - jnp.where(apart == 1, system, 0.0))
    for level in range(1, size.bit_length() - 1):
        for h in range(PAIR):
            part = jnp.where((apart >> level) == 1, systems[h], 0.0)
            split = halves(inverses[h])
            half_way = mul_split(split, halves(part), NN)
            inverses[h] = inverses[h] - mul_split(halves(half_way), split, NN)
    for h in range(PAIR):
        inverse_ref[0, h] = inverses[h]
        joined = jnp.concatenate([values[h], keys[h]], axis=1)
        solved = mul_high(inverses[h] * across[h], joined, NN)
        updates_ref[0, h] = solved[:, :depth]
        weights_ref[0, h] = solved[:, depth:]
        scores = jnp.where(lower, mul(queries[h], keys[h], NT), 0.0)
        seen = mul_high(scores, solved, NN)
        mixed_ref[0, h] = seen[:, :depth]
        reach_ref[0, h] = queries[h].astype(F32) - seen[:, depth:]
        moved = mul_high(keys[h], solved, TN)
        offset_ref[0, h] = moved[:, :depth]
        transfer_ref[0, h] = small_eye - moved[:, depth:]


def specs_of(model, depth, size, reverse=False):
    wide = PAIR * depth
    blocks = model // wide
    rows = [pl.BlockSpec((1, size, wide), functools.partial(lambda part, s, g: (s, 0, part * blocks + g), part)) for part in range(3)]
    before = [pl.BlockSpec((1, 8, wide), functools.partial(lambda part, s, g: (s, 0, part * blocks + g), part)) for part in range(3)]
    return rows, before, wide, blocks


def forward_parts(projected, before, taps, rates, depth):
    seqs, size, model3 = projected.shape
    model = model3 // 3
    rows, prior, wide, blocks = specs_of(model, depth, size)
    tap_specs = [pl.BlockSpec((taps.shape[0], wide), functools.partial(lambda part, s, g: (0, part * blocks + g), part)) for part in range(3)]
    rate_spec = pl.BlockSpec((1, size, HEADS), lambda s, g: (s, 0, 0))
    flip_spec = pl.BlockSpec((1, HEADS, size), lambda s, g: (s, 0, 0))

    def out(*dims):
        return pl.BlockSpec((1, PAIR) + dims, lambda s, g: (s, g, 0, 0)), jax.ShapeDtypeStruct((seqs, HEADS) + dims, F32)

    outs = [out(size, size), out(size, depth), out(size, depth), out(size, depth), out(size, depth), out(depth, depth), out(depth, depth)]
    return pl.pallas_call(
        forward_kernel,
        grid=(seqs, HEADS // PAIR),
        in_specs=rows + prior + tap_specs + [rate_spec, flip_spec],
        out_specs=[o[0] for o in outs],
        out_shape=[o[1] for o in outs],
        compiler_params=pltpu.CompilerParams(vmem_limit_bytes=56 * 2**20),
        name="delta_forward",
    )(projected, projected, projected, before, before, before, taps, taps, taps, rates, jnp.swapaxes(rates, 1, 2))


def backward_kernel(
    q_ref, k_ref, v_ref, qb_ref, kb_ref, vb_ref, qt_ref, kt_ref, vt_ref, rates_ref,
    inverse_ref, updates_ref, weights_ref, state_ref, grad_ref, leaving_ref,
    rows_ref, prior_ref, taps_ref, rate_ref,
):
    depth = state_ref.shape[-1]
    size = q_ref.shape[1]
    first = pl.program_id(1) * PAIR
    row = lax.broadcasted_iota(jnp.int32, (size, size), 0)
    col = lax.broadcasted_iota(jnp.int32, (size, size), 1)
    strict = row > col
    lower = row >= col
    index8 = lax.broadcasted_iota(jnp.int32, (8, depth), 0)
    for h in range(PAIR):
        lanes = slice(h * depth, (h + 1) * depth)

        def load(ref, before, taps):
            return (
                ref[0, :, lanes].astype(F32),
                before[0, :, lanes].astype(F32),
                taps[:, lanes].astype(F32),
            )

        def active(parts):
            conv = conv_parts(*parts)
            gate = jax.nn.sigmoid(conv)
            return conv, gate, conv * gate

        raw = [load(q_ref, qb_ref, qt_ref), load(k_ref, kb_ref, kt_ref), load(v_ref, vb_ref, vt_ref)]
        acts = [active(parts) for parts in raw]
        q_scale = unit_scale(acts[0][2])
        k_scale = unit_scale(acts[1][2])
        q = (acts[0][2] * q_scale * depth ** (-0.5)).astype(BF16)
        k = (acts[1][2] * k_scale).astype(BF16)
        v = acts[2][2].astype(BF16)
        column = column_of(rates_ref[0], first + h)
        inverse = inverse_ref[0, h]
        state = state_ref[0, h]
        grad = grad_ref[0, h]
        leaving = leaving_ref[0, h]
        gram = jnp.where(strict, mul(k, k, NT), 0.0)
        scores = jnp.where(lower, mul(q, k, NT), 0.0)
        errors = updates_ref[0, h] - mul_high(weights_ref[0, h], state, NN)
        missed = v.astype(F32) - mul_high(k, state, NN) - mul_high(gram, errors, NN)
        grad_errors = mul_high(scores, grad, TN) + mul_high(k, leaving, NN)
        grad_right = mul_high(inverse, grad_errors, TN)
        grad_scores = jnp.where(lower, mul_high(grad, errors, NT), 0.0)
        grad_system = jnp.where(strict, -mul_high(grad_right, errors, NT), 0.0) * column
        grad_v = grad_right * column
        grad_q = mul_high(grad, state, NT) + mul_high(grad_scores, k, NN)
        grad_k = (
            mul_high(grad_scores, q, TN)
            + mul_high(errors, leaving, NT)
            - mul_high(grad_v, state, NT)
            + mul_high(grad_system, k, NN)
            + mul_high(grad_system, k, TN)
        )
        rate_ref[0, h] = jnp.sum(grad_right * missed, axis=1, keepdims=True)
        q_un, k_un = acts[0][2], acts[1][2]
        grad_q = (
            q_scale * grad_q
            - q_un * (q_scale * q_scale * q_scale * jnp.sum(grad_q * q_un, axis=1, keepdims=True))
        ) * depth ** (-0.5)
        grad_k = k_scale * grad_k - k_un * (
            k_scale * k_scale * k_scale * jnp.sum(grad_k * k_un, axis=1, keepdims=True)
        )
        for part, grad_act in enumerate((grad_q, grad_k, grad_v)):
            conv, gate, _ = acts[part]
            rows, before, taps = raw[part]
            width = taps.shape[0]
            grad_conv = grad_act * (gate * (1.0 + conv * (1.0 - gate)))
            total = None
            ahead = None
            for lag in range(width):
                by = width - 1 - lag
                tap = taps[lag : lag + 1]
                term = tap * shifted_up(grad_conv, by)
                total = term if total is None else total + term
                taps_ref[0, part, lag : lag + 1, lanes] = jnp.sum(
                    grad_conv * shifted_down(rows, before, by), axis=0, keepdims=True
                )
                if by:
                    early = jnp.where(index8 >= 8 - by, tap * pltpu.roll(grad_conv[:8], 8 - by, 0), 0.0)
                    ahead = early if ahead is None else ahead + early
            rows_ref[part, 0, :, lanes] = total
            prior_ref[0, part, :, lanes] = ahead


def backward_parts(projected, before, taps, rates, inverse, updates, weights, state, grad, leaving, depth):
    seqs, size, model3 = projected.shape
    model = model3 // 3
    width = taps.shape[0]
    rows, prior, wide, blocks = specs_of(model, depth, size)
    tap_specs = [pl.BlockSpec((width, wide), functools.partial(lambda part, s, g: (0, part * blocks + g), part)) for part in range(3)]
    rate_spec = pl.BlockSpec((1, size, HEADS), lambda s, g: (s, 0, 0))

    def heads(*dims):
        return pl.BlockSpec((1, PAIR) + dims, lambda s, g: (s, g, 0, 0))

    return pl.pallas_call(
        backward_kernel,
        grid=(seqs, HEADS // PAIR),
        in_specs=rows + prior + tap_specs + [rate_spec, heads(size, size), heads(size, depth), heads(size, depth), heads(depth, depth), heads(size, depth), heads(depth, depth)],
        out_specs=[
            pl.BlockSpec((3, 1, size, wide), lambda s, g: (0, s, 0, g)),
            pl.BlockSpec((1, 3, 8, wide), lambda s, g: (s, 0, 0, g)),
            pl.BlockSpec((1, 3, width, wide), lambda s, g: (s, 0, 0, g)),
            heads(size, 1),
        ],
        out_shape=[
            jax.ShapeDtypeStruct((3, seqs, size, model), F32),
            jax.ShapeDtypeStruct((seqs, 3, 8, model), F32),
            jax.ShapeDtypeStruct((seqs, 3, width, model), F32),
            jax.ShapeDtypeStruct((seqs, HEADS, size, 1), F32),
        ],
        compiler_params=pltpu.CompilerParams(vmem_limit_bytes=56 * 2**20),
        name="delta_backward",
    )(projected, projected, projected, before, before, before, taps, taps, taps, rates, inverse, updates, weights, state, grad, leaving)


def passed_along(value, axis, by):
    peers = lax.axis_size(axis)
    pairs = [(i, i + by) for i in range(peers) if 0 <= i + by < peers]
    return lax.ppermute(value, axis, pairs)


def apply_map(transfer, state, offset):
    return jnp.einsum("shij,shjk->shik", transfer, state, precision=lax.Precision.HIGH) + offset


def rows_times(left, right):
    return jnp.einsum("sga,ab->sgb", left, right, preferred_element_type=F32)


def rows_back(grad, weight):
    return jnp.einsum("sgb,ab->sga", grad, weight, preferred_element_type=F32)


def weight_grad(left, right):
    return jnp.einsum("sga,sgb->ab", left, right, preferred_element_type=F32)


def norm_back(rows, scale, gain, grad):
    weighted = grad * gain
    gain_grad = jnp.sum(grad * rows * scale, axis=tuple(range(rows.ndim - 1)))
    width = rows.shape[-1]
    row_grad = scale * weighted - rows * scale**3 * (
        jnp.sum(weighted * rows, axis=-1, keepdims=True) / width
    )
    return (gain_grad, row_grad)


BOTH = ("dp", "cp")


def per_device(
    block_input, mixer_gain, qkv_weight, conv_taps, beta_weight, out_gain,
    proj_weight, ffn_gain, gate_up, down_weight, cotangent,
):
    seqs, seg_len, model = block_input.shape
    width = conv_taps.shape[0]
    depth = model // HEADS
    peers = lax.axis_size(BOTH)
    share = model // peers
    tap_share = conv_taps.shape[1]
    small = jnp.concatenate(
        [mixer_gain, ffn_gain, beta_weight.reshape(-1), conv_taps.reshape(-1)]
    )
    small = jnp.pad(small, (0, 1024 - small.size)).reshape(8, 128)
    small = lax.all_gather(small, BOTH, axis=0, tiled=False).reshape(peers, 1024)
    w_qkv = lax.all_gather(qkv_weight, BOTH, axis=0, tiled=True)
    w_proj = lax.all_gather(proj_weight, BOTH, axis=0, tiled=True)
    w_gateup = lax.all_gather(gate_up, BOTH, axis=0, tiled=True)
    w_down = lax.all_gather(down_weight, BOTH, axis=0, tiled=True)
    gain_one = small[:, :share].reshape(-1)
    gain_two = small[:, share : 2 * share].reshape(-1)
    at = 2 * share
    w_beta = small[:, at : at + share * HEADS].reshape(model, HEADS)
    at += share * HEADS
    taps = small[:, at : at + width * tap_share].reshape(peers, width, tap_share)
    taps = jnp.swapaxes(taps, 0, 1).reshape(width, peers * tap_share)

    gain_outf = out_gain.astype(F32)
    resid_in = block_input.astype(F32)
    scale_one = lax.rsqrt(jnp.mean(resid_in * resid_in, axis=-1, keepdims=True) + norm_eps)
    normed_one = (resid_in * scale_one * gain_one.astype(F32)).astype(BF16)
    projected = rows_times(normed_one, w_qkv).astype(BF16)
    tail = projected[:, seg_len - (width - 1) :, :]
    before = jnp.pad(passed_along(tail, "cp", 1), ((0, 0), (8 - (width - 1), 0), (0, 0)))
    rates = jax.nn.sigmoid(rows_times(normed_one, w_beta))
    inverse, updates, weights, reach, alone, transfer, offset = forward_parts(
        projected, before, taps, rates, depth
    )
    carried = jnp.zeros_like(offset)
    for step in range(lax.axis_size("cp") - 1):
        sent = offset if step == 0 else apply_map(transfer, carried, offset)
        carried = passed_along(sent.astype(BF16), "cp", 1).astype(F32)
    mixed = alone + jnp.einsum("shtd,shde->shte", reach, carried, precision=lax.Precision.HIGH)
    scale_mix = lax.rsqrt(jnp.mean(mixed * mixed, axis=-1, keepdims=True) + norm_eps)
    mixed_low = jnp.swapaxes(mixed * scale_mix * gain_outf, 1, 2).reshape(seqs, seg_len, model).astype(BF16)
    attn = rows_times(mixed_low, w_proj)
    middle = resid_in + attn
    scale_two = lax.rsqrt(jnp.mean(middle * middle, axis=-1, keepdims=True) + norm_eps)
    gain_twof = gain_two.astype(F32)
    normed_two = (middle * scale_two * gain_twof).astype(BF16)
    gates = rows_times(normed_two, w_gateup)
    half = gates.shape[-1] // 2
    gate_part = gates[..., :half]
    up_part = gates[..., half:]
    hidden = (jax.nn.silu(gate_part) * up_part).astype(BF16)
    ffn_out = rows_times(hidden, w_down)
    result = middle + ffn_out
    squares = jnp.stack(
        [jnp.sum(result * result), jnp.sum(attn * attn), jnp.sum(ffn_out * ffn_out)]
    )
    upstream = cotangent.astype(F32)
    grad_down = weight_grad(hidden, cotangent).astype(BF16)
    grad_hidden = rows_back(cotangent, w_down)
    sigma = jax.nn.sigmoid(gate_part)
    grad_gate = grad_hidden * up_part * (sigma * (1.0 + gate_part * (1.0 - sigma)))
    grad_up = grad_hidden * (gate_part * sigma)
    grad_gates = jnp.concatenate([grad_gate, grad_up], axis=-1).astype(BF16)
    grad_gateup = weight_grad(normed_two, grad_gates).astype(BF16)
    grad_normed_two = rows_back(grad_gates, w_gateup)
    grad_ffn, grad_from_norm = norm_back(middle, scale_two, gain_twof, grad_normed_two)
    grad_middle = upstream + grad_from_norm
    grad_attn = grad_middle.astype(BF16)
    grad_proj = weight_grad(mixed_low, grad_attn).astype(BF16)
    grad_normed_mix = rows_back(grad_attn, w_proj).astype(BF16).astype(F32)
    grad_normed_mix = jnp.swapaxes(grad_normed_mix.reshape(seqs, seg_len, HEADS, depth), 1, 2)
    grad_out, grad_mixed = norm_back(mixed, scale_mix, gain_outf, grad_normed_mix)
    local_part = jnp.einsum("shtd,shte->shde", reach, grad_mixed, precision=lax.Precision.HIGH)
    flipped = jnp.swapaxes(transfer, -1, -2)
    incoming = jnp.zeros_like(local_part)
    for step in range(lax.axis_size("cp") - 1):
        sent = local_part if step == 0 else apply_map(flipped, incoming, local_part)
        incoming = passed_along(sent.astype(BF16), "cp", -1).astype(F32)
    grad_rows, grad_prior, grad_taps, grad_rates = backward_parts(
        projected, before, taps, rates, inverse, updates, weights, carried, grad_mixed, incoming, depth
    )
    returned = passed_along(grad_prior, "cp", -1)
    grad_rows = jnp.concatenate(
        [
            grad_rows[:, :, : seg_len - 8],
            grad_rows[:, :, seg_len - 8 :] + jnp.swapaxes(returned, 0, 1),
        ],
        axis=2,
    ).astype(BF16)
    grad_projected = jnp.moveaxis(grad_rows, 0, 2).reshape(seqs, seg_len, 3 * model)
    grad_rates = jnp.swapaxes(grad_rates[..., 0], 1, 2)
    grad_logits = grad_rates * rates * (1.0 - rates)
    grad_qkv = weight_grad(normed_one, grad_projected).astype(BF16)
    grad_beta = jnp.einsum("sga,sgb->ab", normed_one.astype(F32), grad_logits, precision=lax.Precision.HIGH)
    grad_normed_one = rows_back(grad_projected, w_qkv)
    grad_normed_one = grad_normed_one + jnp.einsum(
        "sgb,ab->sga", grad_logits, w_beta.astype(F32), precision=lax.Precision.HIGH
    )
    grad_mixer, grad_from_first = norm_back(resid_in, scale_one, gain_one.astype(F32), grad_normed_one)
    grad_input = grad_middle + grad_from_first
    grad_conv = jnp.moveaxis(jnp.sum(grad_taps, axis=0), 0, 1).reshape(width, 3 * model)
    grad_conv = jnp.swapaxes(grad_conv.reshape(width, peers, tap_share), 0, 1).reshape(-1)
    pieces = [grad_mixer, grad_ffn, grad_beta.reshape(-1), grad_conv, squares, grad_out]
    sizes = [p.size for p in pieces]
    packed = jnp.concatenate(pieces)
    packed = jnp.pad(packed, (0, -packed.size % 1024)).reshape(-1, 128)
    packed = lax.psum(packed, BOTH).reshape(-1)
    ends = [sum(sizes[: i + 1]) for i in range(len(sizes))]
    starts = [0] + ends[:-1]
    me = lax.axis_index(BOTH)

    def mine(i):
        own = sizes[i] // peers
        return lax.dynamic_slice(packed[starts[i] : ends[i]], (me * own,), (own,))

    rms_values = jnp.sqrt(packed[starts[4] : ends[4]] / (result.size * peers))

    def scattered(grad):
        return lax.psum_scatter(grad, BOTH, scatter_dimension=0, tiled=True).astype(F32)

    return (
        result.astype(BF16),
        grad_input,
        mine(0),
        scattered(grad_qkv),
        mine(3).reshape(width, tap_share),
        mine(2).reshape(share, HEADS),
        packed[starts[5] : ends[5]],
        scattered(grad_proj),
        mine(1),
        scattered(grad_gateup),
        scattered(grad_down),
        rms_values,
    )


def solution(mesh):
    both = P(BOTH)
    rows = P(BOTH, None)
    tokens = P("dp", "cp", None)
    taps = P(None, BOTH)
    in_specs = (tokens, both, rows, taps, rows, P(), rows, both, rows, rows, tokens)
    out_specs = (tokens, tokens, both, rows, taps, rows, P(), rows, both, rows, rows, P())
    return jax.shard_map(
        per_device, mesh=mesh, in_specs=in_specs, out_specs=out_specs, check_vma=False
    )
```

```python
import functools

import jax
import jax.numpy as jnp
from jax import lax
from jax.experimental import pallas as pl
from jax.experimental.pallas import tpu as pltpu
from jax.sharding import PartitionSpec as P

HEADS = 8
PAIR = 4

norm_eps = 1e-05
unit_eps = 1e-06
F32 = jnp.float32
BF16 = jnp.bfloat16


def halves(value):
    high = value.astype(BF16)
    return high, (value - high.astype(F32)).astype(BF16)


NN = (((1,), (0,)), ((), ()))
NT = (((1,), (1,)), ((), ()))
TN = (((0,), (0,)), ((), ()))


def mul(left, right, dims):
    return lax.dot_general(left, right, dims, preferred_element_type=F32)


def mul_split(left, right, dims):
    return (
        mul(left[0], right[0], dims) + mul(left[0], right[1], dims) + mul(left[1], right[0], dims)
    )


def mul_high(left, right, dims):
    left = (left,) if left.dtype == BF16 else halves(left)
    right = (right,) if right.dtype == BF16 else halves(right)
    total = mul(left[0], right[0], dims)
    if len(right) == 2:
        total = total + mul(left[0], right[1], dims)
    if len(left) == 2:
        total = total + mul(left[1], right[0], dims)
    return total


def shifted_down(rows, before, by):
    if by == 0:
        return rows
    rolled = pltpu.roll(rows, by, 0)
    top = pltpu.roll(before, by, 0)
    index = lax.broadcasted_iota(jnp.int32, before.shape, 0)
    first = jnp.where(index < by, top, rolled[: before.shape[0]])
    return jnp.concatenate([first, rolled[before.shape[0] :]], axis=0)


def shifted_up(rows, by):
    if by == 0:
        return rows
    count = rows.shape[0]
    index = lax.broadcasted_iota(jnp.int32, rows.shape, 0)
    return jnp.where(index < count - by, pltpu.roll(rows, count - by, 0), 0.0)


def conv_parts(rows, before, taps):
    width = taps.shape[0]
    conv = None
    for lag in range(width):
        term = taps[lag : lag + 1] * shifted_down(rows, before, width - 1 - lag)
        conv = term if conv is None else conv + term
    return conv


def unit_scale(active):
    return lax.rsqrt(jnp.sum(active * active, axis=-1, keepdims=True) + unit_eps)


def column_of(rates, head):
    index = lax.broadcasted_iota(jnp.int32, rates.shape, 1)
    return jnp.sum(jnp.where(index == head, rates, 0.0), axis=1, keepdims=True)


def row_of(rates, head):
    index = lax.broadcasted_iota(jnp.int32, rates.shape, 0)
    return jnp.sum(jnp.where(index == head, rates, 0.0), axis=0, keepdims=True)


def forward_kernel(
    q_ref, k_ref, v_ref, qb_ref, kb_ref, vb_ref, qt_ref, kt_ref, vt_ref, rates_ref, flipped_ref,
    inverse_ref, updates_ref, weights_ref, reach_ref, mixed_ref, transfer_ref, offset_ref,
):
    depth = transfer_ref.shape[-1]
    size = q_ref.shape[1]
    first = pl.program_id(1) * PAIR
    row = lax.broadcasted_iota(jnp.int32, (size, size), 0)
    col = lax.broadcasted_iota(jnp.int32, (size, size), 1)
    apart = row ^ col
    strict = row > col
    lower = row >= col
    eye = jnp.where(row == col, 1.0, 0.0)
    small_row = lax.broadcasted_iota(jnp.int32, (depth, depth), 0)
    small_col = lax.broadcasted_iota(jnp.int32, (depth, depth), 1)
    small_eye = jnp.where(small_row == small_col, 1.0, 0.0)
    systems, inverses, queries, keys, values, across = [], [], [], [], [], []
    for h in range(PAIR):
        lanes = slice(h * depth, (h + 1) * depth)

        def active(ref, before, taps):
            conv = conv_parts(
                ref[0, :, lanes].astype(F32),
                before[0, :, lanes].astype(F32),
                taps[:, lanes].astype(F32),
            )
            return conv * jax.nn.sigmoid(conv)

        q = active(q_ref, qb_ref, qt_ref)
        k = active(k_ref, kb_ref, kt_ref)
        v = active(v_ref, vb_ref, vt_ref)
        q = (q * unit_scale(q) * depth ** (-0.5)).astype(BF16)
        k = (k * unit_scale(k)).astype(BF16)
        queries.append(q)
        keys.append(k)
        values.append(v.astype(BF16))
        column = column_of(rates_ref[0], first + h)
        across.append(row_of(flipped_ref[0], first + h))
        system = jnp.where(strict, column * mul(k, k, NT), 0.0)
        systems.append(system)
        inverses.append(eye - jnp.where(apart == 1, system, 0.0))
    for level in range(1, size.bit_length() - 1):
        for h in range(PAIR):
            part = jnp.where((apart >> level) == 1, systems[h], 0.0)
            split = halves(inverses[h])
            half_way = mul_split(split, halves(part), NN)
            inverses[h] = inverses[h] - mul_split(halves(half_way), split, NN)
    for h in range(PAIR):
        inverse_ref[0, h] = inverses[h]
        joined = jnp.concatenate([values[h], keys[h]], axis=1)
        solved = mul_high(inverses[h] * across[h], joined, NN)
        updates_ref[0, h] = solved[:, :depth]
        weights_ref[0, h] = solved[:, depth:]
        scores = jnp.where(lower, mul(queries[h], keys[h], NT), 0.0)
        seen = mul_high(scores, solved, NN)
        mixed_ref[0, h] = seen[:, :depth]
        reach_ref[0, h] = queries[h].astype(F32) - seen[:, depth:]
        moved = mul_high(keys[h], solved, TN)
        offset_ref[0, h] = moved[:, :depth]
        transfer_ref[0, h] = small_eye - moved[:, depth:]


def specs_of(model, depth, size, reverse=False):
    wide = PAIR * depth
    blocks = model // wide
    rows = [pl.BlockSpec((1, size, wide), functools.partial(lambda part, s, g: (s, 0, part * blocks + g), part)) for part in range(3)]
    before = [pl.BlockSpec((1, 8, wide), functools.partial(lambda part, s, g: (s, 0, part * blocks + g), part)) for part in range(3)]
    return rows, before, wide, blocks


def forward_parts(projected, before, taps, rates, depth):
    seqs, size, model3 = projected.shape
    model = model3 // 3
    rows, prior, wide, blocks = specs_of(model, depth, size)
    tap_specs = [pl.BlockSpec((taps.shape[0], wide), functools.partial(lambda part, s, g: (0, part * blocks + g), part)) for part in range(3)]
    rate_spec = pl.BlockSpec((1, size, HEADS), lambda s, g: (s, 0, 0))
    flip_spec = pl.BlockSpec((1, HEADS, size), lambda s, g: (s, 0, 0))

    def out(*dims):
        return pl.BlockSpec((1, PAIR) + dims, lambda s, g: (s, g, 0, 0)), jax.ShapeDtypeStruct((seqs, HEADS) + dims, F32)

    outs = [out(size, size), out(size, depth), out(size, depth), out(size, depth), out(size, depth), out(depth, depth), out(depth, depth)]
    return pl.pallas_call(
        forward_kernel,
        grid=(seqs, HEADS // PAIR),
        in_specs=rows + prior + tap_specs + [rate_spec, flip_spec],
        out_specs=[o[0] for o in outs],
        out_shape=[o[1] for o in outs],
        compiler_params=pltpu.CompilerParams(vmem_limit_bytes=56 * 2**20),
        name="delta_forward",
    )(projected, projected, projected, before, before, before, taps, taps, taps, rates, jnp.swapaxes(rates, 1, 2))


def backward_kernel(
    q_ref, k_ref, v_ref, qb_ref, kb_ref, vb_ref, qt_ref, kt_ref, vt_ref, rates_ref,
    inverse_ref, updates_ref, weights_ref, state_ref, grad_ref, leaving_ref,
    rows_ref, prior_ref, taps_ref, rate_ref,
):
    depth = state_ref.shape[-1]
    size = q_ref.shape[1]
    first = pl.program_id(1) * PAIR
    row = lax.broadcasted_iota(jnp.int32, (size, size), 0)
    col = lax.broadcasted_iota(jnp.int32, (size, size), 1)
    strict = row > col
    lower = row >= col
    index8 = lax.broadcasted_iota(jnp.int32, (8, depth), 0)
    for h in range(PAIR):
        lanes = slice(h * depth, (h + 1) * depth)

        def load(ref, before, taps):
            return (
                ref[0, :, lanes].astype(F32),
                before[0, :, lanes].astype(F32),
                taps[:, lanes].astype(F32),
            )

        def active(parts):
            conv = conv_parts(*parts)
            gate = jax.nn.sigmoid(conv)
            return conv, gate, conv * gate

        raw = [load(q_ref, qb_ref, qt_ref), load(k_ref, kb_ref, kt_ref), load(v_ref, vb_ref, vt_ref)]
        acts = [active(parts) for parts in raw]
        q_scale = unit_scale(acts[0][2])
        k_scale = unit_scale(acts[1][2])
        q = (acts[0][2] * q_scale * depth ** (-0.5)).astype(BF16)
        k = (acts[1][2] * k_scale).astype(BF16)
        v = acts[2][2].astype(BF16)
        column = column_of(rates_ref[0], first + h)
        inverse = inverse_ref[0, h]
        state = state_ref[0, h]
        grad = grad_ref[0, h]
        leaving = leaving_ref[0, h]
        gram = jnp.where(strict, mul(k, k, NT), 0.0)
        scores = jnp.where(lower, mul(q, k, NT), 0.0)
        errors = updates_ref[0, h] - mul_high(weights_ref[0, h], state, NN)
        missed = v.astype(F32) - mul_high(k, state, NN) - mul_high(gram, errors, NN)
        grad_errors = mul_high(scores, grad, TN) + mul_high(k, leaving, NN)
        grad_right = mul_high(inverse, grad_errors, TN)
        grad_scores = jnp.where(lower, mul_high(grad, errors, NT), 0.0)
        grad_system = jnp.where(strict, -mul_high(grad_right, errors, NT), 0.0) * column
        grad_v = grad_right * column
        grad_q = mul_high(grad, state, NT) + mul_high(grad_scores, k, NN)
        grad_k = (
            mul_high(grad_scores, q, TN)
            + mul_high(errors, leaving, NT)
            - mul_high(grad_v, state, NT)
            + mul_high(grad_system, k, NN)
            + mul_high(grad_system, k, TN)
        )
        rate_ref[0, h] = jnp.sum(grad_right * missed, axis=1, keepdims=True)
        q_un, k_un = acts[0][2], acts[1][2]
        grad_q = (
            q_scale * grad_q
            - q_un * (q_scale * q_scale * q_scale * jnp.sum(grad_q * q_un, axis=1, keepdims=True))
        ) * depth ** (-0.5)
        grad_k = k_scale * grad_k - k_un * (
            k_scale * k_scale * k_scale * jnp.sum(grad_k * k_un, axis=1, keepdims=True)
        )
        for part, grad_act in enumerate((grad_q, grad_k, grad_v)):
            conv, gate, _ = acts[part]
            rows, before, taps = raw[part]
            width = taps.shape[0]
            grad_conv = grad_act * (gate * (1.0 + conv * (1.0 - gate)))
            total = None
            ahead = None
            for lag in range(width):
                by = width - 1 - lag
                tap = taps[lag : lag + 1]
                term = tap * shifted_up(grad_conv, by)
                total = term if total is None else total + term
                taps_ref[0, part, lag : lag + 1, lanes] = jnp.sum(
                    grad_conv * shifted_down(rows, before, by), axis=0, keepdims=True
                )
                if by:
                    early = jnp.where(index8 >= 8 - by, tap * pltpu.roll(grad_conv[:8], 8 - by, 0), 0.0)
                    ahead = early if ahead is None else ahead + early
            rows_ref[part, 0, :, lanes] = total
            prior_ref[0, part, :, lanes] = ahead


def backward_parts(projected, before, taps, rates, inverse, updates, weights, state, grad, leaving, depth):
    seqs, size, model3 = projected.shape
    model = model3 // 3
    width = taps.shape[0]
    rows, prior, wide, blocks = specs_of(model, depth, size)
    tap_specs = [pl.BlockSpec((width, wide), functools.partial(lambda part, s, g: (0, part * blocks + g), part)) for part in range(3)]
    rate_spec = pl.BlockSpec((1, size, HEADS), lambda s, g: (s, 0, 0))

    def heads(*dims):
        return pl.BlockSpec((1, PAIR) + dims, lambda s, g: (s, g, 0, 0))

    return pl.pallas_call(
        backward_kernel,
        grid=(seqs, HEADS // PAIR),
        in_specs=rows + prior + tap_specs + [rate_spec, heads(size, size), heads(size, depth), heads(size, depth), heads(depth, depth), heads(size, depth), heads(depth, depth)],
        out_specs=[
            pl.BlockSpec((3, 1, size, wide), lambda s, g: (0, s, 0, g)),
            pl.BlockSpec((1, 3, 8, wide), lambda s, g: (s, 0, 0, g)),
            pl.BlockSpec((1, 3, width, wide), lambda s, g: (s, 0, 0, g)),
            heads(size, 1),
        ],
        out_shape=[
            jax.ShapeDtypeStruct((3, seqs, size, model), F32),
            jax.ShapeDtypeStruct((seqs, 3, 8, model), F32),
            jax.ShapeDtypeStruct((seqs, 3, width, model), F32),
            jax.ShapeDtypeStruct((seqs, HEADS, size, 1), F32),
        ],
        compiler_params=pltpu.CompilerParams(vmem_limit_bytes=56 * 2**20),
        name="delta_backward",
    )(projected, projected, projected, before, before, before, taps, taps, taps, rates, inverse, updates, weights, state, grad, leaving)


BOTH = ("dp", "cp")


class Grid:
    def __init__(self):
        self.cp = lax.axis_size("cp")
        group = lax.axis_size("dp")
        self.core = 2 if group % 2 == 0 else 1
        self.lo = 2 if group // self.core % 2 == 0 else 1
        self.hi = group // self.core // self.lo
        self.sizes = (self.hi, self.lo, self.core, self.cp)

    def place(self):
        member = lax.axis_index("dp")
        return (
            member // (self.lo * self.core),
            member // self.core % self.lo,
            member % self.core,
            lax.axis_index("cp"),
        )

    def swap(self, value, axis, by):
        step = [1] * 4
        for later in range(3):
            step[2 - later] = step[3 - later] * self.sizes[3 - later]
        pairs = []
        for device in range(step[0] * self.sizes[0]):
            here = device // step[axis] % self.sizes[axis]
            pairs.append((device, device + ((here ^ by) - here) * step[axis]))
        return lax.ppermute(value, BOTH, pairs)

    def others(self, value, axis):
        return [self.swap(value, axis, by) for by in range(1, self.sizes[axis])]


HI, LO, CORE, SEG = range(4)


def cut_of(columns):
    return columns // 256 * 128


def place_kernel(spot, own_left, own_right, other_left, other_right, *outs):
    core = spot[2]
    for away, left, right in ((0, own_left, own_right), (1, other_left, other_right)):
        if away >= outs[0].shape[2]:
            continue
        row = jnp.concatenate([left[0, 0, 0], right[0, 0, 0]], axis=1)
        at = 0
        for out in outs:
            wide = out.shape[-1]
            out[0, 0, core ^ away, 0] = row[:, at : at + wide]
            at += wide


def gathered(grid, shard, widths):
    r, total = shard.shape
    cut = cut_of(total)
    parts = [shard] + grid.others(shard, SEG)
    own = []
    for start, stop, axes in ((0, cut, (LO, HI)), (cut, total, (HI, LO))):
        value = jnp.stack([part[:, start:stop] for part in parts])
        for axis in axes:
            value = jnp.stack([value] + grid.others(value, axis))
        own.append(value)
    other = [grid.swap(value, CORE, 1) if grid.core == 2 else value for value in own]

    def source(wide, order):
        def index(a, b, c, spot):
            first, second = a ^ spot[0], b ^ spot[1]
            return (first, second, c ^ spot[3], 0, 0) if order == 0 else (second, first, c ^ spot[3], 0, 0)

        return pl.BlockSpec((1, 1, 1, r, wide), index)

    sources = [source(cut, 0), source(total - cut, 1)]
    outs = pl.pallas_call(
        place_kernel,
        grid_spec=pltpu.PrefetchScalarGridSpec(
            num_scalar_prefetch=1,
            grid=(grid.hi, grid.lo, grid.cp),
            in_specs=sources + sources,
            out_specs=[
                pl.BlockSpec((1, 1, grid.core, 1, r, wide), lambda a, b, c, spot: (a, b, 0, c, 0, 0))
                for wide in widths
            ],
        ),
        out_shape=[jax.ShapeDtypeStruct(grid.sizes + (r, wide), shard.dtype) for wide in widths],
        name="place_rows",
    )(jnp.stack(grid.place()), *own, *other)
    return [out.reshape(-1, out.shape[-1]) for out in outs]


def summed_share(grid, value):
    hi, lo, core, seg = grid.place()
    columns = value.shape[-1]
    value = value.reshape(grid.sizes + (-1, columns))

    def pick(array, index, axis):
        return lax.dynamic_index_in_dim(array, index, axis, keepdims=False)

    def stage(array, axis, dim, here):
        total = pick(array, here, dim).astype(F32)
        for by in range(1, grid.sizes[axis]):
            total = total + grid.swap(pick(array, here ^ by, dim), axis, by).astype(F32)
        return total

    value = stage(value, CORE, 2, core).astype(BF16)
    cut = cut_of(columns)
    left, right = value[..., :cut], value[..., cut:]
    left = stage(left, LO, 1, lo).astype(BF16)
    right = stage(right, HI, 0, hi).astype(BF16)
    left = stage(left, HI, 0, hi)
    right = stage(right, LO, 0, lo)
    joined = jnp.concatenate([left, right], axis=-1).astype(BF16)
    return stage(joined, SEG, 0, seg)


def passed_along(value, axis, by):
    peers = lax.axis_size(axis)
    pairs = [(i, i + by) for i in range(peers) if 0 <= i + by < peers]
    return lax.ppermute(value, axis, pairs)


def apply_map(transfer, state, offset):
    return jnp.einsum("shij,shjk->shik", transfer, state, precision=lax.Precision.HIGH) + offset


def rows_times(left, right):
    return jnp.einsum("sga,ab->sgb", left, right, preferred_element_type=F32)


def rows_back(grad, weight):
    return jnp.einsum("sgb,ab->sga", grad, weight, preferred_element_type=F32)


def weight_grad(left, right):
    return jnp.einsum("sga,sgb->ab", left, right, preferred_element_type=F32)


def norm_back(rows, scale, gain, grad):
    weighted = grad * gain
    gain_grad = jnp.sum(grad * rows * scale, axis=tuple(range(rows.ndim - 1)))
    width = rows.shape[-1]
    row_grad = scale * weighted - rows * scale**3 * (
        jnp.sum(weighted * rows, axis=-1, keepdims=True) / width
    )
    return (gain_grad, row_grad)


def per_device(
    block_input, mixer_gain, qkv_weight, conv_taps, beta_weight, out_gain,
    proj_weight, ffn_gain, gate_up, down_weight, cotangent,
):
    seqs, seg_len, model = block_input.shape
    width = conv_taps.shape[0]
    depth = model // HEADS
    peers = lax.axis_size(BOTH)
    share = model // peers
    tap_share = conv_taps.shape[1]
    grid = Grid()
    small = jnp.concatenate(
        [mixer_gain, ffn_gain, beta_weight.reshape(-1), conv_taps.reshape(-1)]
    )
    small = jnp.pad(small, (0, share * 128 - small.size)).reshape(share, 128)
    w_qkv, small = gathered(grid, jnp.concatenate([qkv_weight, small], axis=1), (3 * model, 128))
    small = small.reshape(peers, share * 128)
    (w_proj,) = gathered(grid, proj_weight, (model,))
    (w_gateup,) = gathered(grid, gate_up, gate_up.shape[1:])
    (w_down,) = gathered(grid, down_weight, (model,))
    gain_one = small[:, :share].reshape(-1)
    gain_two = small[:, share : 2 * share].reshape(-1)
    at = 2 * share
    w_beta = small[:, at : at + share * HEADS].reshape(model, HEADS)
    at += share * HEADS
    taps = small[:, at : at + width * tap_share].reshape(peers, width, tap_share)
    taps = jnp.swapaxes(taps, 0, 1).reshape(width, peers * tap_share)

    gain_outf = out_gain.astype(F32)
    resid_in = block_input.astype(F32)
    scale_one = lax.rsqrt(jnp.mean(resid_in * resid_in, axis=-1, keepdims=True) + norm_eps)
    normed_one = (resid_in * scale_one * gain_one.astype(F32)).astype(BF16)
    projected = rows_times(normed_one, w_qkv).astype(BF16)
    tail = projected[:, seg_len - (width - 1) :, :]
    before = jnp.pad(passed_along(tail, "cp", 1), ((0, 0), (8 - (width - 1), 0), (0, 0)))
    rates = jax.nn.sigmoid(rows_times(normed_one, w_beta))
    inverse, updates, weights, reach, alone, transfer, offset = forward_parts(
        projected, before, taps, rates, depth
    )
    carried = jnp.zeros_like(offset)
    for step in range(lax.axis_size("cp") - 1):
        sent = offset if step == 0 else apply_map(transfer, carried, offset)
        carried = passed_along(sent.astype(BF16), "cp", 1).astype(F32)
    mixed = alone + jnp.einsum("shtd,shde->shte", reach, carried, precision=lax.Precision.HIGH)
    scale_mix = lax.rsqrt(jnp.mean(mixed * mixed, axis=-1, keepdims=True) + norm_eps)
    mixed_low = jnp.swapaxes(mixed * scale_mix * gain_outf, 1, 2).reshape(seqs, seg_len, model).astype(BF16)
    attn = rows_times(mixed_low, w_proj)
    middle = resid_in + attn
    scale_two = lax.rsqrt(jnp.mean(middle * middle, axis=-1, keepdims=True) + norm_eps)
    gain_twof = gain_two.astype(F32)
    normed_two = (middle * scale_two * gain_twof).astype(BF16)
    gates = rows_times(normed_two, w_gateup)
    half = gates.shape[-1] // 2
    gate_part = gates[..., :half]
    up_part = gates[..., half:]
    hidden = (jax.nn.silu(gate_part) * up_part).astype(BF16)
    ffn_out = rows_times(hidden, w_down)
    result = middle + ffn_out
    squares = jnp.stack(
        [jnp.sum(result * result), jnp.sum(attn * attn), jnp.sum(ffn_out * ffn_out)]
    )
    upstream = cotangent.astype(F32)
    grad_down = weight_grad(hidden, cotangent).astype(BF16)
    grad_hidden = rows_back(cotangent, w_down)
    sigma = jax.nn.sigmoid(gate_part)
    grad_gate = grad_hidden * up_part * (sigma * (1.0 + gate_part * (1.0 - sigma)))
    grad_up = grad_hidden * (gate_part * sigma)
    grad_gates = jnp.concatenate([grad_gate, grad_up], axis=-1).astype(BF16)
    grad_gateup = weight_grad(normed_two, grad_gates).astype(BF16)
    grad_normed_two = rows_back(grad_gates, w_gateup)
    grad_ffn, grad_from_norm = norm_back(middle, scale_two, gain_twof, grad_normed_two)
    grad_middle = upstream + grad_from_norm
    grad_attn = grad_middle.astype(BF16)
    grad_proj = weight_grad(mixed_low, grad_attn).astype(BF16)
    grad_normed_mix = rows_back(grad_attn, w_proj).astype(BF16).astype(F32)
    grad_normed_mix = jnp.swapaxes(grad_normed_mix.reshape(seqs, seg_len, HEADS, depth), 1, 2)
    grad_out, grad_mixed = norm_back(mixed, scale_mix, gain_outf, grad_normed_mix)
    local_part = jnp.einsum("shtd,shte->shde", reach, grad_mixed, precision=lax.Precision.HIGH)
    flipped = jnp.swapaxes(transfer, -1, -2)
    incoming = jnp.zeros_like(local_part)
    for step in range(lax.axis_size("cp") - 1):
        sent = local_part if step == 0 else apply_map(flipped, incoming, local_part)
        incoming = passed_along(sent.astype(BF16), "cp", -1).astype(F32)
    grad_rows, grad_prior, grad_taps, grad_rates = backward_parts(
        projected, before, taps, rates, inverse, updates, weights, carried, grad_mixed, incoming, depth
    )
    returned = passed_along(grad_prior, "cp", -1)
    grad_rows = jnp.concatenate(
        [
            grad_rows[:, :, : seg_len - 8],
            grad_rows[:, :, seg_len - 8 :] + jnp.swapaxes(returned, 0, 1),
        ],
        axis=2,
    ).astype(BF16)
    grad_projected = jnp.moveaxis(grad_rows, 0, 2).reshape(seqs, seg_len, 3 * model)
    grad_rates = jnp.swapaxes(grad_rates[..., 0], 1, 2)
    grad_logits = grad_rates * rates * (1.0 - rates)
    grad_qkv = weight_grad(normed_one, grad_projected).astype(BF16)
    grad_beta = jnp.einsum("sga,sgb->ab", normed_one.astype(F32), grad_logits, precision=lax.Precision.HIGH)
    grad_normed_one = rows_back(grad_projected, w_qkv)
    grad_normed_one = grad_normed_one + jnp.einsum(
        "sgb,ab->sga", grad_logits, w_beta.astype(F32), precision=lax.Precision.HIGH
    )
    grad_mixer, grad_from_first = norm_back(resid_in, scale_one, gain_one.astype(F32), grad_normed_one)
    grad_input = grad_middle + grad_from_first
    grad_conv = jnp.moveaxis(jnp.sum(grad_taps, axis=0), 0, 1).reshape(width, 3 * model)
    grad_conv = jnp.swapaxes(grad_conv.reshape(width, peers, tap_share), 0, 1).reshape(-1)
    sums = lax.psum(jnp.concatenate([squares, grad_out]), BOTH)
    rms_values = jnp.sqrt(sums[:3] / (result.size * peers))
    pieces = [grad_mixer, grad_ffn, grad_beta, grad_conv]
    pieces = jnp.concatenate([piece.reshape(peers, -1) for piece in pieces], axis=1)
    pieces = jnp.pad(pieces, ((0, 0), (0, share * 128 - pieces.shape[1])))
    grad_qkv = jnp.concatenate([grad_qkv, pieces.astype(BF16).reshape(model, 128)], axis=1)
    share_qkv = summed_share(grid, grad_qkv)
    own = share_qkv[:, 3 * model :].reshape(-1)
    share_qkv = share_qkv[:, : 3 * model]
    ends = [share, 2 * share, 2 * share + share * HEADS, 2 * share + share * HEADS + width * tap_share]

    return (
        result.astype(BF16),
        grad_input,
        own[: ends[0]],
        share_qkv,
        own[ends[2] : ends[3]].reshape(width, tap_share),
        own[ends[1] : ends[2]].reshape(share, HEADS),
        sums[3:],
        summed_share(grid, grad_proj),
        own[ends[0] : ends[1]],
        summed_share(grid, grad_gateup),
        summed_share(grid, grad_down),
        rms_values,
    )


def solution(mesh):
    both = P(BOTH)
    rows = P(BOTH, None)
    tokens = P("dp", "cp", None)
    taps = P(None, BOTH)
    in_specs = (tokens, both, rows, taps, rows, P(), rows, both, rows, rows, tokens)
    out_specs = (tokens, tokens, both, rows, taps, rows, P(), rows, both, rows, rows, P())
    return jax.shard_map(
        per_device, mesh=mesh, in_specs=in_specs, out_specs=out_specs, check_vma=False
    )
```

```python
import functools

import jax
import jax.numpy as jnp
from jax import lax
from jax.experimental import pallas as pl
from jax.experimental.pallas import tpu as pltpu
from jax.sharding import PartitionSpec as P

HEADS = 8
PAIR = 4

norm_eps = 1e-05
unit_eps = 1e-06
F32 = jnp.float32
BF16 = jnp.bfloat16


def halves(value):
    high = value.astype(BF16)
    return high, (value - high.astype(F32)).astype(BF16)


NN = (((1,), (0,)), ((), ()))
NT = (((1,), (1,)), ((), ()))
TN = (((0,), (0,)), ((), ()))


def mul(left, right, dims):
    return lax.dot_general(left, right, dims, preferred_element_type=F32)


def mul_split(left, right, dims):
    return (
        mul(left[0], right[0], dims) + mul(left[0], right[1], dims) + mul(left[1], right[0], dims)
    )


def mul_high(left, right, dims):
    left = (left,) if left.dtype == BF16 else halves(left)
    right = (right,) if right.dtype == BF16 else halves(right)
    total = mul(left[0], right[0], dims)
    if len(right) == 2:
        total = total + mul(left[0], right[1], dims)
    if len(left) == 2:
        total = total + mul(left[1], right[0], dims)
    return total


def shifted_down(rows, before, by):
    if by == 0:
        return rows
    rolled = pltpu.roll(rows, by, 0)
    top = pltpu.roll(before, by, 0)
    index = lax.broadcasted_iota(jnp.int32, before.shape, 0)
    first = jnp.where(index < by, top, rolled[: before.shape[0]])
    return jnp.concatenate([first, rolled[before.shape[0] :]], axis=0)


def shifted_up(rows, by):
    if by == 0:
        return rows
    count = rows.shape[0]
    index = lax.broadcasted_iota(jnp.int32, rows.shape, 0)
    return jnp.where(index < count - by, pltpu.roll(rows, count - by, 0), 0.0)


def conv_parts(rows, before, taps):
    width = taps.shape[0]
    conv = None
    for lag in range(width):
        term = taps[lag : lag + 1] * shifted_down(rows, before, width - 1 - lag)
        conv = term if conv is None else conv + term
    return conv


def unit_scale(active):
    return lax.rsqrt(jnp.sum(active * active, axis=-1, keepdims=True) + unit_eps)


def column_of(rates, head):
    index = lax.broadcasted_iota(jnp.int32, rates.shape, 1)
    return jnp.sum(jnp.where(index == head, rates, 0.0), axis=1, keepdims=True)


def row_of(rates, head):
    index = lax.broadcasted_iota(jnp.int32, rates.shape, 0)
    return jnp.sum(jnp.where(index == head, rates, 0.0), axis=0, keepdims=True)


def forward_kernel(
    q_ref, k_ref, v_ref, qb_ref, kb_ref, vb_ref, qt_ref, kt_ref, vt_ref, rates_ref, flipped_ref,
    inverse_ref, updates_ref, weights_ref, reach_ref, mixed_ref, transfer_ref, offset_ref,
):
    depth = transfer_ref.shape[-1]
    size = q_ref.shape[1]
    first = pl.program_id(1) * PAIR
    row = lax.broadcasted_iota(jnp.int32, (size, size), 0)
    col = lax.broadcasted_iota(jnp.int32, (size, size), 1)
    apart = row ^ col
    strict = row > col
    lower = row >= col
    eye = jnp.where(row == col, 1.0, 0.0)
    small_row = lax.broadcasted_iota(jnp.int32, (depth, depth), 0)
    small_col = lax.broadcasted_iota(jnp.int32, (depth, depth), 1)
    small_eye = jnp.where(small_row == small_col, 1.0, 0.0)
    systems, inverses, queries, keys, values, across = [], [], [], [], [], []
    for h in range(PAIR):
        lanes = slice(h * depth, (h + 1) * depth)

        def active(ref, before, taps):
            conv = conv_parts(
                ref[0, :, lanes].astype(F32),
                before[0, :, lanes].astype(F32),
                taps[:, lanes].astype(F32),
            )
            return conv * jax.nn.sigmoid(conv)

        q = active(q_ref, qb_ref, qt_ref)
        k = active(k_ref, kb_ref, kt_ref)
        v = active(v_ref, vb_ref, vt_ref)
        q = (q * unit_scale(q) * depth ** (-0.5)).astype(BF16)
        k = (k * unit_scale(k)).astype(BF16)
        queries.append(q)
        keys.append(k)
        values.append(v.astype(BF16))
        column = column_of(rates_ref[0], first + h)
        across.append(row_of(flipped_ref[0], first + h))
        system = jnp.where(strict, column * mul(k, k, NT), 0.0)
        systems.append(system)
        inverses.append(eye - jnp.where(apart == 1, system, 0.0))
    for level in range(1, size.bit_length() - 1):
        for h in range(PAIR):
            part = jnp.where((apart >> level) == 1, systems[h], 0.0)
            split = halves(inverses[h])
            half_way = mul_split(split, halves(part), NN)
            inverses[h] = inverses[h] - mul_split(halves(half_way), split, NN)
    for h in range(PAIR):
        inverse_ref[0, h] = inverses[h]
        joined = jnp.concatenate([values[h], keys[h]], axis=1)
        solved = mul_high(inverses[h] * across[h], joined, NN)
        updates_ref[0, h] = solved[:, :depth]
        weights_ref[0, h] = solved[:, depth:]
        scores = jnp.where(lower, mul(queries[h], keys[h], NT), 0.0)
        seen = mul_high(scores, solved, NN)
        lanes = slice(h * depth, (h + 1) * depth)
        mixed_ref[0, :, lanes] = seen[:, :depth]
        reach_ref[0, :, lanes] = queries[h].astype(F32) - seen[:, depth:]
        moved = mul_high(keys[h], solved, TN)
        offset_ref[0, h] = moved[:, :depth]
        transfer_ref[0, h] = small_eye - moved[:, depth:]


def cost(microseconds):
    return pl.CostEstimate(flops=int(microseconds * 1.15e9), bytes_accessed=2**20, transcendentals=0)


def specs_of(model, depth, size, width, base=0, seq=None):
    wide = PAIR * depth
    blocks = model // wide

    def three(rows, batched):
        def index(part, s, g):
            column = part * blocks + base + g
            if not batched:
                return (0, column)
            return (s if seq is None else seq, 0, column)

        block = (1, rows, wide) if batched else (rows, wide)
        return [pl.BlockSpec(block, functools.partial(index, part)) for part in range(3)]

    return three(size, True) + three(8, True) + three(width, False), wide


def forward_parts(projected, before, taps, rates, depth):
    seqs, size, model3 = projected.shape
    model = model3 // 3
    token_specs, wide = specs_of(model, depth, size, taps.shape[0])
    rate_spec = pl.BlockSpec((1, size, HEADS), lambda s, g: (s, 0, 0))
    flip_spec = pl.BlockSpec((1, HEADS, size), lambda s, g: (s, 0, 0))

    def out(*dims):
        return pl.BlockSpec((1, PAIR) + dims, lambda s, g: (s, g, 0, 0)), jax.ShapeDtypeStruct((seqs, HEADS) + dims, F32)

    flat = pl.BlockSpec((1, size, wide), lambda s, g: (s, 0, g)), jax.ShapeDtypeStruct((seqs, size, model), F32)
    outs = [out(size, size), out(size, depth), out(size, depth), flat, flat, out(depth, depth), out(depth, depth)]
    return pl.pallas_call(
        forward_kernel,
        grid=(seqs, HEADS // PAIR),
        in_specs=token_specs + [rate_spec, flip_spec],
        out_specs=[o[0] for o in outs],
        out_shape=[o[1] for o in outs],
        compiler_params=pltpu.CompilerParams(vmem_limit_bytes=56 * 2**20),
        cost_estimate=cost(37),
        name="delta_forward",
    )(projected, projected, projected, before, before, before, taps, taps, taps, rates, jnp.swapaxes(rates, 1, 2))


def backward_kernel(
    base, fresh, q_ref, k_ref, v_ref, qb_ref, kb_ref, vb_ref, qt_ref, kt_ref, vt_ref, rates_ref,
    inverse_ref, updates_ref, weights_ref, state_ref, grad_ref, leaving_ref, *refs
):
    rows_ref, last_ref, prior_ref, taps_ref, rate_ref = refs[0 if fresh else 5 :]
    depth = state_ref.shape[-1]
    size = q_ref.shape[1]
    first = base * PAIR
    row = lax.broadcasted_iota(jnp.int32, (size, size), 0)
    col = lax.broadcasted_iota(jnp.int32, (size, size), 1)
    strict = row > col
    lower = row >= col
    index8 = lax.broadcasted_iota(jnp.int32, (8, depth), 0)
    for h in range(PAIR):
        lanes = slice(h * depth, (h + 1) * depth)

        def load(ref, before, taps):
            return (
                ref[0, :, lanes].astype(F32),
                before[0, :, lanes].astype(F32),
                taps[:, lanes].astype(F32),
            )

        def active(parts):
            conv = conv_parts(*parts)
            gate = jax.nn.sigmoid(conv)
            return conv, gate, conv * gate

        raw = [load(q_ref, qb_ref, qt_ref), load(k_ref, kb_ref, kt_ref), load(v_ref, vb_ref, vt_ref)]
        acts = [active(parts) for parts in raw]
        q_scale = unit_scale(acts[0][2])
        k_scale = unit_scale(acts[1][2])
        q = (acts[0][2] * q_scale * depth ** (-0.5)).astype(BF16)
        k = (acts[1][2] * k_scale).astype(BF16)
        v = acts[2][2].astype(BF16)
        column = column_of(rates_ref[0], first + h)
        inverse = inverse_ref[0, h]
        state = state_ref[0, h]
        grad = grad_ref[0, :, lanes]
        leaving = leaving_ref[0, h]
        gram = jnp.where(strict, mul(k, k, NT), 0.0)
        scores = jnp.where(lower, mul(q, k, NT), 0.0)
        errors = updates_ref[0, h] - mul_high(weights_ref[0, h], state, NN)
        missed = v.astype(F32) - mul_high(k, state, NN) - mul_high(gram, errors, NN)
        grad_errors = mul_high(scores, grad, TN) + mul_high(k, leaving, NN)
        grad_right = mul_high(inverse, grad_errors, TN)
        grad_scores = jnp.where(lower, mul_high(grad, errors, NT), 0.0)
        grad_system = jnp.where(strict, -mul_high(grad_right, errors, NT), 0.0) * column
        grad_v = grad_right * column
        grad_q = mul_high(grad, state, NT) + mul_high(grad_scores, k, NN)
        grad_k = (
            mul_high(grad_scores, q, TN)
            + mul_high(errors, leaving, NT)
            - mul_high(grad_v, state, NT)
            + mul_high(grad_system, k, NN)
            + mul_high(grad_system, k, TN)
        )
        rate_ref[0, h] = jnp.sum(grad_right * missed, axis=1, keepdims=True)
        q_un, k_un = acts[0][2], acts[1][2]
        grad_q = (
            q_scale * grad_q
            - q_un * (q_scale * q_scale * q_scale * jnp.sum(grad_q * q_un, axis=1, keepdims=True))
        ) * depth ** (-0.5)
        grad_k = k_scale * grad_k - k_un * (
            k_scale * k_scale * k_scale * jnp.sum(grad_k * k_un, axis=1, keepdims=True)
        )
        for part, grad_act in enumerate((grad_q, grad_k, grad_v)):
            conv, gate, _ = acts[part]
            rows, before, taps = raw[part]
            width = taps.shape[0]
            grad_conv = grad_act * (gate * (1.0 + conv * (1.0 - gate)))
            total = None
            ahead = None
            spot = slice((part * PAIR + h) * depth, (part * PAIR + h + 1) * depth)
            for lag in range(width):
                by = width - 1 - lag
                tap = taps[lag : lag + 1]
                term = tap * shifted_up(grad_conv, by)
                total = term if total is None else total + term
                taps_ref[0, lag : lag + 1, spot] = jnp.sum(
                    grad_conv * shifted_down(rows, before, by), axis=0, keepdims=True
                )
                if by:
                    early = jnp.where(index8 >= 8 - by, tap * pltpu.roll(grad_conv[:8], 8 - by, 0), 0.0)
                    ahead = early if ahead is None else ahead + early
            rows_ref[0, :, spot] = total.astype(BF16)
            last_ref[0, :, spot] = total[size - 8 :]
            prior_ref[0, :, spot] = ahead


def backward_parts(seq, base, held, projected, before, taps, rates, inverse, updates, weights, state, grad, leaving, depth):
    seqs, size, model3 = projected.shape
    model = model3 // 3
    width = taps.shape[0]
    token_specs, wide = specs_of(model, depth, size, width, base, seq)
    rate_spec = pl.BlockSpec((1, size, HEADS), lambda s, g: (seq, 0, 0))

    def heads(*dims):
        return pl.BlockSpec((1, PAIR) + dims, lambda s, g: (seq, base, 0, 0))

    def out(rows, kind):
        return pl.BlockSpec((1, rows, 3 * wide), lambda s, g: (seq, 0, 0)), jax.ShapeDtypeStruct((seqs, rows, 3 * wide), kind)

    rate_out = pl.BlockSpec((1, PAIR, size, 1), lambda s, g: (seq, 0, 0, 0)), jax.ShapeDtypeStruct((seqs, PAIR, size, 1), F32)
    outs = [out(size, BF16), out(8, F32), out(8, F32), out(width, F32), rate_out]
    in_specs = token_specs + [rate_spec, heads(size, size), heads(size, depth), heads(size, depth), heads(depth, depth), pl.BlockSpec((1, size, wide), lambda s, g: (seq, 0, base)), heads(depth, depth)]
    count = len(in_specs)
    return pl.pallas_call(
        functools.partial(backward_kernel, base, not held),
        grid=(1, 1),
        in_specs=in_specs + [pl.BlockSpec(memory_space=pl.ANY)] * len(held),
        out_specs=[o[0] for o in outs],
        out_shape=[o[1] for o in outs],
        input_output_aliases={count + i: i for i in range(len(held))},
        compiler_params=pltpu.CompilerParams(vmem_limit_bytes=56 * 2**20),
        cost_estimate=cost(10),
        name="delta_backward",
    )(projected, projected, projected, before, before, before, taps, taps, taps, rates, inverse, updates, weights, state, grad, leaving, *held)


def mix_kernel(alone_ref, reach_ref, state_ref, gain_ref, mixed_ref, low_ref):
    depth = state_ref.shape[-1]
    for h in range(PAIR):
        lanes = slice(h * depth, (h + 1) * depth)
        mixed = alone_ref[0, :, lanes] + mul_high(reach_ref[0, :, lanes], state_ref[0, h], NN)
        scale = lax.rsqrt(jnp.mean(mixed * mixed, axis=-1, keepdims=True) + norm_eps)
        mixed_ref[0, :, lanes] = mixed
        low_ref[0, :, lanes] = (mixed * scale * gain_ref[...]).astype(BF16)


def mix(alone, reach, state, gain):
    seqs, size, model = alone.shape
    depth = state.shape[-1]
    wide = PAIR * depth
    flat = pl.BlockSpec((1, size, wide), lambda s, g: (s, 0, g))
    return pl.pallas_call(
        mix_kernel,
        grid=(seqs, HEADS // PAIR),
        in_specs=[flat, flat, pl.BlockSpec((1, PAIR, depth, depth), lambda s, g: (s, g, 0, 0)), pl.BlockSpec((1, depth), lambda s, g: (0, 0))],
        out_specs=[flat, flat],
        out_shape=[jax.ShapeDtypeStruct(alone.shape, F32), jax.ShapeDtypeStruct(alone.shape, BF16)],
        cost_estimate=cost(5),
        name="mix_heads",
    )(alone, reach, state, gain.reshape(1, depth))


def mix_back_kernel(mixed_ref, reach_ref, gain_ref, grad_ref, back_ref, local_ref, out_ref):
    depth = local_ref.shape[-1]
    total = None
    for h in range(PAIR):
        lanes = slice(h * depth, (h + 1) * depth)
        mixed = mixed_ref[0, :, lanes]
        grad = grad_ref[0, :, lanes].astype(F32)
        scale = lax.rsqrt(jnp.mean(mixed * mixed, axis=-1, keepdims=True) + norm_eps)
        weighted = grad * gain_ref[...]
        part = jnp.sum(grad * mixed * scale, axis=0, keepdims=True)
        total = part if total is None else total + part
        back = scale * weighted - mixed * (scale * scale * scale) * (
            jnp.mean(weighted * mixed, axis=-1, keepdims=True)
        )
        back_ref[0, :, lanes] = back
        local_ref[0, h] = mul_high(reach_ref[0, :, lanes], back, TN)
    out_ref[0, 0] = jnp.broadcast_to(total, out_ref.shape[2:])


def mix_back(mixed, reach, gain, grad):
    seqs, size, model = mixed.shape
    depth = gain.size
    wide = PAIR * depth
    flat = pl.BlockSpec((1, size, wide), lambda s, g: (s, 0, g))
    back, local, total = pl.pallas_call(
        mix_back_kernel,
        grid=(seqs, HEADS // PAIR),
        in_specs=[flat, flat, pl.BlockSpec((1, depth), lambda s, g: (0, 0)), flat],
        out_specs=[flat, pl.BlockSpec((1, PAIR, depth, depth), lambda s, g: (s, g, 0, 0)), pl.BlockSpec((1, 1, 8, depth), lambda s, g: (s, g, 0, 0))],
        out_shape=[
            jax.ShapeDtypeStruct(mixed.shape, F32),
            jax.ShapeDtypeStruct((seqs, HEADS, depth, depth), F32),
            jax.ShapeDtypeStruct((seqs, HEADS // PAIR, 8, depth), F32),
        ],
        cost_estimate=cost(6),
        name="mix_heads_back",
    )(mixed, reach, gain.reshape(1, depth), grad)
    return back, local, jnp.sum(total[:, :, 0], axis=(0, 1))


BOTH = ("dp", "cp")


class Grid:
    def __init__(self):
        self.cp = lax.axis_size("cp")
        group = lax.axis_size("dp")
        self.core = 2 if group % 2 == 0 else 1
        self.lo = 2 if group // self.core % 2 == 0 else 1
        self.hi = group // self.core // self.lo
        self.sizes = (self.hi, self.lo, self.core, self.cp)

    def place(self):
        member = lax.axis_index("dp")
        return (
            member // (self.lo * self.core),
            member // self.core % self.lo,
            member % self.core,
            lax.axis_index("cp"),
        )

    def swap(self, value, axis, by):
        step = [1] * 4
        for later in range(3):
            step[2 - later] = step[3 - later] * self.sizes[3 - later]
        pairs = []
        for device in range(step[0] * self.sizes[0]):
            here = device // step[axis] % self.sizes[axis]
            pairs.append((device, device + ((here ^ by) - here) * step[axis]))
        return lax.ppermute(value, BOTH, pairs)

    def others(self, value, axis):
        return [self.swap(value, axis, by) for by in range(1, self.sizes[axis])]


HI, LO, CORE, SEG = range(4)


def cut_of(columns):
    return columns // 256 * 128


def place_kernel(cuts, spot, own_left, own_right, other_left, other_right, *outs):
    core = spot[2]
    for away, left, right in ((0, own_left, own_right), (1, other_left, other_right)):
        if away >= outs[0].shape[2]:
            continue
        row = jnp.concatenate([left[0, 0, 0], right[0, 0, 0]], axis=1)
        for out, (top, bottom, first, last) in zip(outs, cuts):
            out[0, 0, core ^ away, 0] = row[top:bottom, first:last]


def tied(value, *needed):
    return lax.optimization_barrier((value, needed))[0] if needed else value


class Gather:
    def __init__(self, grid, shard):
        self.grid = grid
        self.shape = shard.shape
        self.cut = cut_of(shard.shape[1])
        self.mine = shard
        self.sent = [shard]
        self.got = grid.others(shard, SEG)

    def exchange(self, axes):
        self.got = [self.grid.others(piece, axis) for piece, axis in zip(self.sent, axes)]

    def first(self, *needed):
        parts = tied([self.mine] + self.got, *needed)
        self.sent = [
            jnp.stack([part[:, : self.cut] for part in parts]),
            jnp.stack([part[:, self.cut :] for part in parts]),
        ]
        self.exchange((LO, HI))

    def second(self, *needed):
        sent, got = tied((self.sent, self.got), *needed)
        self.sent = [jnp.stack([piece] + more) for piece, more in zip(sent, got)]
        self.exchange((HI, LO))

    def third(self, *needed):
        sent, got = tied((self.sent, self.got), *needed)
        self.own = [
            jnp.stack([piece] + more, axis=axis)
            for piece, more, axis in zip(sent, got, (0, 1))
        ]
        self.sent = self.own
        self.other = [
            self.grid.swap(piece, CORE, 1) if self.grid.core == 2 else piece for piece in self.own
        ]

    def placed(self, cuts, *needed):
        grid, (r, total), cut = self.grid, self.shape, self.cut
        own, other = tied((self.own, self.other), *needed)

        def source(wide):
            return pl.BlockSpec(
                (1, 1, 1, r, wide), lambda a, b, c, spot: (a ^ spot[0], b ^ spot[1], c ^ spot[3], 0, 0)
            )

        shapes = [(bottom - top, right - left) for top, bottom, left, right in cuts]
        sources = [source(cut), source(total - cut)]
        outs = pl.pallas_call(
            functools.partial(place_kernel, cuts),
            grid_spec=pltpu.PrefetchScalarGridSpec(
                num_scalar_prefetch=1,
                grid=(grid.hi, grid.lo, grid.cp),
                in_specs=sources + sources,
                out_specs=[
                    pl.BlockSpec((1, 1, grid.core, 1) + shape, lambda a, b, c, spot: (a, b, 0, c, 0, 0))
                    for shape in shapes
                ],
            ),
            out_shape=[jax.ShapeDtypeStruct(grid.sizes + shape, BF16) for shape in shapes],
            cost_estimate=cost(14),
            name="place_rows",
        )(jnp.stack(grid.place()), *own, *other)
        return [out.reshape(-1, out.shape[-1]) for out in outs]


class Share:
    def __init__(self, grid, values=None, keep=None, send=None):
        self.grid = grid
        self.spots = grid.place()
        self.halved = values is None
        if self.halved:
            self.spots = (0, 0, 0, 0)
        else:
            core = self.spots[2]
            values = [value.reshape(grid.sizes + (-1, value.shape[-1])) for value in values]

            def side(index):
                parts = [lax.dynamic_index_in_dim(value, index, 2, keepdims=False) for value in values]
                return parts[0] if len(parts) == 1 else jnp.concatenate(parts, axis=-2)

            keep, send = [side(core)], [side(core ^ 1)]
        self.sent = send
        self.terms = [
            [k, grid.swap(s, CORE, 1)] if grid.core == 2 else [k] for k, s in zip(keep, send)
        ]

    def begin(self, *moves):
        self.terms = []
        self.sent = []
        for array, axis, dim in moves:
            here = self.spots[axis]

            def pick(index):
                return lax.dynamic_index_in_dim(array, index, dim, keepdims=False)

            sent = [pick(here ^ by) for by in range(1, self.grid.sizes[axis])]
            self.sent += sent
            self.terms.append(
                [pick(here)] + [self.grid.swap(term, axis, by + 1) for by, term in enumerate(sent)]
            )

    def summed(self, kind, *needed):
        totals = []
        for terms in tied(self.terms, *needed):
            total = terms[0].astype(F32)
            for term in terms[1:]:
                total = total + term.astype(F32)
            totals.append(total.astype(kind))
        return totals

    def first(self, *needed):
        totals = self.summed(BF16, *needed)
        if not self.halved:
            (value,) = totals
            cut = cut_of(value.shape[-1])
            totals = [value[..., :cut], value[..., cut:]]
        left, right = totals
        self.begin((left, LO, 1), (right, HI, 0))

    def second(self, *needed):
        left, right = self.summed(BF16, *needed)
        self.begin((left, HI, 0), (right, LO, 0))

    def third(self, *needed):
        left, right = self.summed(BF16, *needed)
        self.begin((jnp.concatenate([left, right], axis=-1), SEG, 0))

    def result(self, *needed):
        return self.summed(F32, *needed)[0]


def all_sum(grid, value):
    for axis in (CORE, LO, HI, SEG):
        by = 1
        while by < grid.sizes[axis]:
            value = value + grid.swap(value, axis, by)
            by *= 2
    return value


def natural_rows(grid, spot, own, other):
    rows = []
    for a in range(grid.hi):
        for b in range(grid.lo):
            for k in range(grid.core):
                for c in range(grid.cp):
                    index = (a ^ spot[0], b ^ spot[1], c ^ spot[3])
                    mine, theirs = own[index], other[index]
                    rows.append(jnp.where(spot[2] == k, mine, theirs))
    return jnp.concatenate(rows, axis=0)


def scatter_rows(grid, spot, value, keep, send):
    r = keep.shape[-2]
    for a in range(grid.hi):
        for b in range(grid.lo):
            for c in range(grid.cp):
                index = (a ^ spot[0], b ^ spot[1], c ^ spot[3])
                at = ((a * grid.lo + b) * grid.core * grid.cp + c) * r
                lower = value[at : at + r]
                at += grid.cp * r
                upper = value[at : at + r]
                keep[index] = jnp.where(spot[2] == 0, lower, upper)
                send[index] = jnp.where(spot[2] == 0, upper, lower)


def feed_kernel(
    grid, spot, rows_ref, flipped_ref, cot_ref, og_ref, ou_ref, tg_ref, tu_ref, down_ref,
    out_ref, back_ref, grad_down_ref, kg_ref, sg_ref, ku_ref, su_ref,
):
    rows, cot = rows_ref[...], cot_ref[...]
    w_gate = natural_rows(grid, spot, og_ref, tg_ref)
    w_up = natural_rows(grid, spot, ou_ref, tu_ref)
    down = down_ref[...]
    gate = mul(rows, w_gate, NN)
    up = mul(rows, w_up, NN)
    sigma = jax.nn.sigmoid(gate)
    act = gate * sigma
    hidden = (act * up).astype(BF16)
    grad_hidden = mul(cot, down, NT)
    grad_gate = (grad_hidden * up * (sigma * (1.0 + gate * (1.0 - sigma)))).astype(BF16)
    grad_up = (grad_hidden * act).astype(BF16)
    out = mul(hidden, down, NN)
    back = mul(grad_gate, w_gate, NT) + mul(grad_up, w_up, NT)

    @pl.when(pl.program_id(0) == 0)
    def _():
        out_ref[...] = out
        back_ref[...] = back

    @pl.when(pl.program_id(0) > 0)
    def _():
        out_ref[...] += out
        back_ref[...] += back

    grad_down_ref[...] = mul(hidden, cot, TN).astype(BF16)
    flipped = flipped_ref[...]
    scatter_rows(grid, spot, mul(flipped, grad_gate, NN).astype(BF16), kg_ref, sg_ref)
    scatter_rows(grid, spot, mul(flipped, grad_up, NN).astype(BF16), ku_ref, su_ref)


def feed_forward(grid, rows, cot, gather, w_down):
    tokens, model = rows.shape
    half = w_down.shape[0]
    tile = 256
    r = gather.shape[0]
    lead = (grid.hi, grid.lo, grid.cp, r)
    whole = pl.BlockSpec((tokens, model), lambda j, spot: (0, 0))
    piece = pl.BlockSpec(lead + (tile,), lambda j, spot: (0, 0, 0, 0, j))
    down = pl.BlockSpec((tile, model), lambda j, spot: (j, 0))
    share = jax.ShapeDtypeStruct(lead + (half,), BF16)
    out, back, grad_down, kg, sg, ku, su = pl.pallas_call(
        functools.partial(feed_kernel, grid),
        grid_spec=pltpu.PrefetchScalarGridSpec(
            num_scalar_prefetch=1,
            grid=(half // tile,),
            in_specs=[whole, pl.BlockSpec((model, tokens), lambda j, spot: (0, 0)), whole] + [piece] * 4 + [down],
            out_specs=[whole, whole, down] + [piece] * 4,
        ),
        out_shape=[
            jax.ShapeDtypeStruct((tokens, model), F32),
            jax.ShapeDtypeStruct((tokens, model), F32),
            jax.ShapeDtypeStruct((half, model), BF16),
            share, share, share, share,
        ],
        compiler_params=pltpu.CompilerParams(vmem_limit_bytes=58 * 2**20),
        cost_estimate=cost(33),
        name="feed_forward",
    )(jnp.stack(grid.place()), rows, rows.T, cot, *gather.own, *gather.other, w_down)
    return out, back, grad_down, (kg, ku), (sg, su)


def passed_along(value, axis, by):
    peers = lax.axis_size(axis)
    pairs = [(i, i + by) for i in range(peers) if 0 <= i + by < peers]
    return lax.ppermute(value, axis, pairs)


def apply_map(transfer, state, offset):
    return jnp.einsum("shij,shjk->shik", transfer, state, precision=lax.Precision.HIGH) + offset


def rows_times(left, right):
    return jnp.einsum("sga,ab->sgb", left, right, preferred_element_type=F32)


def rows_back(grad, weight):
    return jnp.einsum("sgb,ab->sga", grad, weight, preferred_element_type=F32)


def weight_grad(left, right):
    return jnp.einsum("sga,sgb->ab", left, right, preferred_element_type=F32)


def norm_back(rows, scale, gain, grad):
    weighted = grad * gain
    gain_grad = jnp.sum(grad * rows * scale, axis=tuple(range(rows.ndim - 1)))
    width = rows.shape[-1]
    row_grad = scale * weighted - rows * scale**3 * (
        jnp.sum(weighted * rows, axis=-1, keepdims=True) / width
    )
    return (gain_grad, row_grad)


def per_device(
    block_input, mixer_gain, qkv_weight, conv_taps, beta_weight, out_gain,
    proj_weight, ffn_gain, gate_up, down_weight, cotangent,
):
    seqs, seg_len, model = block_input.shape
    width = conv_taps.shape[0]
    depth = model // HEADS
    peers = lax.axis_size(BOTH)
    share = model // peers
    tap_share = conv_taps.shape[1]
    hops = lax.axis_size("cp") - 1
    grid = Grid()

    even = -(-share // 16) * 16
    down_share = down_weight.shape[0]
    mats = jnp.concatenate([jnp.pad(proj_weight, ((0, even - share), (0, 0))), down_weight], axis=0)
    small = jnp.concatenate(
        [mixer_gain, ffn_gain, beta_weight.reshape(-1), conv_taps.reshape(-1)]
    )
    small = jnp.pad(small, (0, share * 128 - small.size)).reshape(share, 128)
    get_qkv = Gather(grid, jnp.concatenate([qkv_weight, small], axis=1))
    get_gateup = Gather(grid, tied(gate_up, *get_qkv.got))
    get_qkv.first()
    get_qkv.second()
    get_qkv.third()
    w_qkv, small = get_qkv.placed(((0, share, 0, 3 * model), (0, share, 3 * model, 3 * model + 128)))
    get_gateup.first(w_qkv)
    get_mats = Gather(grid, tied(mats, *get_gateup.sent))
    small = small.reshape(peers, share * 128)
    gain_one = small[:, :share].reshape(-1)
    gain_two = small[:, share : 2 * share].reshape(-1)
    at = 2 * share
    w_beta = small[:, at : at + share * HEADS].reshape(model, HEADS)
    at += share * HEADS
    taps = small[:, at : at + width * tap_share].reshape(peers, width, tap_share)
    taps = jnp.swapaxes(taps, 0, 1).reshape(width, peers * tap_share)

    gain_outf = out_gain.astype(F32)
    resid_in = block_input.astype(F32)
    scale_one = lax.rsqrt(jnp.mean(resid_in * resid_in, axis=-1, keepdims=True) + norm_eps)
    normed_one = (resid_in * scale_one * gain_one.astype(F32)).astype(BF16)
    normed_one = tied(normed_one, *get_gateup.sent, *get_mats.sent)
    projected = rows_times(normed_one, w_qkv).astype(BF16)
    tail = projected[:, seg_len - (width - 1) :, :]
    before = jnp.pad(passed_along(tail, "cp", 1), ((0, 0), (8 - (width - 1), 0), (0, 0)))
    rates = jax.nn.sigmoid(rows_times(normed_one, w_beta))
    get_gateup.second(projected)
    get_mats.first(projected)
    projected = tied(projected, *get_gateup.sent, *get_mats.sent)
    inverse, updates, weights, reach, alone, transfer, offset = forward_parts(
        projected, before, taps, rates, depth
    )
    carried = jnp.zeros(offset.shape, BF16)
    for step in range(hops):
        sent = offset if step == 0 else apply_map(transfer, carried.astype(F32), offset)
        sent = sent.astype(BF16)
        carried = passed_along(sent, "cp", 1)
        if step == 0:
            get_mats.second(sent)
            get_gateup.third(sent)
            carried = tied(carried, *get_mats.sent, *get_gateup.sent)
        if step == 2:
            get_mats.third(sent)
            w_proj, w_down = get_mats.placed(((0, share, 0, model), (even, even + down_share, 0, model)), sent)
            carried = tied(carried, w_down, w_proj)
    mixed, mixed_low = mix(alone, reach, carried, gain_outf)

    attn = rows_times(mixed_low, w_proj)
    middle = resid_in + attn
    scale_two = lax.rsqrt(jnp.mean(middle * middle, axis=-1, keepdims=True) + norm_eps)
    gain_twof = gain_two.astype(F32)
    normed_two = (middle * scale_two * gain_twof).astype(BF16)
    tokens = seqs * seg_len
    ffn_out, grad_normed_two, grad_down, keep, send = feed_forward(
        grid, normed_two.reshape(tokens, model), cotangent.reshape(tokens, model), get_gateup, w_down
    )
    ffn_out = ffn_out.reshape(middle.shape)
    grad_normed_two = grad_normed_two.reshape(middle.shape)
    put_gateup = Share(grid, keep=keep, send=send)
    result = middle + ffn_out
    squares = jnp.stack(
        [jnp.sum(result * result), jnp.sum(attn * attn), jnp.sum(ffn_out * ffn_out)]
    )
    upstream = cotangent.astype(F32)
    grad_ffn, grad_from_norm = norm_back(middle, scale_two, gain_twof, grad_normed_two)
    grad_middle = upstream + grad_from_norm
    grad_attn = grad_middle.astype(BF16)
    grad_proj = weight_grad(mixed_low, grad_attn).astype(BF16)
    put_mats = Share(grid, [grad_proj, grad_down])
    grad_normed_mix = rows_back(tied(grad_attn, grad_proj), w_proj).astype(BF16)

    grad_mixed, local_part, grad_out = mix_back(mixed, reach, gain_outf, grad_normed_mix)
    flipped = jnp.swapaxes(transfer, -1, -2)
    incoming = jnp.zeros(local_part.shape, BF16)
    for step in range(hops):
        sent = local_part if step == 0 else apply_map(flipped, incoming.astype(F32), local_part)
        sent = sent.astype(BF16)
        incoming = passed_along(sent, "cp", -1)
        if step == 0:
            put_gateup.first(sent)
            incoming = tied(incoming, *put_gateup.sent)
        if step == 1:
            put_mats.first(sent)
            incoming = tied(incoming, *put_mats.sent)
    puts = []
    grad_rows = []
    grad_rates = []
    grad_taps = []
    arrays = (projected, before, taps, rates, inverse, updates, weights, carried, grad_mixed)

    def fixed(held):
        rows, last, prior = held[:3]
        returned = passed_along(prior, "cp", -1)
        return lax.dynamic_update_slice(rows, (last + returned).astype(BF16), (0, seg_len - 8, 0))

    for base in range(HEADS // PAIR):
        held = ()
        for seq in range(seqs):
            held = backward_parts(seq, base, held, *arrays, incoming, depth)
            if (base, seq) == (0, 0):
                put_gateup.second(held[0])
                incoming = tied(incoming, *put_gateup.sent)
            if (base, seq) == (0, seqs - 1):
                put_mats.second(held[0])
                incoming = tied(incoming, *put_mats.sent)
                rows_early = fixed(held)
            if (base, seq) == (1, 0):
                put_gateup.third(held[0])
                rows_early = tied(rows_early, held[0])
                puts.append(Share(grid, [weight_grad(normed_one, rows_early).astype(BF16)]))
                incoming = tied(incoming, *put_gateup.sent, *puts[0].sent)
        grad_rates.append(held[4][..., 0])
        grad_taps.append(jnp.sum(held[3], axis=0))
        grad_rows.append(rows_early if base == 0 else fixed(held))
    puts[0].first(held[0])
    puts.append(None)
    grad_rates = jnp.swapaxes(jnp.concatenate(grad_rates, axis=1), 1, 2)
    grad_logits = grad_rates * rates * (1.0 - rates)
    grad_beta = jnp.einsum("sga,sgb->ab", normed_one.astype(F32), grad_logits, precision=lax.Precision.HIGH)
    wide = PAIR * depth
    grad_conv = jnp.stack([part.reshape(width, 3, wide) for part in grad_taps], axis=2).reshape(width, 3 * model)
    grad_conv = jnp.swapaxes(grad_conv.reshape(width, peers, tap_share), 0, 1)
    pieces = [grad_ffn, grad_beta, grad_conv]
    pieces = jnp.concatenate([piece.reshape(peers, -1) for piece in pieces], axis=1)
    pieces = jnp.pad(pieces, ((0, 0), (0, share * 128 - pieces.shape[1]))).astype(BF16)
    late = weight_grad(normed_one, tied(grad_rows[1], *puts[0].sent)).astype(BF16)
    puts[1] = Share(grid, [jnp.concatenate([late, pieces.reshape(model, 128)], axis=1)])
    grad_rows = tied(grad_rows, *puts[1].sent)
    columns = [rows[..., part * wide : (part + 1) * wide] for part in range(3) for rows in grad_rows]
    grad_normed_one = rows_back(jnp.concatenate(columns, axis=-1), w_qkv)
    puts[1].first(grad_normed_one)
    puts[0].second(grad_normed_one)
    put_mats.third(grad_normed_one)
    grad_normed_one = tied(grad_normed_one, *puts[0].sent, *puts[1].sent, *put_mats.sent)
    grad_normed_one = grad_normed_one + jnp.einsum(
        "sgb,ab->sga", grad_logits, w_beta.astype(F32), precision=lax.Precision.HIGH
    )
    grad_mixer, grad_from_first = norm_back(resid_in, scale_one, gain_one.astype(F32), grad_normed_one)
    grad_input = grad_middle + grad_from_first
    flat = jnp.concatenate([squares, grad_out, grad_mixer])
    flat = jnp.pad(flat, (0, -flat.size % 1024)).reshape(-1, 128)
    sums = all_sum(grid, flat).reshape(-1)
    puts[1].second(grad_input)
    puts[0].third(grad_input)
    puts[1].third()
    shares = [put.result() for put in puts]
    own = shares[1][:, 3 * wide :].reshape(-1)
    shares[1] = shares[1][:, : 3 * wide]
    share_qkv = jnp.stack([part.reshape(share, 3, wide) for part in shares], axis=2).reshape(share, 3 * model)
    share_mats = put_mats.result()
    ends = [share, share + share * HEADS, share + share * HEADS + width * tap_share]
    at = 3 + depth
    mixer_share = lax.dynamic_slice(sums[at : at + model], (lax.axis_index(BOTH) * share,), (share,))
    return (
        result.astype(BF16),
        grad_input,
        mixer_share,
        share_qkv,
        own[ends[1] : ends[2]].reshape(width, tap_share),
        own[ends[0] : ends[1]].reshape(share, HEADS),
        sums[3 : 3 + depth],
        share_mats[:share],
        own[: ends[0]],
        put_gateup.result(),
        share_mats[share:],
        jnp.sqrt(sums[:3] / (result.size * peers)),
    )


def solution(mesh):
    both = P(BOTH)
    rows = P(BOTH, None)
    tokens = P("dp", "cp", None)
    taps = P(None, BOTH)
    in_specs = (tokens, both, rows, taps, rows, P(), rows, both, rows, rows, tokens)
    out_specs = (tokens, tokens, both, rows, taps, rows, P(), rows, both, rows, rows, P())
    return jax.shard_map(
        per_device, mesh=mesh, in_specs=in_specs, out_specs=out_specs, check_vma=False
    )
```

```python
import functools

import jax
import jax.numpy as jnp
from jax import lax
from jax.experimental import pallas as pl
from jax.experimental.pallas import tpu as pltpu
from jax.sharding import PartitionSpec as P

HEADS = 8
PAIR = 4

norm_eps = 1e-05
unit_eps = 1e-06
F32 = jnp.float32
BF16 = jnp.bfloat16


def halves(value):
    high = value.astype(BF16)
    return high, (value - high.astype(F32)).astype(BF16)


NN = (((1,), (0,)), ((), ()))
NT = (((1,), (1,)), ((), ()))
TN = (((0,), (0,)), ((), ()))


def mul(left, right, dims):
    return lax.dot_general(left, right, dims, preferred_element_type=F32)


def mul_halves(left, right, dims):
    total = mul(left[0], right[0], dims)
    if len(right) == 2:
        total = total + mul(left[0], right[1], dims)
    if len(left) == 2:
        total = total + mul(left[1], right[0], dims)
    return total


def side_by_side(array):
    half = array.shape[0] // 2
    return jnp.concatenate([array[:half, :half], array[half:, half:]], axis=1)


def on_diagonal(array):
    half = array.shape[0]
    zero = jnp.zeros((half, half), array.dtype)
    return jnp.concatenate(
        [
            jnp.concatenate([array[:, :half], zero], axis=1),
            jnp.concatenate([zero, array[:, half:]], axis=1),
        ],
        axis=0,
    )


def unit_lower_inverses(lowers):
    size = lowers[0].shape[0]
    half = size // 2
    row = lax.broadcasted_iota(jnp.int32, (half, size), 0)
    col = lax.broadcasted_iota(jnp.int32, (half, size), 1) & (half - 1)
    apart = row ^ col
    zero = jnp.zeros((half, size), BF16)
    packed = [side_by_side(lower) for lower in lowers]
    inverses = [
        jnp.where(row == col, 1.0, 0.0) - jnp.where(apart == 1, lower, zero).astype(F32)
        for lower in packed
    ]
    for level in range(1, half.bit_length() - 1):
        between = (apart >> level) == 1
        splits = [halves(inverse) for inverse in inverses]
        middles = [
            mul_halves((jnp.where(between, lower, zero),), [on_diagonal(piece) for piece in split], NN)
            for lower, split in zip(packed, splits)
        ]
        middles = [[on_diagonal(piece) for piece in halves(middle)] for middle in middles]
        inverses = [
            inverse - mul_halves(split, middle, NN)
            for inverse, split, middle in zip(inverses, splits, middles)
        ]
    splits = [halves(inverse) for inverse in inverses]
    tops = [[piece[:, :half] for piece in split] for split in splits]
    bottoms = [[piece[:, half:] for piece in split] for split in splits]
    middles = [mul_halves((lower[half:, :half],), top, NN) for lower, top in zip(lowers, tops)]
    corners = [
        halves(-mul_halves(bottom, halves(middle), NN)) for bottom, middle in zip(bottoms, middles)
    ]
    return zip(tops, corners, bottoms)


def shifted_down(rows, before, by):
    if by == 0:
        return rows
    rolled = pltpu.roll(rows, by, 0)
    top = pltpu.roll(before, by, 0)
    index = lax.broadcasted_iota(jnp.int32, before.shape, 0)
    first = jnp.where(index < by, top, rolled[: before.shape[0]])
    return jnp.concatenate([first, rolled[before.shape[0] :]], axis=0)


def shifted_up(rows, by):
    if by == 0:
        return rows
    count = rows.shape[0]
    index = lax.broadcasted_iota(jnp.int32, rows.shape, 0)
    return jnp.where(index < count - by, pltpu.roll(rows, count - by, 0), 0.0)


def conv_parts(rows, before, taps):
    width = taps.shape[0]
    conv = None
    for lag in range(width):
        term = taps[lag : lag + 1] * shifted_down(rows, before, width - 1 - lag)
        conv = term if conv is None else conv + term
    return conv


def unit_scale(active):
    return lax.rsqrt(jnp.sum(active * active, axis=-1, keepdims=True) + unit_eps)


def column_of(rates, head):
    index = lax.broadcasted_iota(jnp.int32, rates.shape, 1)
    return jnp.sum(jnp.where(index == head, rates, 0.0), axis=1, keepdims=True)


def forward_kernel(
    q_ref, k_ref, v_ref, qb_ref, kb_ref, vb_ref, qt_ref, kt_ref, vt_ref, rates_ref,
    high_ref, rest_ref, updates_ref, weights_ref, reach_ref, mixed_ref, transfer_ref, offset_ref,
):
    depth = transfer_ref.shape[-1]
    size = q_ref.shape[1]
    half = size // 2
    first = pl.program_id(1) * PAIR
    row = lax.broadcasted_iota(jnp.int32, (size, size), 0)
    col = lax.broadcasted_iota(jnp.int32, (size, size), 1)
    strict = row > col
    lower = row >= col
    small_row = lax.broadcasted_iota(jnp.int32, (depth, depth), 0)
    small_col = lax.broadcasted_iota(jnp.int32, (depth, depth), 1)
    small_eye = jnp.where(small_row == small_col, 1.0, 0.0)
    systems, queries, keys, values, columns = [], [], [], [], []
    for h in range(PAIR):
        lanes = slice(h * depth, (h + 1) * depth)

        def active(ref, before, taps):
            conv = conv_parts(
                ref[0, :, lanes].astype(F32),
                before[0, :, lanes].astype(F32),
                taps[:, lanes].astype(F32),
            )
            return conv * jax.nn.sigmoid(conv)

        q = active(q_ref, qb_ref, qt_ref)
        k = active(k_ref, kb_ref, kt_ref)
        v = active(v_ref, vb_ref, vt_ref)
        q = (q * unit_scale(q) * depth ** (-0.5)).astype(BF16)
        k = (k * unit_scale(k)).astype(BF16)
        queries.append(q)
        keys.append(k)
        values.append(v.astype(BF16))
        columns.append(column_of(rates_ref[0], first + h))
        systems.append(jnp.where(strict, columns[h] * mul(k, k, NT), 0.0).astype(BF16))
    zero = jnp.zeros((half, half), BF16)
    for h, (top, corner, bottom) in enumerate(unit_lower_inverses(systems)):
        inverse = [
            jnp.concatenate(
                [jnp.concatenate([a, zero], axis=1), jnp.concatenate([b, c], axis=1)], axis=0
            )
            for a, b, c in zip(top, corner, bottom)
        ]
        high_ref[0, h] = inverse[0]
        rest_ref[0, h] = inverse[1]
        joined = jnp.concatenate([values[h], keys[h]], axis=1).astype(F32) * columns[h]
        solved = mul_halves(inverse, halves(joined), NN).astype(BF16)
        updates_ref[0, h] = solved[:, :depth]
        weights_ref[0, h] = solved[:, depth:]
        scores = jnp.where(lower, mul(queries[h], keys[h], NT), 0.0)
        seen = mul(scores.astype(BF16), solved, NN)
        lanes = slice(h * depth, (h + 1) * depth)
        mixed_ref[0, :, lanes] = seen[:, :depth]
        reach_ref[0, :, lanes] = (queries[h].astype(F32) - seen[:, depth:]).astype(BF16)
        moved = mul(keys[h], solved, TN)
        offset_ref[0, h] = moved[:, :depth]
        transfer_ref[0, h] = small_eye - moved[:, depth:]


def cost(microseconds):
    return pl.CostEstimate(flops=int(microseconds * 1.15e8), bytes_accessed=2**20, transcendentals=0)


def specs_of(model, depth, size, width, base=0, seq=None):
    wide = PAIR * depth
    blocks = model // wide

    def three(rows, batched):
        def index(part, s, g):
            if not batched:
                return (0, part * blocks + base + g)
            return (s if seq is None else seq, 0, (base + g) * 3 + part)

        block = (1, rows, wide) if batched else (rows, wide)
        return [pl.BlockSpec(block, functools.partial(index, part)) for part in range(3)]

    return three(size, True) + three(8, True) + three(width, False), wide


def forward_parts(projected, before, taps, rates, depth):
    seqs, size, _ = projected.shape
    model = HEADS * depth
    token_specs, wide = specs_of(model, depth, size, taps.shape[0])
    rate_spec = pl.BlockSpec((1, size, HEADS), lambda s, g: (s, 0, 0))

    def out(kind, *dims):
        return pl.BlockSpec((1, PAIR) + dims, lambda s, g: (s, g, 0, 0)), jax.ShapeDtypeStruct((seqs, HEADS) + dims, kind)

    def flat(kind):
        return pl.BlockSpec((1, size, wide), lambda s, g: (s, 0, g)), jax.ShapeDtypeStruct((seqs, size, model), kind)

    outs = [out(BF16, size, size), out(BF16, size, size), out(BF16, size, depth), out(BF16, size, depth)]
    outs += [flat(BF16), flat(F32), out(F32, depth, depth), out(F32, depth, depth)]
    return pl.pallas_call(
        forward_kernel,
        grid=(seqs, HEADS // PAIR),
        in_specs=token_specs + [rate_spec],
        out_specs=[o[0] for o in outs],
        out_shape=[o[1] for o in outs],
        compiler_params=pltpu.CompilerParams(vmem_limit_bytes=56 * 2**20),
        cost_estimate=cost(25),
        name="delta_forward",
    )(projected, projected, projected, before, before, before, taps, taps, taps, rates)


def backward_kernel(
    base, fresh, q_ref, k_ref, v_ref, qb_ref, kb_ref, vb_ref, qt_ref, kt_ref, vt_ref, rates_ref,
    high_ref, rest_ref, updates_ref, weights_ref, state_ref, grad_ref, leaving_ref, *refs
):
    rows_ref, last_ref, prior_ref, taps_ref = refs[0 if fresh else 4 :]
    depth = state_ref.shape[-1]
    size = q_ref.shape[1]
    first = base * PAIR
    row = lax.broadcasted_iota(jnp.int32, (size, size), 0)
    col = lax.broadcasted_iota(jnp.int32, (size, size), 1)
    strict = row > col
    lower = row >= col
    index8 = lax.broadcasted_iota(jnp.int32, (8, depth), 0)
    lane = lax.broadcasted_iota(jnp.int32, (size, 128), 1)
    logits = jnp.zeros((size, 128), F32)
    for h in range(PAIR):
        lanes = slice(h * depth, (h + 1) * depth)

        def load(ref, before, taps):
            return (
                ref[0, :, lanes].astype(F32),
                before[0, :, lanes].astype(F32),
                taps[:, lanes].astype(F32),
            )

        def active(parts):
            conv = conv_parts(*parts)
            gate = jax.nn.sigmoid(conv)
            return conv, gate, conv * gate

        raw = [load(q_ref, qb_ref, qt_ref), load(k_ref, kb_ref, kt_ref), load(v_ref, vb_ref, vt_ref)]
        acts = [active(parts) for parts in raw]
        q_scale = unit_scale(acts[0][2])
        k_scale = unit_scale(acts[1][2])
        q = (acts[0][2] * q_scale * depth ** (-0.5)).astype(BF16)
        k = (acts[1][2] * k_scale).astype(BF16)
        v = acts[2][2].astype(BF16)
        column = column_of(rates_ref[0], first + h)
        inverse = (high_ref[0, h], rest_ref[0, h])
        state = state_ref[0, h]
        grad = grad_ref[0, :, lanes]
        leaving = leaving_ref[0, h]
        gram = jnp.where(strict, mul(k, k, NT), 0.0).astype(BF16)
        scores = jnp.where(lower, mul(q, k, NT), 0.0).astype(BF16)
        errors = (updates_ref[0, h].astype(F32) - mul(weights_ref[0, h], state, NN)).astype(BF16)
        missed = v.astype(F32) - mul(k, state, NN) - mul(gram, errors, NN)
        grad_errors = mul(scores, grad, TN) + mul(k, leaving, NN)
        grad_right = mul_halves(inverse, halves(grad_errors), TN)
        low_right = grad_right.astype(BF16)
        grad_scores = jnp.where(lower, mul(grad, errors, NT), 0.0).astype(BF16)
        grad_system = (jnp.where(strict, -mul(low_right, errors, NT), 0.0) * column).astype(BF16)
        grad_v = grad_right * column
        grad_q = mul(grad, state, NT) + mul(grad_scores, k, NN)
        grad_k = (
            mul(grad_scores, q, TN)
            + mul(errors, leaving, NT)
            - mul(grad_v.astype(BF16), state, NT)
            + mul(grad_system, k, NN)
            + mul(grad_system, k, TN)
        )
        grad_rate = jnp.sum(grad_right * missed, axis=1, keepdims=True)
        grad_logit = grad_rate * column * (1.0 - column)
        logits = jnp.where(lane == first + h, grad_logit, logits)
        q_un, k_un = acts[0][2], acts[1][2]
        grad_q = (
            q_scale * grad_q
            - q_un * (q_scale * q_scale * q_scale * jnp.sum(grad_q * q_un, axis=1, keepdims=True))
        ) * depth ** (-0.5)
        grad_k = k_scale * grad_k - k_un * (
            k_scale * k_scale * k_scale * jnp.sum(grad_k * k_un, axis=1, keepdims=True)
        )
        for part, grad_act in enumerate((grad_q, grad_k, grad_v)):
            conv, gate, _ = acts[part]
            rows, before, taps = raw[part]
            width = taps.shape[0]
            grad_conv = grad_act * (gate * (1.0 + conv * (1.0 - gate)))
            total = None
            ahead = None
            spot = slice((part * PAIR + h) * depth, (part * PAIR + h + 1) * depth)
            for lag in range(width):
                by = width - 1 - lag
                tap = taps[lag : lag + 1]
                term = tap * shifted_up(grad_conv, by)
                total = term if total is None else total + term
                at = (part * PAIR + h) * width + lag
                taps_ref[0, at : at + 1] = jnp.sum(
                    grad_conv * shifted_down(rows, before, by), axis=0, keepdims=True
                )
                if by:
                    early = jnp.where(index8 >= 8 - by, tap * pltpu.roll(grad_conv[:8], 8 - by, 0), 0.0)
                    ahead = early if ahead is None else ahead + early
            rows_ref[0, :size, spot] = total.astype(BF16)
            rows_ref[0, size:, spot] = jnp.concatenate([jnp.zeros_like(ahead), ahead], axis=0).astype(BF16)
            last_ref[0, :, spot] = total[size - 8 :]
            prior_ref[0, :, spot] = ahead
    end = slice(3 * PAIR * depth, 3 * PAIR * depth + 128)
    rows_ref[0, :size, end] = logits.astype(BF16)
    rows_ref[0, size:, end] = jnp.zeros((16, 128), BF16)


def backward_parts(seq, base, held, projected, before, taps, rates, high, rest, updates, weights, state, grad, leaving, depth):
    seqs, size, _ = projected.shape
    model = HEADS * depth
    width = taps.shape[0]
    token_specs, wide = specs_of(model, depth, size, width, base, seq)
    rate_spec = pl.BlockSpec((1, size, HEADS), lambda s, g: (seq, 0, 0))

    def heads(*dims):
        return pl.BlockSpec((1, PAIR) + dims, lambda s, g: (seq, base, 0, 0))

    def out(rows, kind, more=0):
        columns = 3 * wide + more
        return pl.BlockSpec((1, rows, columns), lambda s, g: (seq, 0, 0)), jax.ShapeDtypeStruct((seqs, rows, columns), kind)

    tap_rows = 3 * PAIR * width
    taps_out = pl.BlockSpec((1, tap_rows, depth), lambda s, g: (seq, 0, 0)), jax.ShapeDtypeStruct((seqs, tap_rows, depth), F32)
    outs = [out(size + 16, BF16, 128), out(8, F32), out(8, F32), taps_out]
    in_specs = token_specs + [rate_spec, heads(size, size), heads(size, size), heads(size, depth), heads(size, depth), heads(depth, depth), pl.BlockSpec((1, size, wide), lambda s, g: (seq, 0, base)), heads(depth, depth)]
    count = len(in_specs)
    return pl.pallas_call(
        functools.partial(backward_kernel, base, not held),
        grid=(1, 1),
        in_specs=in_specs + [pl.BlockSpec(memory_space=pl.ANY)] * len(held),
        out_specs=[o[0] for o in outs],
        out_shape=[o[1] for o in outs],
        input_output_aliases={count + i: i for i in range(len(held))},
        compiler_params=pltpu.CompilerParams(vmem_limit_bytes=56 * 2**20),
        cost_estimate=cost(10),
        name="delta_backward",
    )(projected, projected, projected, before, before, before, taps, taps, taps, rates, high, rest, updates, weights, state, grad, leaving, *held)


def mix_kernel(alone_ref, reach_ref, state_ref, gain_ref, mixed_ref, low_ref):
    depth = state_ref.shape[-1]
    for h in range(PAIR):
        lanes = slice(h * depth, (h + 1) * depth)
        mixed = alone_ref[0, :, lanes] + mul(reach_ref[0, :, lanes], state_ref[0, h], NN)
        scale = lax.rsqrt(jnp.mean(mixed * mixed, axis=-1, keepdims=True) + norm_eps)
        mixed_ref[0, :, lanes] = mixed
        low_ref[0, :, lanes] = (mixed * scale * gain_ref[...]).astype(BF16)


def mix(alone, reach, state, gain):
    seqs, size, model = alone.shape
    depth = state.shape[-1]
    wide = PAIR * depth
    flat = pl.BlockSpec((1, size, wide), lambda s, g: (s, 0, g))
    return pl.pallas_call(
        mix_kernel,
        grid=(seqs, HEADS // PAIR),
        in_specs=[flat, flat, pl.BlockSpec((1, PAIR, depth, depth), lambda s, g: (s, g, 0, 0)), pl.BlockSpec((1, depth), lambda s, g: (0, 0))],
        out_specs=[flat, flat],
        out_shape=[jax.ShapeDtypeStruct(alone.shape, F32), jax.ShapeDtypeStruct(alone.shape, BF16)],
        cost_estimate=cost(5),
        name="mix_heads",
    )(alone, reach, state, gain.reshape(1, depth))


def mix_back_kernel(mixed_ref, reach_ref, gain_ref, grad_ref, back_ref, local_ref, out_ref):
    depth = local_ref.shape[-1]
    total = None
    for h in range(PAIR):
        lanes = slice(h * depth, (h + 1) * depth)
        mixed = mixed_ref[0, :, lanes]
        grad = grad_ref[0, :, lanes].astype(F32)
        scale = lax.rsqrt(jnp.mean(mixed * mixed, axis=-1, keepdims=True) + norm_eps)
        weighted = grad * gain_ref[...]
        part = jnp.sum(grad * mixed * scale, axis=0, keepdims=True)
        total = part if total is None else total + part
        back = scale * weighted - mixed * (scale * scale * scale) * (
            jnp.mean(weighted * mixed, axis=-1, keepdims=True)
        )
        back = back.astype(BF16)
        back_ref[0, :, lanes] = back
        local_ref[0, h] = mul(reach_ref[0, :, lanes], back, TN)
    out_ref[0, 0] = jnp.broadcast_to(total, out_ref.shape[2:])


def mix_back(mixed, reach, gain, grad):
    seqs, size, model = mixed.shape
    depth = gain.size
    wide = PAIR * depth
    flat = pl.BlockSpec((1, size, wide), lambda s, g: (s, 0, g))
    back, local, total = pl.pallas_call(
        mix_back_kernel,
        grid=(seqs, HEADS // PAIR),
        in_specs=[flat, flat, pl.BlockSpec((1, depth), lambda s, g: (0, 0)), flat],
        out_specs=[flat, pl.BlockSpec((1, PAIR, depth, depth), lambda s, g: (s, g, 0, 0)), pl.BlockSpec((1, 1, 8, depth), lambda s, g: (s, g, 0, 0))],
        out_shape=[
            jax.ShapeDtypeStruct(mixed.shape, BF16),
            jax.ShapeDtypeStruct((seqs, HEADS, depth, depth), F32),
            jax.ShapeDtypeStruct((seqs, HEADS // PAIR, 8, depth), F32),
        ],
        cost_estimate=cost(6),
        name="mix_heads_back",
    )(mixed, reach, gain.reshape(1, depth), grad)
    return back, local, jnp.sum(total[:, :, 0], axis=(0, 1))


def pack_kernel(mixer_ref, ffn_ref, early_ref, late_ref, rest_ref, out_ref):
    at = 0
    for ref in (mixer_ref, ffn_ref, early_ref, late_ref, rest_ref):
        value = ref[...]
        if len(value.shape) == 3:
            value = jnp.sum(value, axis=0)
        out_ref[at : at + value.shape[0]] = value
        at += value.shape[0]


def packed(*pieces):
    rows = sum(piece.shape[-2] for piece in pieces)
    return pl.pallas_call(
        pack_kernel, out_shape=jax.ShapeDtypeStruct((rows, 128), F32), cost_estimate=cost(2), name="pack_sums"
    )(*pieces)


BOTH = ("dp", "cp")


class Grid:
    def __init__(self):
        self.cp = lax.axis_size("cp")
        group = lax.axis_size("dp")
        self.core = 2 if group % 2 == 0 else 1
        self.lo = 2 if group // self.core % 2 == 0 else 1
        self.hi = group // self.core // self.lo
        self.sizes = (self.hi, self.lo, self.core, self.cp)

    def place(self):
        member = lax.axis_index("dp")
        return (
            member // (self.lo * self.core),
            member // self.core % self.lo,
            member % self.core,
            lax.axis_index("cp"),
        )

    def swap(self, value, axis, by):
        step = [1] * 4
        for later in range(3):
            step[2 - later] = step[3 - later] * self.sizes[3 - later]
        pairs = []
        for device in range(step[0] * self.sizes[0]):
            here = device // step[axis] % self.sizes[axis]
            pairs.append((device, device + ((here ^ by) - here) * step[axis]))
        return lax.ppermute(value, BOTH, pairs)

    def others(self, value, axis):
        return [self.swap(value, axis, by) for by in range(1, self.sizes[axis])]


HI, LO, CORE, SEG = range(4)


def cut_of(columns):
    return columns // 256 * 128


def place_kernel(cuts, spot, own_left, own_right, other_left, other_right, *outs):
    core = spot[2]
    for away, left, right in ((0, own_left, own_right), (1, other_left, other_right)):
        if away >= outs[0].shape[2]:
            continue
        row = jnp.concatenate([left[0, 0, 0], right[0, 0, 0]], axis=1)
        for out, (top, bottom, first, last) in zip(outs, cuts):
            out[0, 0, core ^ away, 0] = row[top:bottom, first:last]


def tied(value, *needed):
    return lax.optimization_barrier((value, needed))[0] if needed else value


class Gather:
    def __init__(self, grid, shard):
        self.grid = grid
        self.shape = shard.shape
        self.cut = cut_of(shard.shape[1])
        self.mine = shard
        self.sent = [shard]
        self.got = grid.others(shard, SEG)

    def exchange(self, axes):
        self.got = [self.grid.others(piece, axis) for piece, axis in zip(self.sent, axes)]

    def first(self, *needed):
        parts = tied([self.mine] + self.got, *needed)
        self.sent = [
            jnp.stack([part[:, : self.cut] for part in parts]),
            jnp.stack([part[:, self.cut :] for part in parts]),
        ]
        self.exchange((LO, HI))

    def second(self, *needed):
        sent, got = tied((self.sent, self.got), *needed)
        self.sent = [jnp.stack([piece] + more) for piece, more in zip(sent, got)]
        self.exchange((HI, LO))

    def third(self, *needed):
        sent, got = tied((self.sent, self.got), *needed)
        self.own = [
            jnp.stack([piece] + more, axis=axis)
            for piece, more, axis in zip(sent, got, (0, 1))
        ]
        self.sent = self.own
        self.other = [
            self.grid.swap(piece, CORE, 1) if self.grid.core == 2 else piece for piece in self.own
        ]

    def placed(self, cuts, *needed):
        grid, (r, total), cut = self.grid, self.shape, self.cut
        own, other = tied((self.own, self.other), *needed)

        def source(wide):
            return pl.BlockSpec(
                (1, 1, 1, r, wide), lambda a, b, c, spot: (a ^ spot[0], b ^ spot[1], c ^ spot[3], 0, 0)
            )

        shapes = [(bottom - top, right - left) for top, bottom, left, right in cuts]
        sources = [source(cut), source(total - cut)]
        outs = pl.pallas_call(
            functools.partial(place_kernel, cuts),
            grid_spec=pltpu.PrefetchScalarGridSpec(
                num_scalar_prefetch=1,
                grid=(grid.hi, grid.lo, grid.cp),
                in_specs=sources + sources,
                out_specs=[
                    pl.BlockSpec((1, 1, grid.core, 1) + shape, lambda a, b, c, spot: (a, b, 0, c, 0, 0))
                    for shape in shapes
                ],
            ),
            out_shape=[jax.ShapeDtypeStruct(grid.sizes + shape, BF16) for shape in shapes],
            cost_estimate=cost(14),
            name="place_rows",
        )(jnp.stack(grid.place()), *own, *other)
        return [out.reshape(-1, out.shape[-1]) for out in outs]


class Share:
    def __init__(self, grid, values=None, keep=None, send=None):
        self.grid = grid
        self.spots = grid.place()
        self.halved = values is None
        self.stacked = False
        if self.halved:
            self.spots = (0, 0, 0, self.spots[SEG])
        else:
            core = self.spots[2]
            values = [value.reshape(grid.sizes + (-1, value.shape[-1])) for value in values]

            keep = [pick(value, core, 2) for value in values]
            send = [pick(value, core ^ 1, 2) for value in values]
        self.sent = send
        self.terms = [
            [k, grid.swap(s, CORE, 1)] if grid.core == 2 else [k] for k, s in zip(keep, send)
        ]

    def begin(self, *moves):
        self.terms = []
        self.sent = []
        self.got = []
        for array, axis, dim in moves:
            here = self.spots[axis]
            mine = pick(array, here, dim)
            sent = [pick(array, here ^ by, dim) for by in range(1, self.grid.sizes[axis])]
            got = [self.grid.swap(term, axis, by + 1) for by, term in enumerate(sent)]
            self.sent += sent
            self.got += got
            self.terms.append([mine] + got)

    def summed(self, *needed):
        return [total_of(terms).astype(BF16) for terms in tied(self.terms, *needed)]

    def first(self, *needed):
        totals = self.summed(*needed)
        if self.halved:
            left, right = totals
            self.begin((left, LO, 0), (right, HI, 0))
        else:
            value = totals[0] if len(totals) == 1 else jnp.concatenate(totals, axis=-2)
            cut = cut_of(value.shape[-1])
            self.begin((value[..., :cut], LO, 1), (value[..., cut:], HI, 0))

    def second(self, *needed):
        left, right = self.summed(*needed)
        self.begin((left, HI, 0), (right, LO, 0))

    def ready(self, *needed, more=()):
        halved = self.summed(*needed)
        for put in more:
            halved = halved + put.summed(*needed)
        self.total = jnp.concatenate(halved, axis=-1)

    def third(self, *needed):
        self.begin((tied(self.total, *needed), SEG, 0))

    def third_at_once(self, *needed):
        self.terms = [[lax.all_to_all(tied(self.total, *needed), "cp", 0, 0)]]
        self.stacked = True

    def result(self, *needed):
        terms = tied(self.terms[0], *needed)
        if self.stacked:
            terms = [terms[0][i] for i in range(self.grid.cp)]
        return total_of(terms)


def total_of(terms):
    total = terms[0].astype(F32)
    for term in terms[1:]:
        total = total + term.astype(F32)
    return total


def pick(array, index, dim):
    if isinstance(index, int):
        return lax.index_in_dim(array, index, dim, keepdims=False)
    return lax.dynamic_index_in_dim(array, index, dim, keepdims=False)


def all_sum(grid, value, across, along):
    for axis in (CORE, LO, HI, SEG):
        by = 1
        while by < grid.sizes[axis]:
            if axis == SEG:
                value = tied(value, *(across if by == 1 else along))
            value = value + grid.swap(value, axis, by)
            by *= 2
    return value


def natural_rows(grid, spot, own, other):
    rows = []
    for a in range(grid.hi):
        for b in range(grid.lo):
            for k in range(grid.core):
                for c in range(grid.cp):
                    index = (a ^ spot[0], b ^ spot[1], c ^ spot[3])
                    mine, theirs = own[index], other[index]
                    rows.append(jnp.where(spot[2] == k, mine, theirs))
    return jnp.concatenate(rows, axis=0)


def scatter_rows(grid, spot, value, keep, send, flip):
    r = keep.shape[-2]
    for a in range(grid.hi):
        for b in range(grid.lo):
            for c in range(grid.cp):
                index = (a ^ spot[0], b ^ spot[1], c)
                if flip:
                    index = (index[1], index[0], index[2])
                at = ((a * grid.lo + b) * grid.core * grid.cp + c) * r
                lower = value[at : at + r]
                at += grid.cp * r
                upper = value[at : at + r]
                keep[index] = jnp.where(spot[2] == 0, lower, upper)
                send[index] = jnp.where(spot[2] == 0, upper, lower)


def feed_kernel(
    grid, spot, rows_ref, flipped_ref, cot_ref, og_ref, ou_ref, tg_ref, tu_ref, down_ref,
    out_ref, back_ref, grad_down_ref, kg_ref, sg_ref, ku_ref, su_ref,
):
    tile = down_ref.shape[0]

    @pl.when(pl.program_id(0) == 0)
    def _():
        out_ref[...] = jnp.zeros(out_ref.shape, F32)
        back_ref[...] = jnp.zeros(back_ref.shape, F32)

    cot, down = cot_ref[...], down_ref[...]
    both = jnp.concatenate(
        [natural_rows(grid, spot, og_ref, tg_ref), natural_rows(grid, spot, ou_ref, tu_ref)], axis=1
    )
    gates = mul(rows_ref[...], both, NN)
    grad_hidden = mul(cot, down, NT)
    gate, up = gates[:, :tile], gates[:, tile:]
    sigma = jax.nn.sigmoid(gate)
    act = gate * sigma
    hidden = (act * up).astype(BF16)
    grad_gate = grad_hidden * up * (sigma * (1.0 + gate * (1.0 - sigma)))
    grads = jnp.concatenate([grad_gate.astype(BF16), (grad_hidden * act).astype(BF16)], axis=1)
    out_ref[...] += mul(hidden, down, NN)
    back_ref[...] += mul(grads, both, NT)
    grad_down_ref[...] = mul(hidden, cot, TN).astype(BF16)
    share = mul(flipped_ref[...], grads, NN)
    scatter_rows(grid, spot, share[:, :tile].astype(BF16), kg_ref, sg_ref, True)
    scatter_rows(grid, spot, share[:, tile:].astype(BF16), ku_ref, su_ref, False)


def feed_forward(grid, rows, cot, gather, w_down):
    tokens, model = rows.shape
    half = w_down.shape[0]
    tile = 256
    r = gather.shape[0]
    lead = (grid.hi, grid.lo, grid.cp, r)
    whole = pl.BlockSpec((tokens, model), lambda j, spot: (0, 0))
    piece = pl.BlockSpec(lead + (tile,), lambda j, spot: (0, 0, 0, 0, j))
    down = pl.BlockSpec((tile, model), lambda j, spot: (j, 0))
    turned = (grid.lo, grid.hi, grid.cp, r)
    left = pl.BlockSpec(turned + (tile,), lambda j, spot: (0, 0, 0, 0, j))
    share = [jax.ShapeDtypeStruct(turned + (half,), BF16)] * 2 + [jax.ShapeDtypeStruct(lead + (half,), BF16)] * 2
    out, back, grad_down, kg, sg, ku, su = pl.pallas_call(
        functools.partial(feed_kernel, grid),
        grid_spec=pltpu.PrefetchScalarGridSpec(
            num_scalar_prefetch=1,
            grid=(half // tile,),
            in_specs=[whole, pl.BlockSpec((model, tokens), lambda j, spot: (0, 0)), whole] + [piece] * 4 + [down],
            out_specs=[whole, whole, down, left, left, piece, piece],
        ),
        out_shape=[
            jax.ShapeDtypeStruct((tokens, model), F32),
            jax.ShapeDtypeStruct((tokens, model), F32),
            jax.ShapeDtypeStruct((half, model), BF16),
            *share,
        ],
        compiler_params=pltpu.CompilerParams(vmem_limit_bytes=58 * 2**20),
        cost_estimate=cost(33),
        name="feed_forward",
    )(jnp.stack(grid.place()), rows, rows.T, cot, *gather.own, *gather.other, w_down)
    return out, back, grad_down, (kg, ku), (sg, su)


def passed_along(value, axis, by):
    peers = lax.axis_size(axis)
    pairs = [(i, i + by) for i in range(peers) if 0 <= i + by < peers]
    return lax.ppermute(value, axis, pairs)


def apply_map(transfer, state, offset):
    return jnp.einsum("shij,shjk->shik", transfer, state, precision=lax.Precision.HIGH) + offset


def rows_times(left, right):
    return jnp.einsum("sga,ab->sgb", left, right, preferred_element_type=F32)


def rows_back(grad, weight):
    return jnp.einsum("sgb,ab->sga", grad, weight, preferred_element_type=F32)


def weight_grad(left, right):
    return jnp.einsum("sga,sgb->ab", left, right, preferred_element_type=F32)


def norm_back(rows, scale, gain, grad):
    weighted = grad * gain
    gain_grad = jnp.sum(grad * rows * scale, axis=tuple(range(rows.ndim - 1)))
    width = rows.shape[-1]
    row_grad = scale * weighted - rows * scale**3 * (
        jnp.sum(weighted * rows, axis=-1, keepdims=True) / width
    )
    return (gain_grad, row_grad)


def per_device(
    block_input, mixer_gain, qkv_weight, conv_taps, beta_weight, out_gain,
    proj_weight, ffn_gain, gate_up, down_weight, cotangent,
):
    seqs, seg_len, model = block_input.shape
    width = conv_taps.shape[0]
    depth = model // HEADS
    peers = lax.axis_size(BOTH)
    share = model // peers
    tap_share = conv_taps.shape[1]
    hops = lax.axis_size("cp") - 1
    grid = Grid()

    even = -(-share // 16) * 16
    down_share = down_weight.shape[0]
    mats = jnp.concatenate([jnp.pad(proj_weight, ((0, even - share), (0, 0))), down_weight], axis=0)
    small = jnp.concatenate(
        [beta_weight, mixer_gain[:, None], ffn_gain[:, None], conv_taps.reshape(share, -1)], axis=1
    )
    small = jnp.pad(small, ((0, 0), (0, 128 - small.shape[1])))
    wide = PAIR * depth
    groups = HEADS // PAIR
    columns = [
        qkv_weight[:, part * model + base * wide : part * model + (base + 1) * wide]
        for base in range(groups)
        for part in range(3)
    ]
    get_qkv = Gather(grid, jnp.concatenate(columns + [small], axis=1))
    get_mats = Gather(grid, tied(mats, *get_qkv.got))
    get_qkv.first()
    get_qkv.second()
    get_gateup = Gather(grid, tied(gate_up, get_qkv.got))
    get_qkv.third(*get_mats.got)
    get_mats.first(*get_qkv.own)
    wide_qkv = 3 * model + 128
    w_qkv, small = get_qkv.placed(
        ((0, share, 0, wide_qkv), (0, share, 3 * model, wide_qkv)), *get_mats.sent
    )
    gain_one = small[:, HEADS]
    gain_two = small[:, HEADS + 1]
    taps = small[:, HEADS + 2 : HEADS + 2 + width * tap_share // share].reshape(peers, width, tap_share)
    taps = jnp.swapaxes(taps, 0, 1).reshape(width, peers * tap_share)

    gain_outf = out_gain.astype(F32)
    resid_in = block_input.astype(F32)
    scale_one = lax.rsqrt(jnp.mean(resid_in * resid_in, axis=-1, keepdims=True) + norm_eps)
    normed_one = (resid_in * scale_one * gain_one.astype(F32)).astype(BF16)
    projected = rows_times(normed_one, w_qkv).astype(BF16)
    tail = jnp.concatenate([projected[:, seg_len - 8 :, : 3 * model], normed_one[:, seg_len - 8 :]], axis=-1)
    before = passed_along(tail, "cp", 1)
    early = lax.broadcasted_iota(jnp.int32, before.shape, 1) < 8 - (width - 1)
    before = jnp.where(early, 0.0, before)
    normed_more = jnp.concatenate(
        [normed_one, jnp.zeros((seqs, 8, model), BF16), before[:, :, 3 * model :]], axis=1
    )
    before = before[:, :, : 3 * model]
    rates = jax.nn.sigmoid(rows_times(normed_one, small)[..., :HEADS])
    get_mats.second(tail)
    get_gateup.first(tail, *get_mats.sent)
    projected = tied(projected, *get_gateup.sent, *get_mats.sent)
    high, rest, updates, weights, reach, alone, transfer, offset = forward_parts(
        projected, before, taps, rates, depth
    )
    carried = jnp.zeros(offset.shape, BF16)
    for step in range(hops):
        sent = offset if step == 0 else apply_map(transfer, carried.astype(F32), offset)
        sent = sent.astype(BF16)
        carried = passed_along(sent, "cp", 1)
        if step == 0:
            get_gateup.second(sent)
            get_mats.third(sent, *get_gateup.sent)
            carried = tied(carried, *get_mats.sent, *get_gateup.sent)
        if step == 2:
            get_gateup.third(sent)
            w_proj, w_down = get_mats.placed(((0, share, 0, model), (even, even + down_share, 0, model)), sent)
            carried = tied(carried, w_down, w_proj)
    mixed, mixed_low = mix(alone, reach, carried, gain_outf)

    attn = rows_times(mixed_low, w_proj)
    middle = resid_in + attn
    scale_two = lax.rsqrt(jnp.mean(middle * middle, axis=-1, keepdims=True) + norm_eps)
    gain_twof = gain_two.astype(F32)
    normed_two = (middle * scale_two * gain_twof).astype(BF16)
    tokens = seqs * seg_len
    ffn_out, grad_normed_two, grad_down, keep, send = feed_forward(
        grid, normed_two.reshape(tokens, model), cotangent.reshape(tokens, model), get_gateup, w_down
    )
    ffn_out = ffn_out.reshape(middle.shape)
    put_gateup = Share(grid, keep=keep, send=send)
    result = middle + ffn_out
    squares = jnp.stack(
        [jnp.sum(result * result), jnp.sum(attn * attn), jnp.sum(ffn_out * ffn_out)]
    )
    upstream = cotangent.astype(F32)
    grad_normed_two = grad_normed_two.reshape(middle.shape)
    grad_ffn, grad_from_norm = norm_back(middle, scale_two, gain_twof, grad_normed_two)
    grad_middle = upstream + grad_from_norm
    grad_attn = grad_middle.astype(BF16)
    grad_proj = weight_grad(mixed_low, grad_attn).astype(BF16)
    grad_normed_mix = rows_back(tied(grad_attn, grad_proj), w_proj).astype(BF16)

    grad_mixed, local_part, grad_out = mix_back(mixed, reach, gain_outf, grad_normed_mix)
    flipped = jnp.swapaxes(transfer, -1, -2)
    incoming = jnp.zeros(local_part.shape, BF16)
    for step in range(hops):
        sent = local_part if step == 0 else apply_map(flipped, incoming.astype(F32), local_part)
        sent = sent.astype(BF16)
        incoming = passed_along(sent, "cp", -1)
        if step == 0:
            put_gateup.first(sent)
            incoming = tied(incoming, *put_gateup.sent)
        if step == 1:
            put_mats = Share(grid, tied([grad_proj, grad_down], sent))
            incoming = tied(incoming, *put_mats.sent)
        if step == 2:
            put_mats.first(sent)
            incoming = tied(incoming, *put_mats.sent)
    puts = []
    arrays = (projected, before, taps, rates, high, rest, updates, weights, carried, grad_mixed)

    for base in range(HEADS // PAIR):
        held = ()
        for seq in range(seqs):
            held = backward_parts(seq, base, held, *arrays, incoming, depth)
            if (base, seq) == (0, 0):
                put_gateup.second(held[0])
                incoming = tied(incoming, *put_gateup.sent)
            if (base, seq) == (0, seqs - 1):
                kept = held
                put_mats.second(held[0])
                puts.append(Share(grid, [weight_grad(normed_more, held[0]).astype(BF16)]))
                incoming = tied(incoming, *put_mats.sent, *puts[0].sent)
            if (base, seq) == (1, 0):
                put_gateup.ready(held[0])
                put_gateup.third_at_once()
                put_mats.ready(held[0])
                puts[0].first(held[0])
                incoming = tied(incoming, put_gateup.total, put_mats.total, *puts[0].sent)
    late = weight_grad(normed_more, held[0]).astype(BF16)
    puts.append(Share(grid, [late]))
    put_mats.third_at_once(held[0])
    puts[0].second(*puts[1].sent)
    kept, held = tied((kept, held), *puts[0].sent)
    last_rows = jnp.concatenate([kept[1], held[1]], axis=-1) + passed_along(
        jnp.concatenate([kept[2], held[2]], axis=-1), "cp", -1
    )
    logits = kept[0][:, :seg_len, 3 * wide :] + held[0][:, :seg_len, 3 * wide :]
    grad_projected = jnp.concatenate(
        [kept[0][:, :seg_len, : 3 * wide], held[0][:, :seg_len, : 3 * wide], logits], axis=-1
    )
    puts[1].first(grad_projected, put_gateup.terms[0][0], *puts[0].got)
    last_rows = tied(last_rows, *puts[1].sent)
    grad_projected = lax.dynamic_update_slice(grad_projected, last_rows.astype(BF16), (0, seg_len - 8, 0))
    grad_normed_one = rows_back(grad_projected, w_qkv)
    grad_mixer, grad_from_first = norm_back(resid_in, scale_one, gain_one.astype(F32), grad_normed_one)
    across = puts[1].got
    puts[1].second(put_mats.terms[0][0])
    along = puts[1].got
    grad_input = grad_middle + grad_from_first
    rest = jnp.pad(jnp.concatenate([squares, grad_out]), (0, 256 - 3 - depth)).reshape(2, 128)
    flat = packed(grad_mixer.reshape(-1, 128), grad_ffn.reshape(-1, 128), kept[3], held[3], rest)
    sums = all_sum(grid, flat, across, along)
    counts = [model // 128] * 2 + [6 * PAIR * width, 2]
    starts = [sum(counts[:i]) for i in range(4)]
    found = [sums[start : start + count].reshape(-1) for start, count in zip(starts, counts)]
    puts[1].ready(more=(puts[0],))
    puts[1].third()
    both = puts[1].result()
    held_columns = 3 * wide + 128
    second, first = both[:, :held_columns], both[:, held_columns:]
    share_beta = first[:, 3 * wide : 3 * wide + HEADS] + second[:, 3 * wide : 3 * wide + HEADS]
    parts = [part[:, : 3 * wide].reshape(share, 3, wide) for part in (first, second)]
    share_qkv = jnp.stack(parts, axis=2).reshape(share, 3 * model)
    grad_taps = found[2].reshape(HEADS // PAIR, 3, PAIR, width, depth)
    grad_taps = jnp.transpose(grad_taps, (3, 1, 0, 2, 4)).reshape(width, 3 * model)
    share_gateup = put_gateup.result(*puts[1].sent)
    share_mats = put_mats.result(*puts[1].sent)
    me = lax.axis_index(BOTH)

    def mine(array, count):
        return lax.dynamic_slice_in_dim(array, me * count, count, axis=-1)

    return (
        result.astype(BF16),
        grad_input,
        mine(found[0], share),
        share_qkv,
        mine(grad_taps, tap_share),
        share_beta,
        found[3][3 : 3 + depth],
        share_mats[:share],
        mine(found[1], share),
        share_gateup,
        share_mats[share:],
        jnp.sqrt(found[3][:3] / (result.size * peers)),
    )


def solution(mesh):
    both = P(BOTH)
    rows = P(BOTH, None)
    tokens = P("dp", "cp", None)
    taps = P(None, BOTH)
    in_specs = (tokens, both, rows, taps, rows, P(), rows, both, rows, rows, tokens)
    out_specs = (tokens, tokens, both, rows, taps, rows, P(), rows, both, rows, rows, P())
    return jax.shard_map(
        per_device, mesh=mesh, in_specs=in_specs, out_specs=out_specs, check_vma=False
    )
```

```python
import functools

import jax
import jax.numpy as jnp
from jax import lax
from jax.experimental import pallas as pl
from jax.experimental.pallas import tpu as pltpu
from jax.sharding import PartitionSpec as P

HEADS = 8
PAIR = 4

norm_eps = 1e-05
unit_eps = 1e-06
F32 = jnp.float32
BF16 = jnp.bfloat16


def halves(value):
    high = value.astype(BF16)
    return high, (value - high.astype(F32)).astype(BF16)


NN = (((1,), (0,)), ((), ()))
NT = (((1,), (1,)), ((), ()))
TN = (((0,), (0,)), ((), ()))


def mul(left, right, dims):
    return lax.dot_general(left, right, dims, preferred_element_type=F32)


def mul_halves(left, right, dims):
    total = mul(left[0], right[0], dims)
    if len(right) == 2:
        total = total + mul(left[0], right[1], dims)
    if len(left) == 2:
        total = total + mul(left[1], right[0], dims)
    return total


def side_by_side(array):
    half = array.shape[0] // 2
    return jnp.concatenate([array[:half, :half], array[half:, half:]], axis=1)


def on_diagonal(array):
    half = array.shape[0]
    zero = jnp.zeros((half, half), array.dtype)
    return jnp.concatenate(
        [
            jnp.concatenate([array[:, :half], zero], axis=1),
            jnp.concatenate([zero, array[:, half:]], axis=1),
        ],
        axis=0,
    )


def unit_lower_inverses(lowers):
    size = lowers[0].shape[0]
    half = size // 2
    row = lax.broadcasted_iota(jnp.int32, (half, size), 0)
    col = lax.broadcasted_iota(jnp.int32, (half, size), 1) & (half - 1)
    apart = row ^ col
    zero = jnp.zeros((half, size), BF16)
    packed = [side_by_side(lower) for lower in lowers]
    inverses = [
        jnp.where(row == col, 1.0, 0.0) - jnp.where(apart == 1, lower, zero).astype(F32)
        for lower in packed
    ]
    for level in range(1, half.bit_length() - 1):
        between = (apart >> level) == 1
        splits = [halves(inverse) for inverse in inverses]
        middles = [
            mul_halves((jnp.where(between, lower, zero),), [on_diagonal(piece) for piece in split], NN)
            for lower, split in zip(packed, splits)
        ]
        middles = [[on_diagonal(piece) for piece in halves(middle)] for middle in middles]
        inverses = [
            inverse - mul_halves(split, middle, NN)
            for inverse, split, middle in zip(inverses, splits, middles)
        ]
    splits = [halves(inverse) for inverse in inverses]
    tops = [[piece[:, :half] for piece in split] for split in splits]
    bottoms = [[piece[:, half:] for piece in split] for split in splits]
    middles = [mul_halves((lower[half:, :half],), top, NN) for lower, top in zip(lowers, tops)]
    corners = [
        halves(-mul_halves(bottom, halves(middle), NN)) for bottom, middle in zip(bottoms, middles)
    ]
    return zip(tops, corners, bottoms)


def shifted_down(rows, before, by):
    if by == 0:
        return rows
    rolled = pltpu.roll(rows, by, 0)
    top = pltpu.roll(before, by, 0)
    index = lax.broadcasted_iota(jnp.int32, before.shape, 0)
    first = jnp.where(index < by, top, rolled[: before.shape[0]])
    return jnp.concatenate([first, rolled[before.shape[0] :]], axis=0)


def shifted_up(rows, by):
    if by == 0:
        return rows
    count = rows.shape[0]
    index = lax.broadcasted_iota(jnp.int32, rows.shape, 0)
    return jnp.where(index < count - by, pltpu.roll(rows, count - by, 0), 0.0)


def conv_parts(rows, before, taps):
    width = taps.shape[0]
    conv = None
    for lag in range(width):
        term = taps[lag : lag + 1] * shifted_down(rows, before, width - 1 - lag)
        conv = term if conv is None else conv + term
    return conv


def unit_scale(active):
    return lax.rsqrt(jnp.sum(active * active, axis=-1, keepdims=True) + unit_eps)


def column_of(rates, head):
    index = lax.broadcasted_iota(jnp.int32, rates.shape, 1)
    return jnp.sum(jnp.where(index == head, rates, 0.0), axis=1, keepdims=True)


def forward_kernel(
    q_ref, k_ref, v_ref, qb_ref, kb_ref, vb_ref, qt_ref, kt_ref, vt_ref, rates_ref,
    high_ref, rest_ref, updates_ref, weights_ref, reach_ref, mixed_ref, transfer_ref, offset_ref,
):
    depth = transfer_ref.shape[-1]
    size = q_ref.shape[1]
    half = size // 2
    first = pl.program_id(1) * PAIR
    row = lax.broadcasted_iota(jnp.int32, (size, size), 0)
    col = lax.broadcasted_iota(jnp.int32, (size, size), 1)
    strict = row > col
    lower = row >= col
    small_row = lax.broadcasted_iota(jnp.int32, (depth, depth), 0)
    small_col = lax.broadcasted_iota(jnp.int32, (depth, depth), 1)
    small_eye = jnp.where(small_row == small_col, 1.0, 0.0)
    systems, queries, keys, values, columns = [], [], [], [], []
    for h in range(PAIR):
        lanes = slice(h * depth, (h + 1) * depth)

        def active(ref, before, taps):
            conv = conv_parts(
                ref[0, :, lanes].astype(F32),
                before[0, :, lanes].astype(F32),
                taps[:, lanes].astype(F32),
            )
            return conv * jax.nn.sigmoid(conv)

        q = active(q_ref, qb_ref, qt_ref)
        k = active(k_ref, kb_ref, kt_ref)
        v = active(v_ref, vb_ref, vt_ref)
        q = (q * unit_scale(q) * depth ** (-0.5)).astype(BF16)
        k = (k * unit_scale(k)).astype(BF16)
        queries.append(q)
        keys.append(k)
        values.append(v.astype(BF16))
        columns.append(column_of(rates_ref[0], first + h))
        systems.append(jnp.where(strict, columns[h] * mul(k, k, NT), 0.0).astype(BF16))
    zero = jnp.zeros((half, half), BF16)
    for h, (top, corner, bottom) in enumerate(unit_lower_inverses(systems)):
        inverse = [
            jnp.concatenate(
                [jnp.concatenate([a, zero], axis=1), jnp.concatenate([b, c], axis=1)], axis=0
            )
            for a, b, c in zip(top, corner, bottom)
        ]
        high_ref[0, h] = inverse[0]
        rest_ref[0, h] = inverse[1]
        joined = jnp.concatenate([values[h], keys[h]], axis=1).astype(F32) * columns[h]
        solved = mul_halves(inverse, halves(joined), NN).astype(BF16)
        updates_ref[0, h] = solved[:, :depth]
        weights_ref[0, h] = solved[:, depth:]
        scores = jnp.where(lower, mul(queries[h], keys[h], NT), 0.0)
        seen = mul(scores.astype(BF16), solved, NN)
        lanes = slice(h * depth, (h + 1) * depth)
        mixed_ref[0, :, lanes] = seen[:, :depth]
        reach_ref[0, :, lanes] = (queries[h].astype(F32) - seen[:, depth:]).astype(BF16)
        moved = mul(keys[h], solved, TN)
        offset_ref[0, h] = moved[:, :depth]
        transfer_ref[0, h] = small_eye - moved[:, depth:]


def cost(microseconds):
    return pl.CostEstimate(flops=int(microseconds * 1.15e8), bytes_accessed=2**20, transcendentals=0)


def specs_of(model, depth, size, width, base=0, seq=None):
    wide = PAIR * depth
    blocks = model // wide

    def three(rows, batched):
        def index(part, s, g):
            if not batched:
                return (0, part * blocks + base + g)
            return (s if seq is None else seq, 0, (base + g) * 3 + part)

        block = (1, rows, wide) if batched else (rows, wide)
        return [pl.BlockSpec(block, functools.partial(index, part)) for part in range(3)]

    return three(size, True) + three(8, True) + three(width, False), wide


def forward_parts(projected, before, taps, rates, depth):
    seqs, size, _ = projected.shape
    model = HEADS * depth
    token_specs, wide = specs_of(model, depth, size, taps.shape[0])
    rate_spec = pl.BlockSpec((1, size, HEADS), lambda s, g: (s, 0, 0))

    def out(kind, *dims):
        return pl.BlockSpec((1, PAIR) + dims, lambda s, g: (s, g, 0, 0)), jax.ShapeDtypeStruct((seqs, HEADS) + dims, kind)

    def flat(kind):
        return pl.BlockSpec((1, size, wide), lambda s, g: (s, 0, g)), jax.ShapeDtypeStruct((seqs, size, model), kind)

    outs = [out(BF16, size, size), out(BF16, size, size), out(BF16, size, depth), out(BF16, size, depth)]
    outs += [flat(BF16), flat(F32), out(F32, depth, depth), out(F32, depth, depth)]
    return pl.pallas_call(
        forward_kernel,
        grid=(seqs, HEADS // PAIR),
        in_specs=token_specs + [rate_spec],
        out_specs=[o[0] for o in outs],
        out_shape=[o[1] for o in outs],
        compiler_params=pltpu.CompilerParams(vmem_limit_bytes=56 * 2**20),
        cost_estimate=cost(25),
        name="delta_forward",
    )(projected, projected, projected, before, before, before, taps, taps, taps, rates)


def backward_kernel(
    base, fresh, q_ref, k_ref, v_ref, qb_ref, kb_ref, vb_ref, qt_ref, kt_ref, vt_ref, rates_ref,
    high_ref, rest_ref, updates_ref, weights_ref, state_ref, grad_ref, leaving_ref, *refs
):
    rows_ref, last_ref, prior_ref, taps_ref = refs[0 if fresh else 4 :]
    depth = state_ref.shape[-1]
    size = q_ref.shape[1]
    first = base * PAIR
    row = lax.broadcasted_iota(jnp.int32, (size, size), 0)
    col = lax.broadcasted_iota(jnp.int32, (size, size), 1)
    strict = row > col
    lower = row >= col
    index8 = lax.broadcasted_iota(jnp.int32, (8, depth), 0)
    lane = lax.broadcasted_iota(jnp.int32, (size, 128), 1)
    logits = jnp.zeros((size, 128), F32)
    for h in range(PAIR):
        lanes = slice(h * depth, (h + 1) * depth)

        def load(ref, before, taps):
            return (
                ref[0, :, lanes].astype(F32),
                before[0, :, lanes].astype(F32),
                taps[:, lanes].astype(F32),
            )

        def active(parts):
            conv = conv_parts(*parts)
            gate = jax.nn.sigmoid(conv)
            return conv, gate, conv * gate

        raw = [load(q_ref, qb_ref, qt_ref), load(k_ref, kb_ref, kt_ref), load(v_ref, vb_ref, vt_ref)]
        acts = [active(parts) for parts in raw]
        q_scale = unit_scale(acts[0][2])
        k_scale = unit_scale(acts[1][2])
        q = (acts[0][2] * q_scale * depth ** (-0.5)).astype(BF16)
        k = (acts[1][2] * k_scale).astype(BF16)
        v = acts[2][2].astype(BF16)
        column = column_of(rates_ref[0], first + h)
        inverse = (high_ref[0, h], rest_ref[0, h])
        state = state_ref[0, h]
        grad = grad_ref[0, :, lanes]
        leaving = leaving_ref[0, h]
        gram = jnp.where(strict, mul(k, k, NT), 0.0).astype(BF16)
        scores = jnp.where(lower, mul(q, k, NT), 0.0).astype(BF16)
        errors = (updates_ref[0, h].astype(F32) - mul(weights_ref[0, h], state, NN)).astype(BF16)
        missed = v.astype(F32) - mul(k, state, NN) - mul(gram, errors, NN)
        grad_errors = mul(scores, grad, TN) + mul(k, leaving, NN)
        grad_right = mul_halves(inverse, halves(grad_errors), TN)
        low_right = grad_right.astype(BF16)
        grad_scores = jnp.where(lower, mul(grad, errors, NT), 0.0).astype(BF16)
        grad_system = (jnp.where(strict, -mul(low_right, errors, NT), 0.0) * column).astype(BF16)
        grad_v = grad_right * column
        grad_q = mul(grad, state, NT) + mul(grad_scores, k, NN)
        grad_k = (
            mul(grad_scores, q, TN)
            + mul(errors, leaving, NT)
            - mul(grad_v.astype(BF16), state, NT)
            + mul(grad_system, k, NN)
            + mul(grad_system, k, TN)
        )
        grad_rate = jnp.sum(grad_right * missed, axis=1, keepdims=True)
        grad_logit = grad_rate * column * (1.0 - column)
        logits = jnp.where(lane == first + h, grad_logit, logits)
        q_un, k_un = acts[0][2], acts[1][2]
        grad_q = (
            q_scale * grad_q
            - q_un * (q_scale * q_scale * q_scale * jnp.sum(grad_q * q_un, axis=1, keepdims=True))
        ) * depth ** (-0.5)
        grad_k = k_scale * grad_k - k_un * (
            k_scale * k_scale * k_scale * jnp.sum(grad_k * k_un, axis=1, keepdims=True)
        )
        for part, grad_act in enumerate((grad_q, grad_k, grad_v)):
            conv, gate, _ = acts[part]
            rows, before, taps = raw[part]
            width = taps.shape[0]
            grad_conv = grad_act * (gate * (1.0 + conv * (1.0 - gate)))
            total = None
            ahead = None
            spot = slice((part * PAIR + h) * depth, (part * PAIR + h + 1) * depth)
            for lag in range(width):
                by = width - 1 - lag
                tap = taps[lag : lag + 1]
                term = tap * shifted_up(grad_conv, by)
                total = term if total is None else total + term
                at = (part * PAIR + h) * width + lag
                taps_ref[0, at : at + 1] = jnp.sum(
                    grad_conv * shifted_down(rows, before, by), axis=0, keepdims=True
                )
                if by:
                    early = jnp.where(index8 >= 8 - by, tap * pltpu.roll(grad_conv[:8], 8 - by, 0), 0.0)
                    ahead = early if ahead is None else ahead + early
            rows_ref[0, :size, spot] = total.astype(BF16)
            rows_ref[0, size:, spot] = jnp.concatenate([jnp.zeros_like(ahead), ahead], axis=0).astype(BF16)
            last_ref[0, :, spot] = total[size - 8 :]
            prior_ref[0, :, spot] = ahead
    end = slice(3 * PAIR * depth, 3 * PAIR * depth + 128)
    rows_ref[0, :size, end] = logits.astype(BF16)
    rows_ref[0, size:, end] = jnp.zeros((16, 128), BF16)


def backward_parts(seq, base, held, projected, before, taps, rates, high, rest, updates, weights, state, grad, leaving, depth):
    seqs, size, _ = projected.shape
    model = HEADS * depth
    width = taps.shape[0]
    token_specs, wide = specs_of(model, depth, size, width, base, seq)
    rate_spec = pl.BlockSpec((1, size, HEADS), lambda s, g: (seq, 0, 0))

    def heads(*dims):
        return pl.BlockSpec((1, PAIR) + dims, lambda s, g: (seq, base, 0, 0))

    def out(rows, kind, more=0):
        columns = 3 * wide + more
        return pl.BlockSpec((1, rows, columns), lambda s, g: (seq, 0, 0)), jax.ShapeDtypeStruct((seqs, rows, columns), kind)

    tap_rows = 3 * PAIR * width
    taps_out = pl.BlockSpec((1, tap_rows, depth), lambda s, g: (seq, 0, 0)), jax.ShapeDtypeStruct((seqs, tap_rows, depth), F32)
    outs = [out(size + 16, BF16, 128), out(8, F32), out(8, F32), taps_out]
    in_specs = token_specs + [rate_spec, heads(size, size), heads(size, size), heads(size, depth), heads(size, depth), heads(depth, depth), pl.BlockSpec((1, size, wide), lambda s, g: (seq, 0, base)), heads(depth, depth)]
    count = len(in_specs)
    return pl.pallas_call(
        functools.partial(backward_kernel, base, not held),
        grid=(1, 1),
        in_specs=in_specs + [pl.BlockSpec(memory_space=pl.ANY)] * len(held),
        out_specs=[o[0] for o in outs],
        out_shape=[o[1] for o in outs],
        input_output_aliases={count + i: i for i in range(len(held))},
        compiler_params=pltpu.CompilerParams(vmem_limit_bytes=56 * 2**20),
        cost_estimate=cost(10),
        name="delta_backward",
    )(projected, projected, projected, before, before, before, taps, taps, taps, rates, high, rest, updates, weights, state, grad, leaving, *held)


def mix_kernel(alone_ref, reach_ref, state_ref, gain_ref, mixed_ref, low_ref):
    depth = state_ref.shape[-1]
    for h in range(PAIR):
        lanes = slice(h * depth, (h + 1) * depth)
        mixed = alone_ref[0, :, lanes] + mul(reach_ref[0, :, lanes], state_ref[0, h], NN)
        scale = lax.rsqrt(jnp.mean(mixed * mixed, axis=-1, keepdims=True) + norm_eps)
        mixed_ref[0, :, lanes] = mixed
        low_ref[0, :, lanes] = (mixed * scale * gain_ref[...]).astype(BF16)


def mix(alone, reach, state, gain):
    seqs, size, model = alone.shape
    depth = state.shape[-1]
    wide = PAIR * depth
    flat = pl.BlockSpec((1, size, wide), lambda s, g: (s, 0, g))
    return pl.pallas_call(
        mix_kernel,
        grid=(seqs, HEADS // PAIR),
        in_specs=[flat, flat, pl.BlockSpec((1, PAIR, depth, depth), lambda s, g: (s, g, 0, 0)), pl.BlockSpec((1, depth), lambda s, g: (0, 0))],
        out_specs=[flat, flat],
        out_shape=[jax.ShapeDtypeStruct(alone.shape, F32), jax.ShapeDtypeStruct(alone.shape, BF16)],
        cost_estimate=cost(5),
        name="mix_heads",
    )(alone, reach, state, gain.reshape(1, depth))


def mix_back_kernel(mixed_ref, reach_ref, gain_ref, grad_ref, back_ref, local_ref, out_ref):
    depth = local_ref.shape[-1]
    total = None
    for h in range(PAIR):
        lanes = slice(h * depth, (h + 1) * depth)
        mixed = mixed_ref[0, :, lanes]
        grad = grad_ref[0, :, lanes].astype(F32)
        scale = lax.rsqrt(jnp.mean(mixed * mixed, axis=-1, keepdims=True) + norm_eps)
        weighted = grad * gain_ref[...]
        part = jnp.sum(grad * mixed * scale, axis=0, keepdims=True)
        total = part if total is None else total + part
        back = scale * weighted - mixed * (scale * scale * scale) * (
            jnp.mean(weighted * mixed, axis=-1, keepdims=True)
        )
        back = back.astype(BF16)
        back_ref[0, :, lanes] = back
        local_ref[0, h] = mul(reach_ref[0, :, lanes], back, TN)
    out_ref[0, 0] = jnp.broadcast_to(total, out_ref.shape[2:])


def mix_back(mixed, reach, gain, grad):
    seqs, size, model = mixed.shape
    depth = gain.size
    wide = PAIR * depth
    flat = pl.BlockSpec((1, size, wide), lambda s, g: (s, 0, g))
    back, local, total = pl.pallas_call(
        mix_back_kernel,
        grid=(seqs, HEADS // PAIR),
        in_specs=[flat, flat, pl.BlockSpec((1, depth), lambda s, g: (0, 0)), flat],
        out_specs=[flat, pl.BlockSpec((1, PAIR, depth, depth), lambda s, g: (s, g, 0, 0)), pl.BlockSpec((1, 1, 8, depth), lambda s, g: (s, g, 0, 0))],
        out_shape=[
            jax.ShapeDtypeStruct(mixed.shape, BF16),
            jax.ShapeDtypeStruct((seqs, HEADS, depth, depth), F32),
            jax.ShapeDtypeStruct((seqs, HEADS // PAIR, 8, depth), F32),
        ],
        cost_estimate=cost(6),
        name="mix_heads_back",
    )(mixed, reach, gain.reshape(1, depth), grad)
    return back, local, jnp.sum(total[:, :, 0], axis=(0, 1))


def pack_kernel(mixer_ref, ffn_ref, early_ref, late_ref, rest_ref, out_ref):
    at = 0
    for ref in (mixer_ref, ffn_ref, early_ref, late_ref, rest_ref):
        value = ref[...]
        if len(value.shape) == 3:
            value = jnp.sum(value, axis=0)
        out_ref[at : at + value.shape[0]] = value
        at += value.shape[0]


def packed(*pieces):
    rows = sum(piece.shape[-2] for piece in pieces)
    return pl.pallas_call(
        pack_kernel, out_shape=jax.ShapeDtypeStruct((rows, 128), F32), cost_estimate=cost(2), name="pack_sums"
    )(*pieces)


BOTH = ("dp", "cp")


class Grid:
    def __init__(self):
        self.cp = lax.axis_size("cp")
        group = lax.axis_size("dp")
        self.core = 2 if group % 2 == 0 else 1
        self.lo = 2 if group // self.core % 2 == 0 else 1
        self.hi = group // self.core // self.lo
        self.sizes = (self.hi, self.lo, self.core, self.cp)

    def place(self):
        member = lax.axis_index("dp")
        return (
            member // (self.lo * self.core),
            member // self.core % self.lo,
            member % self.core,
            lax.axis_index("cp"),
        )

    def swap(self, value, axis, by):
        step = [1] * 4
        for later in range(3):
            step[2 - later] = step[3 - later] * self.sizes[3 - later]
        pairs = []
        for device in range(step[0] * self.sizes[0]):
            here = device // step[axis] % self.sizes[axis]
            pairs.append((device, device + ((here ^ by) - here) * step[axis]))
        return lax.ppermute(value, BOTH, pairs)

    def others(self, value, axis):
        return [self.swap(value, axis, by) for by in range(1, self.sizes[axis])]


HI, LO, CORE, SEG = range(4)


def cut_of(columns):
    return columns // 256 * 128


def place_kernel(cuts, spot, own_left, own_right, other_left, other_right, *outs):
    core, seg = spot[2], spot[3]
    for away, left, right in ((0, own_left, own_right), (1, other_left, other_right)):
        if away >= outs[0].shape[2]:
            continue
        cut = left.shape[-1]
        for at in range(left.shape[2]):
            for out, (top, bottom, first, last) in zip(outs, cuts):
                for source, start in ((left, 0), (right, cut)):
                    low, high = max(first, start), min(last, start + source.shape[-1])
                    if low < high:
                        out[0, 0, core ^ away, at, :, low - first : high - first] = source[
                            0, 0, at ^ seg, top:bottom, low - start : high - start
                        ]


def tied(value, *needed):
    return lax.optimization_barrier((value, needed))[0] if needed else value


class Gather:
    def __init__(self, grid, shard):
        self.grid = grid
        self.shape = shard.shape
        self.cut = cut_of(shard.shape[1])
        self.mine = shard
        self.sent = [shard]
        self.got = grid.others(shard, SEG)

    def exchange(self, axes):
        self.got = [self.grid.others(piece, axis) for piece, axis in zip(self.sent, axes)]

    def first(self, *needed):
        parts = tied([self.mine] + self.got, *needed)
        self.sent = [
            jnp.stack([part[:, : self.cut] for part in parts]),
            jnp.stack([part[:, self.cut :] for part in parts]),
        ]
        self.exchange((LO, HI))

    def second(self, *needed):
        sent, got = tied((self.sent, self.got), *needed)
        self.sent = [jnp.stack([piece] + more) for piece, more in zip(sent, got)]
        self.exchange((HI, LO))

    def third(self, *needed):
        sent, got = tied((self.sent, self.got), *needed)
        self.own = [
            jnp.stack([piece] + more, axis=axis)
            for piece, more, axis in zip(sent, got, (0, 1))
        ]
        self.sent = self.own
        self.other = [
            self.grid.swap(piece, CORE, 1) if self.grid.core == 2 else piece for piece in self.own
        ]

    def placed(self, cuts, *needed):
        grid, (r, total), cut = self.grid, self.shape, self.cut
        own, other = tied((self.own, self.other), *needed)

        def source(wide):
            return pl.BlockSpec(
                (1, 1, grid.cp, r, wide), lambda a, b, spot: (a ^ spot[0], b ^ spot[1], 0, 0, 0)
            )

        shapes = [(bottom - top, right - left) for top, bottom, left, right in cuts]
        sources = [source(cut), source(total - cut)]
        outs = pl.pallas_call(
            functools.partial(place_kernel, cuts),
            grid_spec=pltpu.PrefetchScalarGridSpec(
                num_scalar_prefetch=1,
                grid=(grid.hi, grid.lo),
                in_specs=sources + sources,
                out_specs=[
                    pl.BlockSpec((1, 1, grid.core, grid.cp) + shape, lambda a, b, spot: (a, b, 0, 0, 0, 0))
                    for shape in shapes
                ],
            ),
            out_shape=[jax.ShapeDtypeStruct(grid.sizes + shape, BF16) for shape in shapes],
            cost_estimate=cost(14),
            name="place_rows",
        )(jnp.stack(grid.place()), *own, *other)
        return [out.reshape(-1, out.shape[-1]) for out in outs]


class Share:
    def __init__(self, grid, values=None, keep=None, send=None):
        self.grid = grid
        self.spots = grid.place()
        self.halved = values is None
        self.stacked = False
        if self.halved:
            self.spots = (0, 0, 0, self.spots[SEG])
        else:
            core = self.spots[2]
            values = [value.reshape(grid.sizes + (-1, value.shape[-1])) for value in values]

            keep = [pick(value, core, 2) for value in values]
            send = [pick(value, core ^ 1, 2) for value in values]
        self.sent = send
        self.terms = [
            [k, grid.swap(s, CORE, 1)] if grid.core == 2 else [k] for k, s in zip(keep, send)
        ]

    def begin(self, *moves):
        self.terms = []
        self.sent = []
        self.got = []
        for array, axis, dim in moves:
            here = self.spots[axis]
            mine = pick(array, here, dim)
            sent = [pick(array, here ^ by, dim) for by in range(1, self.grid.sizes[axis])]
            got = [self.grid.swap(term, axis, by + 1) for by, term in enumerate(sent)]
            self.sent += sent
            self.got += got
            self.terms.append([mine] + got)

    def summed(self, *needed):
        return [total_of(terms).astype(BF16) for terms in tied(self.terms, *needed)]

    def first(self, *needed):
        totals = self.summed(*needed)
        if self.halved:
            left, right = totals
            self.begin((left, LO, 0), (right, HI, 0))
        else:
            value = totals[0] if len(totals) == 1 else jnp.concatenate(totals, axis=-2)
            cut = cut_of(value.shape[-1])
            self.begin((value[..., :cut], LO, 1), (value[..., cut:], HI, 0))

    def second(self, *needed):
        left, right = self.summed(*needed)
        self.begin((left, HI, 0), (right, LO, 0))

    def ready(self, *needed, more=()):
        halved = self.summed(*needed)
        for put in more:
            halved = halved + put.summed(*needed)
        self.total = jnp.concatenate(halved, axis=-1)

    def third(self, *needed):
        self.begin((tied(self.total, *needed), SEG, 0))

    def third_at_once(self, *needed):
        self.terms = [[lax.all_to_all(tied(self.total, *needed), "cp", 0, 0)]]
        self.stacked = True

    def result(self, *needed):
        terms = tied(self.terms[0], *needed)
        if self.stacked:
            terms = [terms[0][i] for i in range(self.grid.cp)]
        return total_of(terms)


def total_of(terms):
    total = terms[0].astype(F32)
    for term in terms[1:]:
        total = total + term.astype(F32)
    return total


def pick(array, index, dim):
    if isinstance(index, int):
        return lax.index_in_dim(array, index, dim, keepdims=False)
    return lax.dynamic_index_in_dim(array, index, dim, keepdims=False)


def all_sum(grid, value, across, along):
    for axis in (CORE, LO, HI, SEG):
        by = 1
        while by < grid.sizes[axis]:
            if axis == SEG:
                value = tied(value, *(across if by == 1 else along))
            value = value + grid.swap(value, axis, by)
            by *= 2
    return value


def natural_rows(grid, spot, own, other):
    rows = []
    for a in range(grid.hi):
        for b in range(grid.lo):
            for k in range(grid.core):
                for c in range(grid.cp):
                    index = (a ^ spot[0], b ^ spot[1], c ^ spot[3])
                    mine, theirs = own[index], other[index]
                    rows.append(jnp.where(spot[2] == k, mine, theirs))
    return jnp.concatenate(rows, axis=0)


def scatter_rows(grid, spot, value, keep, send, flip):
    r = keep.shape[-2]
    for a in range(grid.hi):
        for b in range(grid.lo):
            for c in range(grid.cp):
                index = (a ^ spot[0], b ^ spot[1], c)
                if flip:
                    index = (index[1], index[0], index[2])
                at = ((a * grid.lo + b) * grid.core * grid.cp + c) * r
                lower = value[at : at + r]
                at += grid.cp * r
                upper = value[at : at + r]
                keep[index] = jnp.where(spot[2] == 0, lower, upper)
                send[index] = jnp.where(spot[2] == 0, upper, lower)


def feed_kernel(
    grid, spot, rows_ref, flipped_ref, cot_ref, og_ref, ou_ref, tg_ref, tu_ref, down_ref,
    out_ref, back_ref, grad_down_ref, kg_ref, sg_ref, ku_ref, su_ref,
):
    tile = down_ref.shape[0]

    @pl.when(pl.program_id(0) == 0)
    def _():
        out_ref[...] = jnp.zeros(out_ref.shape, F32)
        back_ref[...] = jnp.zeros(back_ref.shape, F32)

    cot, down = cot_ref[...], down_ref[...]
    both = jnp.concatenate(
        [natural_rows(grid, spot, og_ref, tg_ref), natural_rows(grid, spot, ou_ref, tu_ref)], axis=1
    )
    gates = mul(rows_ref[...], both, NN)
    grad_hidden = mul(cot, down, NT)
    gate, up = gates[:, :tile], gates[:, tile:]
    sigma = jax.nn.sigmoid(gate)
    act = gate * sigma
    hidden = (act * up).astype(BF16)
    grad_gate = grad_hidden * up * (sigma * (1.0 + gate * (1.0 - sigma)))
    grads = jnp.concatenate([grad_gate.astype(BF16), (grad_hidden * act).astype(BF16)], axis=1)
    out_ref[...] += mul(hidden, down, NN)
    back_ref[...] += mul(grads, both, NT)
    grad_down_ref[...] = mul(hidden, cot, TN).astype(BF16)
    share = mul(flipped_ref[...], grads, NN)
    scatter_rows(grid, spot, share[:, :tile].astype(BF16), kg_ref, sg_ref, True)
    scatter_rows(grid, spot, share[:, tile:].astype(BF16), ku_ref, su_ref, False)


def feed_forward(grid, rows, cot, gather, w_down):
    tokens, model = rows.shape
    half = w_down.shape[0]
    tile = 256
    r = gather.shape[0]
    lead = (grid.hi, grid.lo, grid.cp, r)
    whole = pl.BlockSpec((tokens, model), lambda j, spot: (0, 0))
    piece = pl.BlockSpec(lead + (tile,), lambda j, spot: (0, 0, 0, 0, j))
    down = pl.BlockSpec((tile, model), lambda j, spot: (j, 0))
    turned = (grid.lo, grid.hi, grid.cp, r)
    left = pl.BlockSpec(turned + (tile,), lambda j, spot: (0, 0, 0, 0, j))
    share = [jax.ShapeDtypeStruct(turned + (half,), BF16)] * 2 + [jax.ShapeDtypeStruct(lead + (half,), BF16)] * 2
    out, back, grad_down, kg, sg, ku, su = pl.pallas_call(
        functools.partial(feed_kernel, grid),
        grid_spec=pltpu.PrefetchScalarGridSpec(
            num_scalar_prefetch=1,
            grid=(half // tile,),
            in_specs=[whole, pl.BlockSpec((model, tokens), lambda j, spot: (0, 0)), whole] + [piece] * 4 + [down],
            out_specs=[whole, whole, down, left, left, piece, piece],
        ),
        out_shape=[
            jax.ShapeDtypeStruct((tokens, model), F32),
            jax.ShapeDtypeStruct((tokens, model), F32),
            jax.ShapeDtypeStruct((half, model), BF16),
            *share,
        ],
        compiler_params=pltpu.CompilerParams(vmem_limit_bytes=58 * 2**20),
        cost_estimate=cost(33),
        name="feed_forward",
    )(jnp.stack(grid.place()), rows, rows.T, cot, *gather.own, *gather.other, w_down)
    return out, back, grad_down, (kg, ku), (sg, su)


def passed_along(value, axis, by):
    peers = lax.axis_size(axis)
    pairs = [(i, i + by) for i in range(peers) if 0 <= i + by < peers]
    return lax.ppermute(value, axis, pairs)


def apply_map(transfer, state, offset):
    return jnp.einsum("shij,shjk->shik", transfer, state, precision=lax.Precision.HIGH) + offset


def rows_times(left, right):
    return jnp.einsum("sga,ab->sgb", left, right, preferred_element_type=F32)


def rows_back(grad, weight):
    return jnp.einsum("sgb,ab->sga", grad, weight, preferred_element_type=F32)


def weight_grad(left, right):
    return jnp.einsum("sga,sgb->ab", left, right, preferred_element_type=F32)


def norm_back(rows, scale, gain, grad):
    weighted = grad * gain
    gain_grad = jnp.sum(grad * rows * scale, axis=tuple(range(rows.ndim - 1)))
    width = rows.shape[-1]
    row_grad = scale * weighted - rows * scale**3 * (
        jnp.sum(weighted * rows, axis=-1, keepdims=True) / width
    )
    return (gain_grad, row_grad)


def per_device(
    block_input, mixer_gain, qkv_weight, conv_taps, beta_weight, out_gain,
    proj_weight, ffn_gain, gate_up, down_weight, cotangent,
):
    seqs, seg_len, model = block_input.shape
    width = conv_taps.shape[0]
    depth = model // HEADS
    peers = lax.axis_size(BOTH)
    share = model // peers
    tap_share = conv_taps.shape[1]
    hops = lax.axis_size("cp") - 1
    grid = Grid()

    even = -(-share // 16) * 16
    down_share = down_weight.shape[0]
    mats = jnp.concatenate([jnp.pad(proj_weight, ((0, even - share), (0, 0))), down_weight], axis=0)
    small = jnp.concatenate(
        [beta_weight, mixer_gain[:, None], ffn_gain[:, None], conv_taps.reshape(share, -1)], axis=1
    )
    small = jnp.pad(small, ((0, 0), (0, 128 - small.shape[1])))
    wide = PAIR * depth
    groups = HEADS // PAIR
    columns = [
        qkv_weight[:, part * model + base * wide : part * model + (base + 1) * wide]
        for base in range(groups)
        for part in range(3)
    ]
    get_qkv = Gather(grid, jnp.concatenate(columns + [small], axis=1))
    get_mats = Gather(grid, tied(mats, *get_qkv.got))
    get_qkv.first()
    get_qkv.second()
    get_gateup = Gather(grid, tied(gate_up, get_qkv.got))
    get_qkv.third(*get_mats.got)
    get_mats.first(*get_qkv.own)
    wide_qkv = 3 * model + 128
    w_qkv, small = get_qkv.placed(
        ((0, share, 0, wide_qkv), (0, share, 3 * model, wide_qkv)), *get_mats.sent
    )
    gain_one = small[:, HEADS]
    gain_two = small[:, HEADS + 1]
    taps = small[:, HEADS + 2 : HEADS + 2 + width * tap_share // share].reshape(peers, width, tap_share)
    taps = jnp.swapaxes(taps, 0, 1).reshape(width, peers * tap_share)

    gain_outf = out_gain.astype(F32)
    resid_in = block_input.astype(F32)
    scale_one = lax.rsqrt(jnp.mean(resid_in * resid_in, axis=-1, keepdims=True) + norm_eps)
    normed_one = (resid_in * scale_one * gain_one.astype(F32)).astype(BF16)
    projected = rows_times(normed_one, w_qkv).astype(BF16)
    tail = jnp.concatenate([projected[:, seg_len - 8 :, : 3 * model], normed_one[:, seg_len - 8 :]], axis=-1)
    before = passed_along(tail, "cp", 1)
    early = lax.broadcasted_iota(jnp.int32, before.shape, 1) < 8 - (width - 1)
    before = jnp.where(early, 0.0, before)
    normed_more = jnp.concatenate(
        [normed_one, jnp.zeros((seqs, 8, model), BF16), before[:, :, 3 * model :]], axis=1
    )
    before = before[:, :, : 3 * model]
    rates = jax.nn.sigmoid(rows_times(normed_one, small)[..., :HEADS])
    get_mats.second(tail)
    get_gateup.first(tail, *get_mats.sent)
    projected = tied(projected, *get_gateup.sent, *get_mats.sent)
    high, rest, updates, weights, reach, alone, transfer, offset = forward_parts(
        projected, before, taps, rates, depth
    )
    carried = jnp.zeros(offset.shape, BF16)
    for step in range(hops):
        sent = offset if step == 0 else apply_map(transfer, carried.astype(F32), offset)
        sent = sent.astype(BF16)
        carried = passed_along(sent, "cp", 1)
        if step == 0:
            get_gateup.second(sent)
            get_mats.third(sent, *get_gateup.sent)
            carried = tied(carried, *get_mats.sent, *get_gateup.sent)
        if step == 2:
            get_gateup.third(sent)
            w_proj, w_down = get_mats.placed(((0, share, 0, model), (even, even + down_share, 0, model)), sent)
            carried = tied(carried, w_down, w_proj)
    mixed, mixed_low = mix(alone, reach, carried, gain_outf)

    attn = rows_times(mixed_low, w_proj)
    middle = resid_in + attn
    scale_two = lax.rsqrt(jnp.mean(middle * middle, axis=-1, keepdims=True) + norm_eps)
    gain_twof = gain_two.astype(F32)
    normed_two = (middle * scale_two * gain_twof).astype(BF16)
    tokens = seqs * seg_len
    ffn_out, grad_normed_two, grad_down, keep, send = feed_forward(
        grid, normed_two.reshape(tokens, model), cotangent.reshape(tokens, model), get_gateup, w_down
    )
    ffn_out = ffn_out.reshape(middle.shape)
    put_gateup = Share(grid, keep=keep, send=send)
    result = middle + ffn_out
    squares = jnp.stack(
        [jnp.sum(result * result), jnp.sum(attn * attn), jnp.sum(ffn_out * ffn_out)]
    )
    upstream = cotangent.astype(F32)
    grad_normed_two = grad_normed_two.reshape(middle.shape)
    grad_ffn, grad_from_norm = norm_back(middle, scale_two, gain_twof, grad_normed_two)
    grad_middle = upstream + grad_from_norm
    grad_attn = grad_middle.astype(BF16)
    grad_proj = weight_grad(mixed_low, grad_attn).astype(BF16)
    grad_normed_mix = rows_back(tied(grad_attn, grad_proj), w_proj).astype(BF16)

    grad_mixed, local_part, grad_out = mix_back(mixed, reach, gain_outf, grad_normed_mix)
    flipped = jnp.swapaxes(transfer, -1, -2)
    incoming = jnp.zeros(local_part.shape, BF16)
    for step in range(hops):
        sent = local_part if step == 0 else apply_map(flipped, incoming.astype(F32), local_part)
        sent = sent.astype(BF16)
        incoming = passed_along(sent, "cp", -1)
        if step == 0:
            put_gateup.first(sent)
            incoming = tied(incoming, *put_gateup.sent)
        if step == 1:
            put_mats = Share(grid, tied([grad_proj, grad_down], sent))
            incoming = tied(incoming, *put_mats.sent)
        if step == 2:
            put_mats.first(sent)
            incoming = tied(incoming, *put_mats.sent)
    puts = []
    arrays = (projected, before, taps, rates, high, rest, updates, weights, carried, grad_mixed)

    for base in range(HEADS // PAIR):
        held = ()
        for seq in range(seqs):
            held = backward_parts(seq, base, held, *arrays, incoming, depth)
            if (base, seq) == (0, 0):
                put_gateup.second(held[0])
                incoming = tied(incoming, *put_gateup.sent)
            if (base, seq) == (0, seqs - 1):
                kept = held
                put_mats.second(held[0])
                puts.append(Share(grid, [weight_grad(normed_more, held[0]).astype(BF16)]))
                incoming = tied(incoming, *put_mats.sent, *puts[0].sent)
            if (base, seq) == (1, 0):
                put_gateup.ready(held[0])
                put_gateup.third_at_once()
                put_mats.ready(held[0])
                puts[0].first(held[0])
                incoming = tied(incoming, put_gateup.total, put_mats.total, *puts[0].sent)
    late = weight_grad(normed_more, held[0]).astype(BF16)
    puts.append(Share(grid, [late]))
    put_mats.third_at_once(held[0])
    puts[0].second(*puts[1].sent)
    kept, held = tied((kept, held), *puts[0].sent)
    last_rows = jnp.concatenate([kept[1], held[1]], axis=-1)
    returned = passed_along(jnp.concatenate([kept[2], held[2]], axis=-1), "cp", -1)
    logits = kept[0][:, :seg_len, 3 * wide :] + held[0][:, :seg_len, 3 * wide :]
    grad_projected = jnp.concatenate(
        [kept[0][:, :seg_len, : 3 * wide], held[0][:, :seg_len, : 3 * wide], logits], axis=-1
    )
    puts[1].first(grad_projected, put_gateup.terms[0][0], *puts[0].got)
    last_rows, returned = tied((last_rows, returned), *puts[1].sent)
    last_rows = last_rows + returned
    grad_projected = lax.dynamic_update_slice(grad_projected, last_rows.astype(BF16), (0, seg_len - 8, 0))
    grad_normed_one = rows_back(grad_projected, w_qkv)
    grad_mixer, grad_from_first = norm_back(resid_in, scale_one, gain_one.astype(F32), grad_normed_one)
    across = puts[1].got
    puts[1].second(put_mats.terms[0][0])
    along = puts[1].got
    grad_input = grad_middle + grad_from_first
    rest = jnp.pad(jnp.concatenate([squares, grad_out]), (0, 256 - 3 - depth)).reshape(2, 128)
    flat = packed(tied(grad_mixer, *across).reshape(-1, 128), grad_ffn.reshape(-1, 128), kept[3], held[3], rest)
    sums = all_sum(grid, flat, across, along)
    counts = [model // 128] * 2 + [6 * PAIR * width, 2]
    starts = [sum(counts[:i]) for i in range(4)]
    found = [sums[start : start + count].reshape(-1) for start, count in zip(starts, counts)]
    puts[1].ready(more=(puts[0],))
    puts[1].third()
    both = puts[1].result()
    held_columns = 3 * wide + 128
    second, first = both[:, :held_columns], both[:, held_columns:]
    share_beta = first[:, 3 * wide : 3 * wide + HEADS] + second[:, 3 * wide : 3 * wide + HEADS]
    parts = [part[:, : 3 * wide].reshape(share, 3, wide) for part in (first, second)]
    share_qkv = jnp.stack(parts, axis=2).reshape(share, 3 * model)
    grad_taps = found[2].reshape(HEADS // PAIR, 3, PAIR, width, depth)
    grad_taps = jnp.transpose(grad_taps, (3, 1, 0, 2, 4)).reshape(width, 3 * model)
    share_gateup = put_gateup.result(*puts[1].sent)
    share_mats = put_mats.result(*puts[1].sent)
    me = lax.axis_index(BOTH)

    def mine(array, count):
        return lax.dynamic_slice_in_dim(array, me * count, count, axis=-1)

    return (
        result.astype(BF16),
        grad_input,
        mine(found[0], share),
        share_qkv,
        mine(grad_taps, tap_share),
        share_beta,
        found[3][3 : 3 + depth],
        share_mats[:share],
        mine(found[1], share),
        share_gateup,
        share_mats[share:],
        jnp.sqrt(found[3][:3] / (result.size * peers)),
    )


def solution(mesh):
    both = P(BOTH)
    rows = P(BOTH, None)
    tokens = P("dp", "cp", None)
    taps = P(None, BOTH)
    in_specs = (tokens, both, rows, taps, rows, P(), rows, both, rows, rows, tokens)
    out_specs = (tokens, tokens, both, rows, taps, rows, P(), rows, both, rows, rows, P())
    return jax.shard_map(
        per_device, mesh=mesh, in_specs=in_specs, out_specs=out_specs, check_vma=False
    )
```

```python
import functools

import jax
import jax.numpy as jnp
from jax import lax
from jax.experimental import pallas as pl
from jax.experimental.pallas import tpu as pltpu
from jax.sharding import PartitionSpec as P

HEADS = 8
PAIR = 4

norm_eps = 1e-05
unit_eps = 1e-06
LEAD = 16
F32 = jnp.float32
BF16 = jnp.bfloat16


def halves(value):
    high = value.astype(BF16)
    return high, (value - high.astype(F32)).astype(BF16)


NN = (((1,), (0,)), ((), ()))
NT = (((1,), (1,)), ((), ()))
TN = (((0,), (0,)), ((), ()))


def mul(left, right, dims):
    return lax.dot_general(left, right, dims, preferred_element_type=F32)


def mul_halves(left, right, dims):
    total = mul(left[0], right[0], dims)
    if len(right) == 2:
        total = total + mul(left[0], right[1], dims)
    if len(left) == 2:
        total = total + mul(left[1], right[0], dims)
    return total


def side_by_side(array):
    half = array.shape[0] // 2
    return jnp.concatenate([array[:half, :half], array[half:, half:]], axis=1)


def on_diagonal(array):
    half = array.shape[0]
    zero = jnp.zeros((half, half), array.dtype)
    return jnp.concatenate(
        [
            jnp.concatenate([array[:, :half], zero], axis=1),
            jnp.concatenate([zero, array[:, half:]], axis=1),
        ],
        axis=0,
    )


def unit_lower_inverses(lowers):
    size = lowers[0].shape[0]
    half = size // 2
    row = lax.broadcasted_iota(jnp.int32, (half, size), 0)
    col = lax.broadcasted_iota(jnp.int32, (half, size), 1) & (half - 1)
    apart = row ^ col
    zero = jnp.zeros((half, size), BF16)
    packed = [side_by_side(lower) for lower in lowers]
    inverses = [
        jnp.where(row == col, 1.0, 0.0) - jnp.where(apart == 1, lower, zero).astype(F32)
        for lower in packed
    ]
    for level in range(1, half.bit_length() - 1):
        between = (apart >> level) == 1
        splits = [halves(inverse) for inverse in inverses]
        middles = [
            mul_halves((jnp.where(between, lower, zero),), [on_diagonal(piece) for piece in split], NN)
            for lower, split in zip(packed, splits)
        ]
        middles = [[on_diagonal(piece) for piece in halves(middle)] for middle in middles]
        inverses = [
            inverse - mul_halves(split, middle, NN)
            for inverse, split, middle in zip(inverses, splits, middles)
        ]
    splits = [halves(inverse) for inverse in inverses]
    tops = [[piece[:, :half] for piece in split] for split in splits]
    bottoms = [[piece[:, half:] for piece in split] for split in splits]
    middles = [mul_halves((lower[half:, :half],), top, NN) for lower, top in zip(lowers, tops)]
    corners = [
        halves(-mul_halves(bottom, halves(middle), NN)) for bottom, middle in zip(bottoms, middles)
    ]
    return zip(tops, corners, bottoms)


def shifted_down(rows, before, by):
    if by == 0:
        return rows
    rolled = pltpu.roll(rows, by, 0)
    top = pltpu.roll(before, by, 0)
    index = lax.broadcasted_iota(jnp.int32, before.shape, 0)
    first = jnp.where(index < by, top, rolled[: before.shape[0]])
    return jnp.concatenate([first, rolled[before.shape[0] :]], axis=0)


def shifted_up(rows, by):
    if by == 0:
        return rows
    count = rows.shape[0]
    index = lax.broadcasted_iota(jnp.int32, rows.shape, 0)
    return jnp.where(index < count - by, pltpu.roll(rows, count - by, 0), 0.0)


def conv_parts(rows, before, taps):
    width = taps.shape[0]
    conv = None
    for lag in range(width):
        term = taps[lag : lag + 1] * shifted_down(rows, before, width - 1 - lag)
        conv = term if conv is None else conv + term
    return conv


def unit_scale(active):
    return lax.rsqrt(jnp.sum(active * active, axis=-1, keepdims=True) + unit_eps)


def column_of(rates, head):
    index = lax.broadcasted_iota(jnp.int32, rates.shape, 1)
    return jnp.sum(jnp.where(index == head, rates, 0.0), axis=1, keepdims=True)


def forward_kernel(
    q_ref, k_ref, v_ref, qt_ref, kt_ref, vt_ref, rates_ref,
    high_ref, rest_ref, updates_ref, weights_ref, reach_ref, mixed_ref, transfer_ref, offset_ref,
):
    depth = transfer_ref.shape[-1]
    size = q_ref.shape[1] - LEAD
    half = size // 2
    first = pl.program_id(1) * PAIR
    row = lax.broadcasted_iota(jnp.int32, (size, size), 0)
    col = lax.broadcasted_iota(jnp.int32, (size, size), 1)
    strict = row > col
    lower = row >= col
    small_row = lax.broadcasted_iota(jnp.int32, (depth, depth), 0)
    small_col = lax.broadcasted_iota(jnp.int32, (depth, depth), 1)
    small_eye = jnp.where(small_row == small_col, 1.0, 0.0)
    systems, queries, keys, values, columns = [], [], [], [], []
    for h in range(PAIR):
        lanes = slice(h * depth, (h + 1) * depth)

        def active(ref, taps):
            rows = ref[0, :, lanes].astype(F32)
            conv = conv_parts(rows[LEAD:], rows[LEAD - 8 : LEAD], taps[:, lanes].astype(F32))
            return conv * jax.nn.sigmoid(conv)

        q = active(q_ref, qt_ref)
        k = active(k_ref, kt_ref)
        v = active(v_ref, vt_ref)
        q = (q * unit_scale(q) * depth ** (-0.5)).astype(BF16)
        k = (k * unit_scale(k)).astype(BF16)
        queries.append(q)
        keys.append(k)
        values.append(v.astype(BF16))
        columns.append(column_of(rates_ref[0, LEAD:], first + h))
        systems.append(jnp.where(strict, columns[h] * mul(k, k, NT), 0.0).astype(BF16))
    zero = jnp.zeros((half, half), BF16)
    for h, (top, corner, bottom) in enumerate(unit_lower_inverses(systems)):
        inverse = [
            jnp.concatenate(
                [jnp.concatenate([a, zero], axis=1), jnp.concatenate([b, c], axis=1)], axis=0
            )
            for a, b, c in zip(top, corner, bottom)
        ]
        high_ref[0, h] = inverse[0]
        rest_ref[0, h] = inverse[1]
        joined = jnp.concatenate([values[h], keys[h]], axis=1).astype(F32) * columns[h]
        solved = mul_halves(inverse, halves(joined), NN).astype(BF16)
        updates_ref[0, h] = solved[:, :depth]
        weights_ref[0, h] = solved[:, depth:]
        scores = jnp.where(lower, mul(queries[h], keys[h], NT), 0.0)
        seen = mul(scores.astype(BF16), solved, NN)
        lanes = slice(h * depth, (h + 1) * depth)
        mixed_ref[0, :, lanes] = seen[:, :depth]
        reach_ref[0, :, lanes] = (queries[h].astype(F32) - seen[:, depth:]).astype(BF16)
        moved = mul(keys[h], solved, TN)
        offset_ref[0, h] = moved[:, :depth]
        transfer_ref[0, h] = small_eye - moved[:, depth:]


def cost(microseconds):
    return pl.CostEstimate(flops=int(microseconds * 1.15e8), bytes_accessed=2**20, transcendentals=0)


def specs_of(model, depth, size, width, base=0, seq=None):
    wide = PAIR * depth
    blocks = model // wide

    def three(rows, batched):
        def index(part, s, g):
            if not batched:
                return (0, part * blocks + base + g)
            return (s if seq is None else seq, 0, (base + g) * 3 + part)

        block = (1, rows, wide) if batched else (rows, wide)
        return [pl.BlockSpec(block, functools.partial(index, part)) for part in range(3)]

    return three(LEAD + size, True) + three(width, False), wide


def forward_parts(projected, taps, rates, depth):
    seqs, size, _ = projected.shape
    size -= LEAD
    model = HEADS * depth
    token_specs, wide = specs_of(model, depth, size, taps.shape[0])
    rate_spec = pl.BlockSpec((1, LEAD + size, HEADS), lambda s, g: (s, 0, 0))

    def out(kind, *dims):
        return pl.BlockSpec((1, PAIR) + dims, lambda s, g: (s, g, 0, 0)), jax.ShapeDtypeStruct((seqs, HEADS) + dims, kind)

    def flat(kind):
        return pl.BlockSpec((1, size, wide), lambda s, g: (s, 0, g)), jax.ShapeDtypeStruct((seqs, size, model), kind)

    outs = [out(BF16, size, size), out(BF16, size, size), out(BF16, size, depth), out(BF16, size, depth)]
    outs += [flat(BF16), flat(F32), out(F32, depth, depth), out(F32, depth, depth)]
    return pl.pallas_call(
        forward_kernel,
        grid=(seqs, HEADS // PAIR),
        in_specs=token_specs + [rate_spec],
        out_specs=[o[0] for o in outs],
        out_shape=[o[1] for o in outs],
        compiler_params=pltpu.CompilerParams(vmem_limit_bytes=56 * 2**20),
        cost_estimate=cost(25),
        name="delta_forward",
    )(projected, projected, projected, taps, taps, taps, rates)


def backward_kernel(
    base, fresh, q_ref, k_ref, v_ref, qt_ref, kt_ref, vt_ref, rates_ref,
    high_ref, rest_ref, updates_ref, weights_ref, state_ref, grad_ref, leaving_ref, *refs
):
    rows_ref, last_ref, prior_ref, taps_ref = refs[0 if fresh else 4 :]
    depth = state_ref.shape[-1]
    size = q_ref.shape[1] - LEAD
    first = base * PAIR
    row = lax.broadcasted_iota(jnp.int32, (size, size), 0)
    col = lax.broadcasted_iota(jnp.int32, (size, size), 1)
    strict = row > col
    lower = row >= col
    index8 = lax.broadcasted_iota(jnp.int32, (8, depth), 0)
    lane = lax.broadcasted_iota(jnp.int32, (size, 128), 1)
    logits = jnp.zeros((size, 128), F32)
    for h in range(PAIR):
        lanes = slice(h * depth, (h + 1) * depth)

        def load(ref, taps):
            rows = ref[0, :, lanes].astype(F32)
            return rows[LEAD:], rows[LEAD - 8 : LEAD], taps[:, lanes].astype(F32)

        def active(parts):
            conv = conv_parts(*parts)
            gate = jax.nn.sigmoid(conv)
            return conv, gate, conv * gate

        raw = [load(q_ref, qt_ref), load(k_ref, kt_ref), load(v_ref, vt_ref)]
        acts = [active(parts) for parts in raw]
        q_scale = unit_scale(acts[0][2])
        k_scale = unit_scale(acts[1][2])
        q = (acts[0][2] * q_scale * depth ** (-0.5)).astype(BF16)
        k = (acts[1][2] * k_scale).astype(BF16)
        v = acts[2][2].astype(BF16)
        column = column_of(rates_ref[0, LEAD:], first + h)
        inverse = (high_ref[0, h], rest_ref[0, h])
        state = state_ref[0, h]
        grad = grad_ref[0, :, lanes]
        leaving = leaving_ref[0, h]
        gram = jnp.where(strict, mul(k, k, NT), 0.0).astype(BF16)
        scores = jnp.where(lower, mul(q, k, NT), 0.0).astype(BF16)
        errors = (updates_ref[0, h].astype(F32) - mul(weights_ref[0, h], state, NN)).astype(BF16)
        missed = v.astype(F32) - mul(k, state, NN) - mul(gram, errors, NN)
        grad_errors = mul(scores, grad, TN) + mul(k, leaving, NN)
        grad_right = mul_halves(inverse, halves(grad_errors), TN)
        low_right = grad_right.astype(BF16)
        grad_scores = jnp.where(lower, mul(grad, errors, NT), 0.0).astype(BF16)
        grad_system = (jnp.where(strict, -mul(low_right, errors, NT), 0.0) * column).astype(BF16)
        grad_v = grad_right * column
        grad_q = mul(grad, state, NT) + mul(grad_scores, k, NN)
        grad_k = (
            mul(grad_scores, q, TN)
            + mul(errors, leaving, NT)
            - mul(grad_v.astype(BF16), state, NT)
            + mul(grad_system, k, NN)
            + mul(grad_system, k, TN)
        )
        grad_rate = jnp.sum(grad_right * missed, axis=1, keepdims=True)
        grad_logit = grad_rate * column * (1.0 - column)
        logits = jnp.where(lane == first + h, grad_logit, logits)
        q_un, k_un = acts[0][2], acts[1][2]
        grad_q = (
            q_scale * grad_q
            - q_un * (q_scale * q_scale * q_scale * jnp.sum(grad_q * q_un, axis=1, keepdims=True))
        ) * depth ** (-0.5)
        grad_k = k_scale * grad_k - k_un * (
            k_scale * k_scale * k_scale * jnp.sum(grad_k * k_un, axis=1, keepdims=True)
        )
        for part, grad_act in enumerate((grad_q, grad_k, grad_v)):
            conv, gate, _ = acts[part]
            rows, before, taps = raw[part]
            width = taps.shape[0]
            grad_conv = grad_act * (gate * (1.0 + conv * (1.0 - gate)))
            total = None
            ahead = None
            spot = slice((part * PAIR + h) * depth, (part * PAIR + h + 1) * depth)
            for lag in range(width):
                by = width - 1 - lag
                tap = taps[lag : lag + 1]
                term = tap * shifted_up(grad_conv, by)
                total = term if total is None else total + term
                at = (part * PAIR + h) * width + lag
                taps_ref[0, at : at + 1] = jnp.sum(
                    grad_conv * shifted_down(rows, before, by), axis=0, keepdims=True
                )
                if by:
                    early = jnp.where(index8 >= 8 - by, tap * pltpu.roll(grad_conv[:8], 8 - by, 0), 0.0)
                    ahead = early if ahead is None else ahead + early
            rows_ref[0, LEAD:, spot] = total.astype(BF16)
            rows_ref[0, :LEAD, spot] = jnp.concatenate([jnp.zeros_like(ahead), ahead], axis=0).astype(BF16)
            last_ref[0, :, spot] = total[size - 8 :]
            prior_ref[0, :, spot] = ahead
    end = slice(3 * PAIR * depth, 3 * PAIR * depth + 128)
    rows_ref[0, LEAD:, end] = logits.astype(BF16)
    rows_ref[0, :LEAD, end] = jnp.zeros((LEAD, 128), BF16)


def backward_parts(seq, base, held, projected, taps, rates, high, rest, updates, weights, state, grad, leaving, depth):
    seqs, size, _ = projected.shape
    size -= LEAD
    model = HEADS * depth
    width = taps.shape[0]
    token_specs, wide = specs_of(model, depth, size, width, base, seq)
    rate_spec = pl.BlockSpec((1, LEAD + size, HEADS), lambda s, g: (seq, 0, 0))

    def heads(*dims):
        return pl.BlockSpec((1, PAIR) + dims, lambda s, g: (seq, base, 0, 0))

    def out(rows, kind, more=0):
        columns = 3 * wide + more
        return pl.BlockSpec((1, rows, columns), lambda s, g: (seq, 0, 0)), jax.ShapeDtypeStruct((seqs, rows, columns), kind)

    tap_rows = 3 * PAIR * width
    taps_out = pl.BlockSpec((1, tap_rows, depth), lambda s, g: (seq, 0, 0)), jax.ShapeDtypeStruct((seqs, tap_rows, depth), F32)
    outs = [out(LEAD + size, BF16, 128), out(8, F32), out(8, F32), taps_out]
    in_specs = token_specs + [rate_spec, heads(size, size), heads(size, size), heads(size, depth), heads(size, depth), heads(depth, depth), pl.BlockSpec((1, size, wide), lambda s, g: (seq, 0, base)), heads(depth, depth)]
    count = len(in_specs)
    return pl.pallas_call(
        functools.partial(backward_kernel, base, not held),
        grid=(1, 1),
        in_specs=in_specs + [pl.BlockSpec(memory_space=pl.ANY)] * len(held),
        out_specs=[o[0] for o in outs],
        out_shape=[o[1] for o in outs],
        input_output_aliases={count + i: i for i in range(len(held))},
        compiler_params=pltpu.CompilerParams(vmem_limit_bytes=56 * 2**20),
        cost_estimate=cost(10),
        name="delta_backward",
    )(projected, projected, projected, taps, taps, taps, rates, high, rest, updates, weights, state, grad, leaving, *held)


def mix_kernel(alone_ref, reach_ref, state_ref, gain_ref, mixed_ref, low_ref):
    depth = state_ref.shape[-1]
    for h in range(PAIR):
        lanes = slice(h * depth, (h + 1) * depth)
        mixed = alone_ref[0, :, lanes] + mul(reach_ref[0, :, lanes], state_ref[0, h], NN)
        scale = lax.rsqrt(jnp.mean(mixed * mixed, axis=-1, keepdims=True) + norm_eps)
        mixed_ref[0, :, lanes] = mixed
        low_ref[0, :, lanes] = (mixed * scale * gain_ref[...]).astype(BF16)


def mix(alone, reach, state, gain):
    seqs, size, model = alone.shape
    depth = state.shape[-1]
    wide = PAIR * depth
    flat = pl.BlockSpec((1, size, wide), lambda s, g: (s, 0, g))
    return pl.pallas_call(
        mix_kernel,
        grid=(seqs, HEADS // PAIR),
        in_specs=[flat, flat, pl.BlockSpec((1, PAIR, depth, depth), lambda s, g: (s, g, 0, 0)), pl.BlockSpec((1, depth), lambda s, g: (0, 0))],
        out_specs=[flat, flat],
        out_shape=[jax.ShapeDtypeStruct(alone.shape, F32), jax.ShapeDtypeStruct(alone.shape, BF16)],
        cost_estimate=cost(5),
        name="mix_heads",
    )(alone, reach, state, gain.reshape(1, depth))


def mix_back_kernel(mixed_ref, reach_ref, gain_ref, grad_ref, back_ref, local_ref, out_ref):
    depth = local_ref.shape[-1]
    total = None
    for h in range(PAIR):
        lanes = slice(h * depth, (h + 1) * depth)
        mixed = mixed_ref[0, :, lanes]
        grad = grad_ref[0, :, lanes].astype(F32)
        scale = lax.rsqrt(jnp.mean(mixed * mixed, axis=-1, keepdims=True) + norm_eps)
        weighted = grad * gain_ref[...]
        part = jnp.sum(grad * mixed * scale, axis=0, keepdims=True)
        total = part if total is None else total + part
        back = scale * weighted - mixed * (scale * scale * scale) * (
            jnp.mean(weighted * mixed, axis=-1, keepdims=True)
        )
        back = back.astype(BF16)
        back_ref[0, :, lanes] = back
        local_ref[0, h] = mul(reach_ref[0, :, lanes], back, TN)
    out_ref[0, 0] = jnp.broadcast_to(total, out_ref.shape[2:])


def mix_back(mixed, reach, gain, grad):
    seqs, size, model = mixed.shape
    depth = gain.size
    wide = PAIR * depth
    flat = pl.BlockSpec((1, size, wide), lambda s, g: (s, 0, g))
    back, local, total = pl.pallas_call(
        mix_back_kernel,
        grid=(seqs, HEADS // PAIR),
        in_specs=[flat, flat, pl.BlockSpec((1, depth), lambda s, g: (0, 0)), flat],
        out_specs=[flat, pl.BlockSpec((1, PAIR, depth, depth), lambda s, g: (s, g, 0, 0)), pl.BlockSpec((1, 1, 8, depth), lambda s, g: (s, g, 0, 0))],
        out_shape=[
            jax.ShapeDtypeStruct(mixed.shape, BF16),
            jax.ShapeDtypeStruct((seqs, HEADS, depth, depth), F32),
            jax.ShapeDtypeStruct((seqs, HEADS // PAIR, 8, depth), F32),
        ],
        cost_estimate=cost(6),
        name="mix_heads_back",
    )(mixed, reach, gain.reshape(1, depth), grad)
    return back, local, jnp.sum(total[:, :, 0], axis=(0, 1))


def pack_kernel(mixer_ref, ffn_ref, early_ref, late_ref, rest_ref, out_ref):
    at = 0
    for ref in (mixer_ref, ffn_ref, early_ref, late_ref, rest_ref):
        value = ref[...]
        if len(value.shape) == 3:
            value = jnp.sum(value, axis=0)
        out_ref[at : at + value.shape[0]] = value
        at += value.shape[0]


def packed(*pieces):
    rows = sum(piece.shape[-2] for piece in pieces)
    return pl.pallas_call(
        pack_kernel, out_shape=jax.ShapeDtypeStruct((rows, 128), F32), cost_estimate=cost(2), name="pack_sums"
    )(*pieces)


BOTH = ("dp", "cp")


class Grid:
    def __init__(self):
        self.cp = lax.axis_size("cp")
        group = lax.axis_size("dp")
        self.core = 2 if group % 2 == 0 else 1
        self.lo = 2 if group // self.core % 2 == 0 else 1
        self.hi = group // self.core // self.lo
        self.sizes = (self.hi, self.lo, self.core, self.cp)

    def place(self):
        member = lax.axis_index("dp")
        return (
            member // (self.lo * self.core),
            member // self.core % self.lo,
            member % self.core,
            lax.axis_index("cp"),
        )

    def swap(self, value, axis, by):
        step = [1] * 4
        for later in range(3):
            step[2 - later] = step[3 - later] * self.sizes[3 - later]
        pairs = []
        for device in range(step[0] * self.sizes[0]):
            here = device // step[axis] % self.sizes[axis]
            pairs.append((device, device + ((here ^ by) - here) * step[axis]))
        return lax.ppermute(value, BOTH, pairs)

    def others(self, value, axis):
        return [self.swap(value, axis, by) for by in range(1, self.sizes[axis])]


HI, LO, CORE, SEG = range(4)


def cut_of(columns):
    return columns // 256 * 128


def place_kernel(cuts, spot, own_left, own_right, other_left, other_right, *outs):
    core, seg = spot[2], spot[3]
    for away, left, right in ((0, own_left, own_right), (1, other_left, other_right)):
        if away >= outs[0].shape[2]:
            continue
        cut = left.shape[-1]
        for at in range(left.shape[2]):
            for out, (top, bottom, first, last) in zip(outs, cuts):
                for source, start in ((left, 0), (right, cut)):
                    low, high = max(first, start), min(last, start + source.shape[-1])
                    if low < high:
                        out[0, 0, core ^ away, at, :, low - first : high - first] = source[
                            0, 0, at ^ seg, top:bottom, low - start : high - start
                        ]


def tied(value, *needed):
    return lax.optimization_barrier((value, needed))[0] if needed else value


class Gather:
    def __init__(self, grid, shard, at_once=False):
        self.grid = grid
        self.shape = shard.shape
        self.cut = cut_of(shard.shape[1])
        self.mine = shard
        self.sent = [shard]
        self.at_once = at_once
        if at_once:
            all_of = lax.all_to_all(jnp.stack([shard] * grid.cp), "cp", 0, 0)
            self.got = [all_of]
        else:
            self.got = grid.others(shard, SEG)

    def exchange(self, axes):
        self.got = [self.grid.others(piece, axis) for piece, axis in zip(self.sent, axes)]

    def first(self, *needed):
        parts = tied([self.mine] + self.got, *needed)
        if self.at_once:
            here = self.grid.place()[SEG]
            parts = [pick(parts[1], here ^ by, 0) for by in range(self.grid.cp)]
        self.sent = [
            jnp.stack([part[:, : self.cut] for part in parts]),
            jnp.stack([part[:, self.cut :] for part in parts]),
        ]
        self.exchange((LO, HI))

    def second(self, *needed):
        sent, got = tied((self.sent, self.got), *needed)
        self.sent = [jnp.stack([piece] + more) for piece, more in zip(sent, got)]
        self.exchange((HI, LO))

    def third(self, *needed):
        sent, got = tied((self.sent, self.got), *needed)
        self.own = [
            jnp.stack([piece] + more, axis=axis)
            for piece, more, axis in zip(sent, got, (0, 1))
        ]
        self.sent = self.own
        self.other = [
            self.grid.swap(piece, CORE, 1) if self.grid.core == 2 else piece for piece in self.own
        ]

    def placed(self, cuts, *needed):
        grid, (r, total), cut = self.grid, self.shape, self.cut
        own, other = tied((self.own, self.other), *needed)

        def source(wide):
            return pl.BlockSpec(
                (1, 1, grid.cp, r, wide), lambda a, b, spot: (a ^ spot[0], b ^ spot[1], 0, 0, 0)
            )

        shapes = [(bottom - top, right - left) for top, bottom, left, right in cuts]
        sources = [source(cut), source(total - cut)]
        outs = pl.pallas_call(
            functools.partial(place_kernel, cuts),
            grid_spec=pltpu.PrefetchScalarGridSpec(
                num_scalar_prefetch=1,
                grid=(grid.hi, grid.lo),
                in_specs=sources + sources,
                out_specs=[
                    pl.BlockSpec((1, 1, grid.core, grid.cp) + shape, lambda a, b, spot: (a, b, 0, 0, 0, 0))
                    for shape in shapes
                ],
            ),
            out_shape=[jax.ShapeDtypeStruct(grid.sizes + shape, BF16) for shape in shapes],
            cost_estimate=cost(14),
            name="place_rows",
        )(jnp.stack(grid.place()), *own, *other)
        return [out.reshape(-1, out.shape[-1]) for out in outs]


class Share:
    def __init__(self, grid, values=None, keep=None, send=None):
        self.grid = grid
        self.spots = grid.place()
        self.halved = values is None
        self.stacked = False
        if self.halved:
            self.spots = (0, 0, 0, self.spots[SEG])
        else:
            core = self.spots[2]
            values = [value.reshape(grid.sizes + (-1, value.shape[-1])) for value in values]

            keep = [pick(value, core, 2) for value in values]
            send = [pick(value, core ^ 1, 2) for value in values]
        self.sent = send
        self.terms = [
            [k, grid.swap(s, CORE, 1)] if grid.core == 2 else [k] for k, s in zip(keep, send)
        ]

    def begin(self, *moves):
        self.terms = []
        self.sent = []
        self.got = []
        for array, axis, dim in moves:
            here = self.spots[axis]
            mine = pick(array, here, dim)
            sent = [pick(array, here ^ by, dim) for by in range(1, self.grid.sizes[axis])]
            got = [self.grid.swap(term, axis, by + 1) for by, term in enumerate(sent)]
            self.sent += sent
            self.got += got
            self.terms.append([mine] + got)

    def summed(self, *needed):
        return [total_of(terms).astype(BF16) for terms in tied(self.terms, *needed)]

    def first(self, *needed):
        totals = self.summed(*needed)
        if self.halved:
            left, right = totals
            self.begin((left, LO, 0), (right, HI, 0))
        else:
            value = totals[0] if len(totals) == 1 else jnp.concatenate(totals, axis=-2)
            cut = cut_of(value.shape[-1])
            self.begin((value[..., :cut], LO, 1), (value[..., cut:], HI, 0))

    def second(self, *needed):
        left, right = self.summed(*needed)
        self.begin((left, HI, 0), (right, LO, 0))

    def ready(self, *needed, more=()):
        halved = self.summed(*needed)
        for put in more:
            halved = halved + put.summed(*needed)
        self.total = jnp.concatenate(halved, axis=-1)

    def third(self, *needed):
        self.begin((tied(self.total, *needed), SEG, 0))

    def third_at_once(self, *needed):
        self.terms = [[lax.all_to_all(tied(self.total, *needed), "cp", 0, 0)]]
        self.stacked = True

    def result(self, *needed):
        terms = tied(self.terms[0], *needed)
        if self.stacked:
            terms = [terms[0][i] for i in range(self.grid.cp)]
        return total_of(terms)


def total_of(terms):
    total = terms[0].astype(F32)
    for term in terms[1:]:
        total = total + term.astype(F32)
    return total


def pick(array, index, dim):
    if isinstance(index, int):
        return lax.index_in_dim(array, index, dim, keepdims=False)
    return lax.dynamic_index_in_dim(array, index, dim, keepdims=False)


def all_sum(grid, value, across, along):
    for axis in (CORE, LO, HI, SEG):
        by = 1
        while by < grid.sizes[axis]:
            if axis == SEG:
                value = tied(value, *(across if by == 1 else along))
            value = value + grid.swap(value, axis, by)
            by *= 2
    return value


def natural_rows(grid, spot, own, other):
    rows = []
    for a in range(grid.hi):
        for b in range(grid.lo):
            for k in range(grid.core):
                for c in range(grid.cp):
                    index = (a ^ spot[0], b ^ spot[1], c ^ spot[3])
                    mine, theirs = own[index], other[index]
                    rows.append(jnp.where(spot[2] == k, mine, theirs))
    return jnp.concatenate(rows, axis=0)


def scatter_rows(grid, spot, value, keep, send, flip):
    r = keep.shape[-2]
    for a in range(grid.hi):
        for b in range(grid.lo):
            for c in range(grid.cp):
                index = (a ^ spot[0], b ^ spot[1], c)
                if flip:
                    index = (index[1], index[0], index[2])
                at = ((a * grid.lo + b) * grid.core * grid.cp + c) * r
                lower = value[at : at + r]
                at += grid.cp * r
                upper = value[at : at + r]
                keep[index] = jnp.where(spot[2] == 0, lower, upper)
                send[index] = jnp.where(spot[2] == 0, upper, lower)


def feed_kernel(
    grid, spot, rows_ref, flipped_ref, cot_ref, og_ref, ou_ref, tg_ref, tu_ref, down_ref,
    out_ref, back_ref, grad_down_ref, kg_ref, sg_ref, ku_ref, su_ref,
):
    tile = down_ref.shape[0]

    @pl.when(pl.program_id(0) == 0)
    def _():
        out_ref[...] = jnp.zeros(out_ref.shape, F32)
        back_ref[...] = jnp.zeros(back_ref.shape, F32)

    cot, down = cot_ref[...], down_ref[...]
    both = jnp.concatenate(
        [natural_rows(grid, spot, og_ref, tg_ref), natural_rows(grid, spot, ou_ref, tu_ref)], axis=1
    )
    gates = mul(rows_ref[...], both, NN)
    grad_hidden = mul(cot, down, NT)
    gate, up = gates[:, :tile], gates[:, tile:]
    sigma = jax.nn.sigmoid(gate)
    act = gate * sigma
    hidden = (act * up).astype(BF16)
    grad_gate = grad_hidden * up * (sigma * (1.0 + gate * (1.0 - sigma)))
    grads = jnp.concatenate([grad_gate.astype(BF16), (grad_hidden * act).astype(BF16)], axis=1)
    out_ref[...] += mul(hidden, down, NN)
    back_ref[...] += mul(grads, both, NT)
    grad_down_ref[...] = mul(hidden, cot, TN).astype(BF16)
    share = mul(flipped_ref[...], grads, NN)
    scatter_rows(grid, spot, share[:, :tile].astype(BF16), kg_ref, sg_ref, True)
    scatter_rows(grid, spot, share[:, tile:].astype(BF16), ku_ref, su_ref, False)


def feed_forward(grid, rows, cot, gather, w_down):
    tokens, model = rows.shape
    half = w_down.shape[0]
    tile = 256
    r = gather.shape[0]
    lead = (grid.hi, grid.lo, grid.cp, r)
    whole = pl.BlockSpec((tokens, model), lambda j, spot: (0, 0))
    piece = pl.BlockSpec(lead + (tile,), lambda j, spot: (0, 0, 0, 0, j))
    down = pl.BlockSpec((tile, model), lambda j, spot: (j, 0))
    turned = (grid.lo, grid.hi, grid.cp, r)
    left = pl.BlockSpec(turned + (tile,), lambda j, spot: (0, 0, 0, 0, j))
    share = [jax.ShapeDtypeStruct(turned + (half,), BF16)] * 2 + [jax.ShapeDtypeStruct(lead + (half,), BF16)] * 2
    out, back, grad_down, kg, sg, ku, su = pl.pallas_call(
        functools.partial(feed_kernel, grid),
        grid_spec=pltpu.PrefetchScalarGridSpec(
            num_scalar_prefetch=1,
            grid=(half // tile,),
            in_specs=[whole, pl.BlockSpec((model, tokens), lambda j, spot: (0, 0)), whole] + [piece] * 4 + [down],
            out_specs=[whole, whole, down, left, left, piece, piece],
        ),
        out_shape=[
            jax.ShapeDtypeStruct((tokens, model), F32),
            jax.ShapeDtypeStruct((tokens, model), F32),
            jax.ShapeDtypeStruct((half, model), BF16),
            *share,
        ],
        compiler_params=pltpu.CompilerParams(vmem_limit_bytes=58 * 2**20),
        cost_estimate=cost(33),
        name="feed_forward",
    )(jnp.stack(grid.place()), rows, rows.T, cot, *gather.own, *gather.other, w_down)
    return out, back, grad_down, (kg, ku), (sg, su)


def passed_along(value, axis, by):
    peers = lax.axis_size(axis)
    pairs = [(i, i + by) for i in range(peers) if 0 <= i + by < peers]
    return lax.ppermute(value, axis, pairs)


def apply_map(transfer, state, offset):
    return jnp.einsum("shij,shjk->shik", transfer, state, precision=lax.Precision.HIGH) + offset


def rows_times(left, right):
    return jnp.einsum("sga,ab->sgb", left, right, preferred_element_type=F32)


def rows_back(grad, weight):
    return jnp.einsum("sgb,ab->sga", grad, weight, preferred_element_type=F32)


def weight_grad(left, right):
    return jnp.einsum("sga,sgb->ab", left, right, preferred_element_type=F32)


def norm_back(rows, scale, gain, grad):
    weighted = grad * gain
    gain_grad = jnp.sum(grad * rows * scale, axis=tuple(range(rows.ndim - 1)))
    width = rows.shape[-1]
    row_grad = scale * weighted - rows * scale**3 * (
        jnp.sum(weighted * rows, axis=-1, keepdims=True) / width
    )
    return (gain_grad, row_grad)


def per_device(
    block_input, mixer_gain, qkv_weight, conv_taps, beta_weight, out_gain,
    proj_weight, ffn_gain, gate_up, down_weight, cotangent,
):
    seqs, seg_len, model = block_input.shape
    width = conv_taps.shape[0]
    depth = model // HEADS
    peers = lax.axis_size(BOTH)
    share = model // peers
    tap_share = conv_taps.shape[1]
    hops = lax.axis_size("cp") - 1
    grid = Grid()

    ahead = passed_along(block_input[:, seg_len - LEAD :], "cp", 1)
    even = -(-share // 16) * 16
    down_share = down_weight.shape[0]
    mats = jnp.concatenate([jnp.pad(proj_weight, ((0, even - share), (0, 0))), down_weight], axis=0)
    small = jnp.concatenate(
        [beta_weight, mixer_gain[:, None], ffn_gain[:, None], conv_taps.reshape(share, -1)], axis=1
    )
    small = jnp.pad(small, ((0, 0), (0, 128 - small.shape[1])))
    wide = PAIR * depth
    groups = HEADS // PAIR
    columns = [
        qkv_weight[:, part * model + base * wide : part * model + (base + 1) * wide]
        for base in range(groups)
        for part in range(3)
    ]
    get_qkv = Gather(grid, jnp.concatenate(columns + [small], axis=1))
    get_gateup = Gather(grid, tied(gate_up, *get_qkv.got), True)
    get_qkv.first(ahead)
    get_qkv.second()
    get_mats = Gather(grid, tied(mats, get_qkv.got))
    get_qkv.third()
    get_gateup.first(*get_qkv.own)
    wide_qkv = 3 * model + 128
    w_qkv, small = get_qkv.placed(
        ((0, share, 0, wide_qkv), (0, share, 3 * model, wide_qkv)), *get_gateup.sent
    )
    gain_one = small[:, HEADS]
    gain_two = small[:, HEADS + 1]
    taps = small[:, HEADS + 2 : HEADS + 2 + width * tap_share // share].reshape(peers, width, tap_share)
    taps = jnp.swapaxes(taps, 0, 1).reshape(width, peers * tap_share)

    gain_outf = out_gain.astype(F32)
    resid_in = block_input.astype(F32)
    scale_one = lax.rsqrt(jnp.mean(resid_in * resid_in, axis=-1, keepdims=True) + norm_eps)
    extended = jnp.concatenate([ahead, block_input], axis=1).astype(F32)
    scale = lax.rsqrt(jnp.mean(extended * extended, axis=-1, keepdims=True) + norm_eps)
    normed_one = (extended * scale * gain_one.astype(F32)).astype(BF16)
    projected = rows_times(normed_one, w_qkv).astype(BF16)
    rates = jax.nn.sigmoid(rows_times(normed_one, small)[..., :HEADS])
    get_gateup.second(projected)
    get_mats.first(projected, *get_gateup.sent)
    projected = tied(projected, *get_gateup.sent, *get_mats.sent)
    high, rest, updates, weights, reach, alone, transfer, offset = forward_parts(
        projected, taps, rates, depth
    )
    carried = jnp.zeros(offset.shape, BF16)
    for step in range(hops):
        sent = offset if step == 0 else apply_map(transfer, carried.astype(F32), offset)
        sent = sent.astype(BF16)
        carried = passed_along(sent, "cp", 1)
        if step == 0:
            get_mats.second(sent)
            get_gateup.third(sent, *get_mats.sent)
            carried = tied(carried, *get_mats.sent, *get_gateup.sent)
        if step == 2:
            get_mats.third(sent)
            w_proj, w_down = get_mats.placed(((0, share, 0, model), (even, even + down_share, 0, model)), sent)
            carried = tied(carried, w_down, w_proj)
    mixed, mixed_low = mix(alone, reach, carried, gain_outf)

    attn = rows_times(mixed_low, w_proj)
    middle = resid_in + attn
    scale_two = lax.rsqrt(jnp.mean(middle * middle, axis=-1, keepdims=True) + norm_eps)
    gain_twof = gain_two.astype(F32)
    normed_two = (middle * scale_two * gain_twof).astype(BF16)
    tokens = seqs * seg_len
    ffn_out, grad_normed_two, grad_down, keep, send = feed_forward(
        grid, normed_two.reshape(tokens, model), cotangent.reshape(tokens, model), get_gateup, w_down
    )
    ffn_out = ffn_out.reshape(middle.shape)
    put_gateup = Share(grid, keep=keep, send=send)
    result = middle + ffn_out
    squares = jnp.stack(
        [jnp.sum(result * result), jnp.sum(attn * attn), jnp.sum(ffn_out * ffn_out)]
    )
    upstream = cotangent.astype(F32)
    grad_normed_two = grad_normed_two.reshape(middle.shape)
    grad_ffn, grad_from_norm = norm_back(middle, scale_two, gain_twof, grad_normed_two)
    grad_middle = upstream + grad_from_norm
    grad_attn = grad_middle.astype(BF16)
    grad_proj = weight_grad(mixed_low, grad_attn).astype(BF16)
    grad_normed_mix = rows_back(tied(grad_attn, grad_proj), w_proj).astype(BF16)

    grad_mixed, local_part, grad_out = mix_back(mixed, reach, gain_outf, grad_normed_mix)
    flipped = jnp.swapaxes(transfer, -1, -2)
    incoming = jnp.zeros(local_part.shape, BF16)
    for step in range(hops):
        sent = local_part if step == 0 else apply_map(flipped, incoming.astype(F32), local_part)
        sent = sent.astype(BF16)
        incoming = passed_along(sent, "cp", -1)
        if step == 0:
            put_gateup.first(sent)
            incoming = tied(incoming, *put_gateup.sent)
        if step == 1:
            put_mats = Share(grid, tied([grad_proj, grad_down], sent))
            incoming = tied(incoming, *put_mats.sent)
        if step == 2:
            put_mats.first(sent)
            incoming = tied(incoming, *put_mats.sent)
    puts = []
    arrays = (projected, taps, rates, high, rest, updates, weights, carried, grad_mixed)

    for base in range(HEADS // PAIR):
        held = ()
        for seq in range(seqs):
            held = backward_parts(seq, base, held, *arrays, incoming, depth)
            if (base, seq) == (0, 0):
                put_gateup.second(held[0])
                incoming = tied(incoming, *put_gateup.sent)
            if (base, seq) == (0, seqs - 1):
                kept = held
                put_mats.second(held[0])
                puts.append(Share(grid, [weight_grad(normed_one, held[0]).astype(BF16)]))
                incoming = tied(incoming, *put_mats.sent, *puts[0].sent)
            if (base, seq) == (1, 0):
                put_gateup.ready(held[0])
                put_gateup.third_at_once()
                put_mats.ready(held[0])
                puts[0].first(held[0])
                incoming = tied(incoming, put_gateup.total, put_mats.total, *puts[0].sent)
    late = weight_grad(normed_one, held[0]).astype(BF16)
    puts.append(Share(grid, [late]))
    put_mats.third_at_once(held[0])
    puts[0].second(*puts[1].sent)
    kept, held = tied((kept, held), *puts[0].sent)
    last_rows = jnp.concatenate([kept[1], held[1]], axis=-1)
    returned = passed_along(jnp.concatenate([kept[2], held[2]], axis=-1), "cp", -1)
    logits = kept[0][:, LEAD:, 3 * wide :] + held[0][:, LEAD:, 3 * wide :]
    grad_projected = jnp.concatenate(
        [kept[0][:, LEAD:, : 3 * wide], held[0][:, LEAD:, : 3 * wide], logits], axis=-1
    )
    puts[1].first(grad_projected, put_gateup.terms[0][0], *puts[0].got)
    last_rows, returned = tied((last_rows, returned), *puts[1].sent)
    last_rows = last_rows + returned
    grad_projected = lax.dynamic_update_slice(grad_projected, last_rows.astype(BF16), (0, seg_len - 8, 0))
    grad_normed_one = rows_back(grad_projected, w_qkv)
    grad_mixer, grad_from_first = norm_back(resid_in, scale_one, gain_one.astype(F32), grad_normed_one)
    across = puts[1].got
    puts[1].second()
    along = puts[1].got
    grad_input = grad_middle + grad_from_first
    rest = jnp.pad(jnp.concatenate([squares, grad_out]), (0, 256 - 3 - depth)).reshape(2, 128)
    flat = packed(tied(grad_mixer, *across).reshape(-1, 128), grad_ffn.reshape(-1, 128), kept[3], held[3], rest)
    sums = all_sum(grid, flat, across + [put_mats.terms[0][0]], along)
    counts = [model // 128] * 2 + [6 * PAIR * width, 2]
    starts = [sum(counts[:i]) for i in range(4)]
    found = [sums[start : start + count].reshape(-1) for start, count in zip(starts, counts)]
    puts[1].ready(more=(puts[0],))
    puts[1].third()
    both = puts[1].result()
    held_columns = 3 * wide + 128
    second, first = both[:, :held_columns], both[:, held_columns:]
    share_beta = first[:, 3 * wide : 3 * wide + HEADS] + second[:, 3 * wide : 3 * wide + HEADS]
    parts = [part[:, : 3 * wide].reshape(share, 3, wide) for part in (first, second)]
    share_qkv = jnp.stack(parts, axis=2).reshape(share, 3 * model)
    grad_taps = found[2].reshape(HEADS // PAIR, 3, PAIR, width, depth)
    grad_taps = jnp.transpose(grad_taps, (3, 1, 0, 2, 4)).reshape(width, 3 * model)
    share_gateup = put_gateup.result(*puts[1].sent)
    share_mats = put_mats.result(*puts[1].sent)
    me = lax.axis_index(BOTH)

    def mine(array, count):
        return lax.dynamic_slice_in_dim(array, me * count, count, axis=-1)

    return (
        result.astype(BF16),
        grad_input,
        mine(found[0], share),
        share_qkv,
        mine(grad_taps, tap_share),
        share_beta,
        found[3][3 : 3 + depth],
        share_mats[:share],
        mine(found[1], share),
        share_gateup,
        share_mats[share:],
        jnp.sqrt(found[3][:3] / (result.size * peers)),
    )


def solution(mesh):
    both = P(BOTH)
    rows = P(BOTH, None)
    tokens = P("dp", "cp", None)
    taps = P(None, BOTH)
    in_specs = (tokens, both, rows, taps, rows, P(), rows, both, rows, rows, tokens)
    out_specs = (tokens, tokens, both, rows, taps, rows, P(), rows, both, rows, rows, P())
    return jax.shard_map(
        per_device, mesh=mesh, in_specs=in_specs, out_specs=out_specs, check_vma=False
    )
```

```python
import functools

import jax
import jax.numpy as jnp
from jax import lax
from jax.experimental import pallas as pl
from jax.experimental.pallas import tpu as pltpu
from jax.sharding import PartitionSpec as P

HEADS = 8
PAIR = 4

norm_eps = 1e-05
unit_eps = 1e-06
LEAD = 16
F32 = jnp.float32
BF16 = jnp.bfloat16


def halves(value):
    high = value.astype(BF16)
    return high, (value - high.astype(F32)).astype(BF16)


NN = (((1,), (0,)), ((), ()))
NT = (((1,), (1,)), ((), ()))
TN = (((0,), (0,)), ((), ()))


def mul(left, right, dims):
    return lax.dot_general(left, right, dims, preferred_element_type=F32)


def mul_halves(left, right, dims):
    total = mul(left[0], right[0], dims)
    if len(right) == 2:
        total = total + mul(left[0], right[1], dims)
    if len(left) == 2:
        total = total + mul(left[1], right[0], dims)
    return total


def side_by_side(array):
    half = array.shape[0] // 2
    return jnp.concatenate([array[:half, :half], array[half:, half:]], axis=1)


def on_diagonal(array):
    half = array.shape[0]
    zero = jnp.zeros((half, half), array.dtype)
    return jnp.concatenate(
        [
            jnp.concatenate([array[:, :half], zero], axis=1),
            jnp.concatenate([zero, array[:, half:]], axis=1),
        ],
        axis=0,
    )


def unit_lower_inverses(lowers):
    size = lowers[0].shape[0]
    half = size // 2
    row = lax.broadcasted_iota(jnp.int32, (half, size), 0)
    col = lax.broadcasted_iota(jnp.int32, (half, size), 1) & (half - 1)
    apart = row ^ col
    zero = jnp.zeros((half, size), BF16)
    packed = [side_by_side(lower) for lower in lowers]
    inverses = [
        jnp.where(row == col, 1.0, 0.0) - jnp.where(apart == 1, lower, zero).astype(F32)
        for lower in packed
    ]
    for level in range(1, half.bit_length() - 1):
        between = (apart >> level) == 1
        splits = [halves(inverse) for inverse in inverses]
        middles = [
            mul_halves((jnp.where(between, lower, zero),), [on_diagonal(piece) for piece in split], NN)
            for lower, split in zip(packed, splits)
        ]
        middles = [[on_diagonal(piece) for piece in halves(middle)] for middle in middles]
        inverses = [
            inverse - mul_halves(split, middle, NN)
            for inverse, split, middle in zip(inverses, splits, middles)
        ]
    splits = [halves(inverse) for inverse in inverses]
    tops = [[piece[:, :half] for piece in split] for split in splits]
    bottoms = [[piece[:, half:] for piece in split] for split in splits]
    middles = [mul_halves((lower[half:, :half],), top, NN) for lower, top in zip(lowers, tops)]
    corners = [
        halves(-mul_halves(bottom, halves(middle), NN)) for bottom, middle in zip(bottoms, middles)
    ]
    return zip(tops, corners, bottoms)


def shifted_down(rows, before, by):
    if by == 0:
        return rows
    rolled = pltpu.roll(rows, by, 0)
    top = pltpu.roll(before, by, 0)
    index = lax.broadcasted_iota(jnp.int32, before.shape, 0)
    first = jnp.where(index < by, top, rolled[: before.shape[0]])
    return jnp.concatenate([first, rolled[before.shape[0] :]], axis=0)


def shifted_up(rows, by):
    if by == 0:
        return rows
    count = rows.shape[0]
    index = lax.broadcasted_iota(jnp.int32, rows.shape, 0)
    return jnp.where(index < count - by, pltpu.roll(rows, count - by, 0), 0.0)


def conv_parts(rows, before, taps):
    width = taps.shape[0]
    conv = None
    for lag in range(width):
        term = taps[lag : lag + 1] * shifted_down(rows, before, width - 1 - lag)
        conv = term if conv is None else conv + term
    return conv


def unit_scale(active):
    return lax.rsqrt(jnp.sum(active * active, axis=-1, keepdims=True) + unit_eps)


def column_of(rates, head):
    index = lax.broadcasted_iota(jnp.int32, rates.shape, 1)
    return jnp.sum(jnp.where(index == head, rates, 0.0), axis=1, keepdims=True)


def forward_kernel(
    q_ref, k_ref, v_ref, qt_ref, kt_ref, vt_ref, rates_ref,
    high_ref, rest_ref, updates_ref, weights_ref, reach_ref, mixed_ref, transfer_ref, offset_ref,
):
    depth = transfer_ref.shape[-1]
    size = q_ref.shape[1] - LEAD
    half = size // 2
    first = pl.program_id(1) * PAIR
    row = lax.broadcasted_iota(jnp.int32, (size, size), 0)
    col = lax.broadcasted_iota(jnp.int32, (size, size), 1)
    strict = row > col
    lower = row >= col
    small_row = lax.broadcasted_iota(jnp.int32, (depth, depth), 0)
    small_col = lax.broadcasted_iota(jnp.int32, (depth, depth), 1)
    small_eye = jnp.where(small_row == small_col, 1.0, 0.0)
    systems, queries, keys, values, columns = [], [], [], [], []
    for h in range(PAIR):
        lanes = slice(h * depth, (h + 1) * depth)

        def active(ref, taps):
            rows = ref[0, :, lanes].astype(F32)
            conv = conv_parts(rows[LEAD:], rows[LEAD - 8 : LEAD], taps[:, lanes].astype(F32))
            return conv * jax.nn.sigmoid(conv)

        q = active(q_ref, qt_ref)
        k = active(k_ref, kt_ref)
        v = active(v_ref, vt_ref)
        q = (q * unit_scale(q) * depth ** (-0.5)).astype(BF16)
        k = (k * unit_scale(k)).astype(BF16)
        queries.append(q)
        keys.append(k)
        values.append(v.astype(BF16))
        columns.append(column_of(rates_ref[0, LEAD:], first + h))
        systems.append(jnp.where(strict, columns[h] * mul(k, k, NT), 0.0).astype(BF16))
    zero = jnp.zeros((half, half), BF16)
    for h, (top, corner, bottom) in enumerate(unit_lower_inverses(systems)):
        inverse = [
            jnp.concatenate(
                [jnp.concatenate([a, zero], axis=1), jnp.concatenate([b, c], axis=1)], axis=0
            )
            for a, b, c in zip(top, corner, bottom)
        ]
        high_ref[0, h] = inverse[0]
        rest_ref[0, h] = inverse[1]
        joined = jnp.concatenate([values[h], keys[h]], axis=1).astype(F32) * columns[h]
        solved = mul_halves(inverse, halves(joined), NN).astype(BF16)
        updates_ref[0, h] = solved[:, :depth]
        weights_ref[0, h] = solved[:, depth:]
        scores = jnp.where(lower, mul(queries[h], keys[h], NT), 0.0)
        seen = mul(scores.astype(BF16), solved, NN)
        lanes = slice(h * depth, (h + 1) * depth)
        mixed_ref[0, :, lanes] = seen[:, :depth]
        reach_ref[0, :, lanes] = (queries[h].astype(F32) - seen[:, depth:]).astype(BF16)
        moved = mul(keys[h], solved, TN)
        offset_ref[0, h] = moved[:, :depth]
        transfer_ref[0, h] = small_eye - moved[:, depth:]


def cost(microseconds):
    return pl.CostEstimate(flops=int(microseconds * 3.0e7), bytes_accessed=2**20, transcendentals=0)


def specs_of(model, depth, size, width, base=0, seq=None):
    wide = PAIR * depth
    blocks = model // wide

    def three(rows, batched):
        def index(part, s, g):
            if not batched:
                return (0, part * blocks + base + g)
            return (s if seq is None else seq, 0, (base + g) * 3 + part)

        block = (1, rows, wide) if batched else (rows, wide)
        return [pl.BlockSpec(block, functools.partial(index, part)) for part in range(3)]

    return three(LEAD + size, True) + three(width, False), wide


def forward_parts(projected, taps, rates, depth):
    seqs, size, _ = projected.shape
    size -= LEAD
    model = HEADS * depth
    token_specs, wide = specs_of(model, depth, size, taps.shape[0])
    rate_spec = pl.BlockSpec((1, LEAD + size, HEADS), lambda s, g: (s, 0, 0))

    def out(kind, *dims):
        return pl.BlockSpec((1, PAIR) + dims, lambda s, g: (s, g, 0, 0)), jax.ShapeDtypeStruct((seqs, HEADS) + dims, kind)

    def flat(kind):
        return pl.BlockSpec((1, size, wide), lambda s, g: (s, 0, g)), jax.ShapeDtypeStruct((seqs, size, model), kind)

    outs = [out(BF16, size, size), out(BF16, size, size), out(BF16, size, depth), out(BF16, size, depth)]
    outs += [flat(BF16), flat(F32), out(F32, depth, depth), out(F32, depth, depth)]
    return pl.pallas_call(
        forward_kernel,
        grid=(seqs, HEADS // PAIR),
        in_specs=token_specs + [rate_spec],
        out_specs=[o[0] for o in outs],
        out_shape=[o[1] for o in outs],
        compiler_params=pltpu.CompilerParams(vmem_limit_bytes=56 * 2**20),
        cost_estimate=cost(25),
        name="delta_forward",
    )(projected, projected, projected, taps, taps, taps, rates)


def backward_kernel(
    base, fresh, q_ref, k_ref, v_ref, qt_ref, kt_ref, vt_ref, rates_ref,
    high_ref, rest_ref, updates_ref, weights_ref, state_ref, grad_ref, leaving_ref, *refs
):
    rows_ref, last_ref, prior_ref, taps_ref = refs[0 if fresh else 4 :]
    depth = state_ref.shape[-1]
    size = q_ref.shape[1] - LEAD
    first = base * PAIR
    row = lax.broadcasted_iota(jnp.int32, (size, size), 0)
    col = lax.broadcasted_iota(jnp.int32, (size, size), 1)
    strict = row > col
    lower = row >= col
    index8 = lax.broadcasted_iota(jnp.int32, (8, depth), 0)
    lane = lax.broadcasted_iota(jnp.int32, (size, 128), 1)
    logits = jnp.zeros((size, 128), F32)
    for h in range(PAIR):
        lanes = slice(h * depth, (h + 1) * depth)

        def load(ref, taps):
            rows = ref[0, :, lanes].astype(F32)
            return rows[LEAD:], rows[LEAD - 8 : LEAD], taps[:, lanes].astype(F32)

        def active(parts):
            conv = conv_parts(*parts)
            gate = jax.nn.sigmoid(conv)
            return conv, gate, conv * gate

        raw = [load(q_ref, qt_ref), load(k_ref, kt_ref), load(v_ref, vt_ref)]
        acts = [active(parts) for parts in raw]
        q_scale = unit_scale(acts[0][2])
        k_scale = unit_scale(acts[1][2])
        q = (acts[0][2] * q_scale * depth ** (-0.5)).astype(BF16)
        k = (acts[1][2] * k_scale).astype(BF16)
        v = acts[2][2].astype(BF16)
        column = column_of(rates_ref[0, LEAD:], first + h)
        inverse = (high_ref[0, h], rest_ref[0, h])
        state = state_ref[0, h]
        grad = grad_ref[0, :, lanes]
        leaving = leaving_ref[0, h]
        gram = jnp.where(strict, mul(k, k, NT), 0.0).astype(BF16)
        scores = jnp.where(lower, mul(q, k, NT), 0.0).astype(BF16)
        errors = (updates_ref[0, h].astype(F32) - mul(weights_ref[0, h], state, NN)).astype(BF16)
        missed = v.astype(F32) - mul(k, state, NN) - mul(gram, errors, NN)
        grad_errors = mul(scores, grad, TN) + mul(k, leaving, NN)
        grad_right = mul_halves(inverse, halves(grad_errors), TN)
        low_right = grad_right.astype(BF16)
        grad_scores = jnp.where(lower, mul(grad, errors, NT), 0.0).astype(BF16)
        grad_system = (jnp.where(strict, -mul(low_right, errors, NT), 0.0) * column).astype(BF16)
        grad_v = grad_right * column
        grad_q = mul(grad, state, NT) + mul(grad_scores, k, NN)
        grad_k = (
            mul(grad_scores, q, TN)
            + mul(errors, leaving, NT)
            - mul(grad_v.astype(BF16), state, NT)
            + mul(grad_system, k, NN)
            + mul(grad_system, k, TN)
        )
        grad_rate = jnp.sum(grad_right * missed, axis=1, keepdims=True)
        grad_logit = grad_rate * column * (1.0 - column)
        logits = jnp.where(lane == first + h, grad_logit, logits)
        q_un, k_un = acts[0][2], acts[1][2]
        grad_q = (
            q_scale * grad_q
            - q_un * (q_scale * q_scale * q_scale * jnp.sum(grad_q * q_un, axis=1, keepdims=True))
        ) * depth ** (-0.5)
        grad_k = k_scale * grad_k - k_un * (
            k_scale * k_scale * k_scale * jnp.sum(grad_k * k_un, axis=1, keepdims=True)
        )
        for part, grad_act in enumerate((grad_q, grad_k, grad_v)):
            conv, gate, _ = acts[part]
            rows, before, taps = raw[part]
            width = taps.shape[0]
            grad_conv = grad_act * (gate * (1.0 + conv * (1.0 - gate)))
            total = None
            ahead = None
            spot = slice((part * PAIR + h) * depth, (part * PAIR + h + 1) * depth)
            for lag in range(width):
                by = width - 1 - lag
                tap = taps[lag : lag + 1]
                term = tap * shifted_up(grad_conv, by)
                total = term if total is None else total + term
                at = (part * PAIR + h) * width + lag
                taps_ref[0, at : at + 1] = jnp.sum(
                    grad_conv * shifted_down(rows, before, by), axis=0, keepdims=True
                )
                if by:
                    early = jnp.where(index8 >= 8 - by, tap * pltpu.roll(grad_conv[:8], 8 - by, 0), 0.0)
                    ahead = early if ahead is None else ahead + early
            rows_ref[0, LEAD:, spot] = total.astype(BF16)
            rows_ref[0, :LEAD, spot] = jnp.concatenate([jnp.zeros_like(ahead), ahead], axis=0).astype(BF16)
            last_ref[0, :, spot] = total[size - 8 :]
            prior_ref[0, :, spot] = ahead
    end = slice(3 * PAIR * depth, 3 * PAIR * depth + 128)
    rows_ref[0, LEAD:, end] = logits.astype(BF16)
    rows_ref[0, :LEAD, end] = jnp.zeros((LEAD, 128), BF16)


def backward_parts(seq, base, held, projected, taps, rates, high, rest, updates, weights, state, grad, leaving, depth):
    seqs, size, _ = projected.shape
    size -= LEAD
    model = HEADS * depth
    width = taps.shape[0]
    token_specs, wide = specs_of(model, depth, size, width, base, seq)
    rate_spec = pl.BlockSpec((1, LEAD + size, HEADS), lambda s, g: (seq, 0, 0))

    def heads(*dims):
        return pl.BlockSpec((1, PAIR) + dims, lambda s, g: (seq, base, 0, 0))

    def out(rows, kind, more=0):
        columns = 3 * wide + more
        return pl.BlockSpec((1, rows, columns), lambda s, g: (seq, 0, 0)), jax.ShapeDtypeStruct((seqs, rows, columns), kind)

    tap_rows = 3 * PAIR * width
    taps_out = pl.BlockSpec((1, tap_rows, depth), lambda s, g: (seq, 0, 0)), jax.ShapeDtypeStruct((seqs, tap_rows, depth), F32)
    outs = [out(LEAD + size, BF16, 128), out(8, F32), out(8, F32), taps_out]
    in_specs = token_specs + [rate_spec, heads(size, size), heads(size, size), heads(size, depth), heads(size, depth), heads(depth, depth), pl.BlockSpec((1, size, wide), lambda s, g: (seq, 0, base)), heads(depth, depth)]
    count = len(in_specs)
    return pl.pallas_call(
        functools.partial(backward_kernel, base, not held),
        grid=(1, 1),
        in_specs=in_specs + [pl.BlockSpec(memory_space=pl.ANY)] * len(held),
        out_specs=[o[0] for o in outs],
        out_shape=[o[1] for o in outs],
        input_output_aliases={count + i: i for i in range(len(held))},
        compiler_params=pltpu.CompilerParams(vmem_limit_bytes=56 * 2**20),
        cost_estimate=cost(10),
        name="delta_backward",
    )(projected, projected, projected, taps, taps, taps, rates, high, rest, updates, weights, state, grad, leaving, *held)


def mix_kernel(alone_ref, reach_ref, state_ref, gain_ref, mixed_ref, low_ref):
    depth = state_ref.shape[-1]
    for h in range(PAIR):
        lanes = slice(h * depth, (h + 1) * depth)
        mixed = alone_ref[0, :, lanes] + mul(reach_ref[0, :, lanes], state_ref[0, h], NN)
        scale = lax.rsqrt(jnp.mean(mixed * mixed, axis=-1, keepdims=True) + norm_eps)
        mixed_ref[0, :, lanes] = mixed
        low_ref[0, :, lanes] = (mixed * scale * gain_ref[...]).astype(BF16)


def mix(alone, reach, state, gain):
    seqs, size, model = alone.shape
    depth = state.shape[-1]
    wide = PAIR * depth
    flat = pl.BlockSpec((1, size, wide), lambda s, g: (s, 0, g))
    return pl.pallas_call(
        mix_kernel,
        grid=(seqs, HEADS // PAIR),
        in_specs=[flat, flat, pl.BlockSpec((1, PAIR, depth, depth), lambda s, g: (s, g, 0, 0)), pl.BlockSpec((1, depth), lambda s, g: (0, 0))],
        out_specs=[flat, flat],
        out_shape=[jax.ShapeDtypeStruct(alone.shape, F32), jax.ShapeDtypeStruct(alone.shape, BF16)],
        cost_estimate=cost(5),
        name="mix_heads",
    )(alone, reach, state, gain.reshape(1, depth))


def mix_back_kernel(mixed_ref, reach_ref, gain_ref, grad_ref, back_ref, local_ref, out_ref):
    depth = local_ref.shape[-1]
    total = None
    for h in range(PAIR):
        lanes = slice(h * depth, (h + 1) * depth)
        mixed = mixed_ref[0, :, lanes]
        grad = grad_ref[0, :, lanes].astype(F32)
        scale = lax.rsqrt(jnp.mean(mixed * mixed, axis=-1, keepdims=True) + norm_eps)
        weighted = grad * gain_ref[...]
        part = jnp.sum(grad * mixed * scale, axis=0, keepdims=True)
        total = part if total is None else total + part
        back = scale * weighted - mixed * (scale * scale * scale) * (
            jnp.mean(weighted * mixed, axis=-1, keepdims=True)
        )
        back = back.astype(BF16)
        back_ref[0, :, lanes] = back
        local_ref[0, h] = mul(reach_ref[0, :, lanes], back, TN)
    out_ref[0, 0] = jnp.broadcast_to(total, out_ref.shape[2:])


def mix_back(mixed, reach, gain, grad):
    seqs, size, model = mixed.shape
    depth = gain.size
    wide = PAIR * depth
    flat = pl.BlockSpec((1, size, wide), lambda s, g: (s, 0, g))
    back, local, total = pl.pallas_call(
        mix_back_kernel,
        grid=(seqs, HEADS // PAIR),
        in_specs=[flat, flat, pl.BlockSpec((1, depth), lambda s, g: (0, 0)), flat],
        out_specs=[flat, pl.BlockSpec((1, PAIR, depth, depth), lambda s, g: (s, g, 0, 0)), pl.BlockSpec((1, 1, 8, depth), lambda s, g: (s, g, 0, 0))],
        out_shape=[
            jax.ShapeDtypeStruct(mixed.shape, BF16),
            jax.ShapeDtypeStruct((seqs, HEADS, depth, depth), F32),
            jax.ShapeDtypeStruct((seqs, HEADS // PAIR, 8, depth), F32),
        ],
        cost_estimate=cost(6),
        name="mix_heads_back",
    )(mixed, reach, gain.reshape(1, depth), grad)
    return back, local, jnp.sum(total[:, :, 0], axis=(0, 1))


def pack_kernel(mixer_ref, ffn_ref, early_ref, late_ref, rest_ref, out_ref):
    at = 0
    for ref in (mixer_ref, ffn_ref, early_ref, late_ref, rest_ref):
        value = ref[...]
        if len(value.shape) == 3:
            value = jnp.sum(value, axis=0)
        out_ref[at : at + value.shape[0]] = value
        at += value.shape[0]


def packed(*pieces):
    rows = sum(piece.shape[-2] for piece in pieces)
    return pl.pallas_call(
        pack_kernel, out_shape=jax.ShapeDtypeStruct((rows, 128), F32), cost_estimate=cost(2), name="pack_sums"
    )(*pieces)


BOTH = ("dp", "cp")


class Grid:
    def __init__(self):
        self.cp = lax.axis_size("cp")
        group = lax.axis_size("dp")
        self.core = 2 if group % 2 == 0 else 1
        self.lo = 2 if group // self.core % 2 == 0 else 1
        self.hi = group // self.core // self.lo
        self.sizes = (self.hi, self.lo, self.core, self.cp)

    def place(self):
        member = lax.axis_index("dp")
        return (
            member // (self.lo * self.core),
            member // self.core % self.lo,
            member % self.core,
            lax.axis_index("cp"),
        )

    def swap(self, value, axis, by):
        step = [1] * 4
        for later in range(3):
            step[2 - later] = step[3 - later] * self.sizes[3 - later]
        pairs = []
        for device in range(step[0] * self.sizes[0]):
            here = device // step[axis] % self.sizes[axis]
            pairs.append((device, device + ((here ^ by) - here) * step[axis]))
        return lax.ppermute(value, BOTH, pairs)

    def others(self, value, axis):
        return [self.swap(value, axis, by) for by in range(1, self.sizes[axis])]


HI, LO, CORE, SEG = range(4)


def cut_of(columns):
    return columns // 256 * 128


def place_kernel(cuts, spot, own_left, own_right, other_left, other_right, *outs):
    core, seg = spot[2], spot[3]
    for away, left, right in ((0, own_left, own_right), (1, other_left, other_right)):
        if away >= outs[0].shape[2]:
            continue
        cut = left.shape[-1]
        for at in range(left.shape[2]):
            for out, (top, bottom, first, last) in zip(outs, cuts):
                for source, start in ((left, 0), (right, cut)):
                    low, high = max(first, start), min(last, start + source.shape[-1])
                    if low < high:
                        out[0, 0, core ^ away, at, :, low - first : high - first] = source[
                            0, 0, at ^ seg, top:bottom, low - start : high - start
                        ]


def tied(value, *needed):
    return lax.optimization_barrier((value, needed))[0] if needed else value


class Gather:
    def __init__(self, grid, shard, at_once=False):
        self.grid = grid
        self.shape = shard.shape
        self.cut = cut_of(shard.shape[1])
        self.mine = shard
        self.sent = [shard]
        self.at_once = at_once
        if at_once:
            all_of = lax.all_to_all(jnp.stack([shard] * grid.cp), "cp", 0, 0)
            self.got = [all_of]
        else:
            self.got = grid.others(shard, SEG)

    def exchange(self, axes):
        self.got = [self.grid.others(piece, axis) for piece, axis in zip(self.sent, axes)]

    def first(self, *needed):
        parts = tied([self.mine] + self.got, *needed)
        if self.at_once:
            here = self.grid.place()[SEG]
            parts = [pick(parts[1], here ^ by, 0) for by in range(self.grid.cp)]
        self.sent = [
            jnp.stack([part[:, : self.cut] for part in parts]),
            jnp.stack([part[:, self.cut :] for part in parts]),
        ]
        self.exchange((LO, HI))

    def second(self, *needed):
        sent, got = tied((self.sent, self.got), *needed)
        self.sent = [jnp.stack([piece] + more) for piece, more in zip(sent, got)]
        self.exchange((HI, LO))

    def third(self, *needed):
        sent, got = tied((self.sent, self.got), *needed)
        self.own = [
            jnp.stack([piece] + more, axis=axis)
            for piece, more, axis in zip(sent, got, (0, 1))
        ]
        self.sent = self.own
        self.other = [
            self.grid.swap(piece, CORE, 1) if self.grid.core == 2 else piece for piece in self.own
        ]

    def placed(self, cuts, *needed):
        grid, (r, total), cut = self.grid, self.shape, self.cut
        own, other = tied((self.own, self.other), *needed)

        def source(wide):
            return pl.BlockSpec(
                (1, 1, grid.cp, r, wide), lambda a, b, spot: (a ^ spot[0], b ^ spot[1], 0, 0, 0)
            )

        shapes = [(bottom - top, right - left) for top, bottom, left, right in cuts]
        sources = [source(cut), source(total - cut)]
        outs = pl.pallas_call(
            functools.partial(place_kernel, cuts),
            grid_spec=pltpu.PrefetchScalarGridSpec(
                num_scalar_prefetch=1,
                grid=(grid.hi, grid.lo),
                in_specs=sources + sources,
                out_specs=[
                    pl.BlockSpec((1, 1, grid.core, grid.cp) + shape, lambda a, b, spot: (a, b, 0, 0, 0, 0))
                    for shape in shapes
                ],
            ),
            out_shape=[jax.ShapeDtypeStruct(grid.sizes + shape, BF16) for shape in shapes],
            cost_estimate=cost(14),
            name="place_rows",
        )(jnp.stack(grid.place()), *own, *other)
        return [out.reshape(-1, out.shape[-1]) for out in outs]


class Share:
    def __init__(self, grid, values=None, keep=None, send=None):
        self.grid = grid
        self.spots = grid.place()
        self.halved = values is None
        self.stacked = False
        if self.halved:
            self.spots = (0, 0, 0, self.spots[SEG])
        else:
            core = self.spots[2]
            values = [value.reshape(grid.sizes + (-1, value.shape[-1])) for value in values]

            keep = [pick(value, core, 2) for value in values]
            send = [pick(value, core ^ 1, 2) for value in values]
        self.sent = send
        self.terms = [
            [k, grid.swap(s, CORE, 1)] if grid.core == 2 else [k] for k, s in zip(keep, send)
        ]

    def begin(self, *moves):
        self.terms = []
        self.sent = []
        self.got = []
        for array, axis, dim in moves:
            here = self.spots[axis]
            mine = pick(array, here, dim)
            sent = [pick(array, here ^ by, dim) for by in range(1, self.grid.sizes[axis])]
            got = [self.grid.swap(term, axis, by + 1) for by, term in enumerate(sent)]
            self.sent += sent
            self.got += got
            self.terms.append([mine] + got)

    def summed(self, *needed):
        return [total_of(terms).astype(BF16) for terms in tied(self.terms, *needed)]

    def first(self, *needed):
        totals = self.summed(*needed)
        if self.halved:
            left, right = totals
            self.begin((left, LO, 0), (right, HI, 0))
        else:
            value = totals[0] if len(totals) == 1 else jnp.concatenate(totals, axis=-2)
            cut = cut_of(value.shape[-1])
            self.begin((value[..., :cut], LO, 1), (value[..., cut:], HI, 0))

    def second(self, *needed):
        left, right = self.summed(*needed)
        self.begin((left, HI, 0), (right, LO, 0))

    def ready(self, *needed, more=()):
        halved = self.summed(*needed)
        for put in more:
            halved = halved + put.summed(*needed)
        self.total = jnp.concatenate(halved, axis=-1)

    def third(self, *needed):
        self.begin((tied(self.total, *needed), SEG, 0))

    def third_at_once(self, *needed):
        self.terms = [[lax.all_to_all(tied(self.total, *needed), "cp", 0, 0)]]
        self.stacked = True

    def result(self, *needed):
        terms = tied(self.terms[0], *needed)
        if self.stacked:
            terms = [terms[0][i] for i in range(self.grid.cp)]
        return total_of(terms)


def total_of(terms):
    total = terms[0].astype(F32)
    for term in terms[1:]:
        total = total + term.astype(F32)
    return total


def pick(array, index, dim):
    if isinstance(index, int):
        return lax.index_in_dim(array, index, dim, keepdims=False)
    return lax.dynamic_index_in_dim(array, index, dim, keepdims=False)


def all_sum(grid, value, across, along):
    for axis in (CORE, LO, HI, SEG):
        by = 1
        while by < grid.sizes[axis]:
            if axis == SEG:
                value = tied(value, *(across if by == 1 else along))
            value = value + grid.swap(value, axis, by)
            by *= 2
    return value


def natural_rows(grid, spot, own, other):
    rows = []
    for a in range(grid.hi):
        for b in range(grid.lo):
            for k in range(grid.core):
                for c in range(grid.cp):
                    index = (a ^ spot[0], b ^ spot[1], c ^ spot[3])
                    mine, theirs = own[index], other[index]
                    rows.append(jnp.where(spot[2] == k, mine, theirs))
    return jnp.concatenate(rows, axis=0)


def scatter_rows(grid, spot, value, keep, send, flip):
    r = keep.shape[-2]
    for a in range(grid.hi):
        for b in range(grid.lo):
            for c in range(grid.cp):
                index = (a ^ spot[0], b ^ spot[1], c)
                if flip:
                    index = (index[1], index[0], index[2])
                at = ((a * grid.lo + b) * grid.core * grid.cp + c) * r
                lower = value[at : at + r]
                at += grid.cp * r
                upper = value[at : at + r]
                keep[index] = jnp.where(spot[2] == 0, lower, upper)
                send[index] = jnp.where(spot[2] == 0, upper, lower)


def feed_kernel(
    grid, spot, rows_ref, flipped_ref, cot_ref, og_ref, ou_ref, tg_ref, tu_ref, down_ref,
    out_ref, back_ref, grad_down_ref, kg_ref, sg_ref, ku_ref, su_ref,
):
    tile = down_ref.shape[0]

    @pl.when(pl.program_id(0) == 0)
    def _():
        out_ref[...] = jnp.zeros(out_ref.shape, F32)
        back_ref[...] = jnp.zeros(back_ref.shape, F32)

    cot, down = cot_ref[...], down_ref[...]
    both = jnp.concatenate(
        [natural_rows(grid, spot, og_ref, tg_ref), natural_rows(grid, spot, ou_ref, tu_ref)], axis=1
    )
    gates = mul(rows_ref[...], both, NN)
    grad_hidden = mul(cot, down, NT)
    gate, up = gates[:, :tile], gates[:, tile:]
    sigma = jax.nn.sigmoid(gate)
    act = gate * sigma
    hidden = (act * up).astype(BF16)
    grad_gate = grad_hidden * up * (sigma * (1.0 + gate * (1.0 - sigma)))
    grads = jnp.concatenate([grad_gate.astype(BF16), (grad_hidden * act).astype(BF16)], axis=1)
    out_ref[...] += mul(hidden, down, NN)
    back_ref[...] += mul(grads, both, NT)
    grad_down_ref[...] = mul(hidden, cot, TN).astype(BF16)
    share = mul(flipped_ref[...], grads, NN)
    scatter_rows(grid, spot, share[:, :tile].astype(BF16), kg_ref, sg_ref, True)
    scatter_rows(grid, spot, share[:, tile:].astype(BF16), ku_ref, su_ref, False)


def feed_forward(grid, rows, cot, gather, w_down):
    tokens, model = rows.shape
    half = w_down.shape[0]
    tile = 256
    r = gather.shape[0]
    lead = (grid.hi, grid.lo, grid.cp, r)
    whole = pl.BlockSpec((tokens, model), lambda j, spot: (0, 0))
    piece = pl.BlockSpec(lead + (tile,), lambda j, spot: (0, 0, 0, 0, j))
    down = pl.BlockSpec((tile, model), lambda j, spot: (j, 0))
    turned = (grid.lo, grid.hi, grid.cp, r)
    left = pl.BlockSpec(turned + (tile,), lambda j, spot: (0, 0, 0, 0, j))
    share = [jax.ShapeDtypeStruct(turned + (half,), BF16)] * 2 + [jax.ShapeDtypeStruct(lead + (half,), BF16)] * 2
    out, back, grad_down, kg, sg, ku, su = pl.pallas_call(
        functools.partial(feed_kernel, grid),
        grid_spec=pltpu.PrefetchScalarGridSpec(
            num_scalar_prefetch=1,
            grid=(half // tile,),
            in_specs=[whole, pl.BlockSpec((model, tokens), lambda j, spot: (0, 0)), whole] + [piece] * 4 + [down],
            out_specs=[whole, whole, down, left, left, piece, piece],
        ),
        out_shape=[
            jax.ShapeDtypeStruct((tokens, model), F32),
            jax.ShapeDtypeStruct((tokens, model), F32),
            jax.ShapeDtypeStruct((half, model), BF16),
            *share,
        ],
        compiler_params=pltpu.CompilerParams(vmem_limit_bytes=58 * 2**20),
        cost_estimate=cost(33),
        name="feed_forward",
    )(jnp.stack(grid.place()), rows, rows.T, cot, *gather.own, *gather.other, w_down)
    return out, back, grad_down, (kg, ku), (sg, su)


def passed_along(value, axis, by):
    peers = lax.axis_size(axis)
    pairs = [(i, i + by) for i in range(peers) if 0 <= i + by < peers]
    return lax.ppermute(value, axis, pairs)


def apply_map(transfer, state, offset):
    return jnp.einsum("shij,shjk->shik", transfer, state, precision=lax.Precision.HIGH) + offset


def rows_times(left, right):
    return jnp.einsum("sga,ab->sgb", left, right, preferred_element_type=F32)


def rows_back(grad, weight):
    return jnp.einsum("sgb,ab->sga", grad, weight, preferred_element_type=F32)


def weight_grad(left, right):
    return jnp.einsum("sga,sgb->ab", left, right, preferred_element_type=F32)


def norm_back(rows, scale, gain, grad):
    weighted = grad * gain
    gain_grad = jnp.sum(grad * rows * scale, axis=tuple(range(rows.ndim - 1)))
    width = rows.shape[-1]
    row_grad = scale * weighted - rows * scale**3 * (
        jnp.sum(weighted * rows, axis=-1, keepdims=True) / width
    )
    return (gain_grad, row_grad)


def per_device(
    block_input, mixer_gain, qkv_weight, conv_taps, beta_weight, out_gain,
    proj_weight, ffn_gain, gate_up, down_weight, cotangent,
):
    seqs, seg_len, model = block_input.shape
    width = conv_taps.shape[0]
    depth = model // HEADS
    peers = lax.axis_size(BOTH)
    share = model // peers
    tap_share = conv_taps.shape[1]
    hops = lax.axis_size("cp") - 1
    grid = Grid()

    ahead = passed_along(block_input[:, seg_len - LEAD :], "cp", 1)
    even = -(-share // 16) * 16
    down_share = down_weight.shape[0]
    mats = jnp.concatenate([jnp.pad(proj_weight, ((0, even - share), (0, 0))), down_weight], axis=0)
    small = jnp.concatenate(
        [beta_weight, mixer_gain[:, None], ffn_gain[:, None], conv_taps.reshape(share, -1)], axis=1
    )
    small = jnp.pad(small, ((0, 0), (0, 128 - small.shape[1])))
    wide = PAIR * depth
    groups = HEADS // PAIR
    columns = [
        qkv_weight[:, part * model + base * wide : part * model + (base + 1) * wide]
        for base in range(groups)
        for part in range(3)
    ]
    get_qkv = Gather(grid, jnp.concatenate(columns + [small], axis=1))
    get_gateup = Gather(grid, tied(gate_up, *get_qkv.got), True)
    get_qkv.first(ahead)
    get_qkv.second()
    get_mats = Gather(grid, tied(mats, get_qkv.got))
    get_qkv.third()
    get_gateup.first(*get_qkv.own)
    wide_qkv = 3 * model + 128
    w_qkv, small = get_qkv.placed(
        ((0, share, 0, wide_qkv), (0, share, 3 * model, wide_qkv)), *get_gateup.sent
    )
    gain_one = small[:, HEADS]
    gain_two = small[:, HEADS + 1]
    taps = small[:, HEADS + 2 : HEADS + 2 + width * tap_share // share].reshape(peers, width, tap_share)
    taps = jnp.swapaxes(taps, 0, 1).reshape(width, peers * tap_share)

    gain_outf = out_gain.astype(F32)
    resid_in = block_input.astype(F32)
    scale_one = lax.rsqrt(jnp.mean(resid_in * resid_in, axis=-1, keepdims=True) + norm_eps)
    extended = jnp.concatenate([ahead, block_input], axis=1).astype(F32)
    scale = lax.rsqrt(jnp.mean(extended * extended, axis=-1, keepdims=True) + norm_eps)
    normed_one = (extended * scale * gain_one.astype(F32)).astype(BF16)
    projected = rows_times(normed_one, w_qkv).astype(BF16)
    rates = jax.nn.sigmoid(rows_times(normed_one, small)[..., :HEADS])
    get_gateup.second(projected)
    get_mats.first(projected, *get_gateup.sent)
    projected = tied(projected, *get_gateup.sent, *get_mats.sent)
    high, rest, updates, weights, reach, alone, transfer, offset = forward_parts(
        projected, taps, rates, depth
    )
    carried = jnp.zeros(offset.shape, BF16)
    for step in range(hops):
        sent = offset if step == 0 else apply_map(transfer, carried.astype(F32), offset)
        sent = sent.astype(BF16)
        carried = passed_along(sent, "cp", 1)
        if step == 0:
            get_mats.second(sent)
            get_gateup.third(sent, *get_mats.sent)
            carried = tied(carried, *get_mats.sent, *get_gateup.sent)
        if step == 2:
            get_mats.third(sent)
            w_proj, w_down = get_mats.placed(((0, share, 0, model), (even, even + down_share, 0, model)), sent)
            carried = tied(carried, w_down, w_proj)
    mixed, mixed_low = mix(alone, reach, carried, gain_outf)

    attn = rows_times(mixed_low, w_proj)
    middle = resid_in + attn
    scale_two = lax.rsqrt(jnp.mean(middle * middle, axis=-1, keepdims=True) + norm_eps)
    gain_twof = gain_two.astype(F32)
    normed_two = (middle * scale_two * gain_twof).astype(BF16)
    tokens = seqs * seg_len
    ffn_out, grad_normed_two, grad_down, keep, send = feed_forward(
        grid, normed_two.reshape(tokens, model), cotangent.reshape(tokens, model), get_gateup, w_down
    )
    ffn_out = ffn_out.reshape(middle.shape)
    put_gateup = Share(grid, keep=keep, send=send)
    result = middle + ffn_out
    squares = jnp.stack(
        [jnp.sum(result * result), jnp.sum(attn * attn), jnp.sum(ffn_out * ffn_out)]
    )
    upstream = cotangent.astype(F32)
    grad_normed_two = grad_normed_two.reshape(middle.shape)
    grad_ffn, grad_from_norm = norm_back(middle, scale_two, gain_twof, grad_normed_two)
    grad_middle = upstream + grad_from_norm
    grad_attn = grad_middle.astype(BF16)
    grad_proj = weight_grad(mixed_low, grad_attn).astype(BF16)
    grad_normed_mix = rows_back(tied(grad_attn, grad_proj), w_proj).astype(BF16)

    grad_mixed, local_part, grad_out = mix_back(mixed, reach, gain_outf, grad_normed_mix)
    flipped = jnp.swapaxes(transfer, -1, -2)
    incoming = jnp.zeros(local_part.shape, BF16)
    for step in range(hops):
        sent = local_part if step == 0 else apply_map(flipped, incoming.astype(F32), local_part)
        sent = sent.astype(BF16)
        incoming = passed_along(sent, "cp", -1)
        if step == 0:
            put_gateup.first(sent)
            incoming = tied(incoming, *put_gateup.sent)
        if step == 1:
            put_mats = Share(grid, tied([grad_proj, grad_down], sent))
            incoming = tied(incoming, *put_mats.sent)
        if step == 2:
            extras = jnp.pad(jnp.concatenate([squares, grad_out]), (0, 256 - 3 - depth)).reshape(2, 128)
            put_mats.first(sent)
            incoming = tied(incoming, extras, grad_ffn, *put_mats.sent)
    puts = []
    arrays = (projected, taps, rates, high, rest, updates, weights, carried, grad_mixed)

    for base in range(HEADS // PAIR):
        held = ()
        for seq in range(seqs):
            held = backward_parts(seq, base, held, *arrays, incoming, depth)
            if (base, seq) == (0, 0):
                put_gateup.second(held[0])
                incoming = tied(incoming, *put_gateup.sent)
            if (base, seq) == (0, seqs - 1):
                kept = held
                put_mats.second(held[0])
                puts.append(Share(grid, [weight_grad(normed_one, held[0]).astype(BF16)]))
                incoming = tied(incoming, *put_mats.sent, *puts[0].sent)
            if (base, seq) == (1, 0):
                put_gateup.ready(held[0])
                put_gateup.third_at_once()
                put_mats.ready(held[0])
                puts[0].first(held[0])
                incoming = tied(incoming, put_gateup.total, put_mats.total, *puts[0].sent)
    late = weight_grad(normed_one, held[0]).astype(BF16)
    puts.append(Share(grid, [late]))
    put_mats.third_at_once(held[0])
    puts[0].second(*puts[1].sent)
    kept, held = tied((kept, held), *puts[0].sent)
    last_rows = jnp.concatenate([kept[1], held[1]], axis=-1)
    returned = passed_along(jnp.concatenate([kept[2], held[2]], axis=-1), "cp", -1)
    logits = kept[0][:, LEAD:, 3 * wide :] + held[0][:, LEAD:, 3 * wide :]
    grad_projected = jnp.concatenate(
        [kept[0][:, LEAD:, : 3 * wide], held[0][:, LEAD:, : 3 * wide], logits], axis=-1
    )
    puts[1].first(grad_projected, put_gateup.terms[0][0], *puts[0].got)
    last_rows, returned = tied((last_rows, returned), *puts[1].sent)
    last_rows = last_rows + returned
    grad_projected = lax.dynamic_update_slice(grad_projected, last_rows.astype(BF16), (0, seg_len - 8, 0))
    grad_normed_one = rows_back(grad_projected, w_qkv)
    grad_mixer, grad_from_first = norm_back(resid_in, scale_one, gain_one.astype(F32), grad_normed_one)
    across = puts[1].got
    puts[1].second()
    along = puts[1].got
    grad_input = grad_middle + grad_from_first
    flat = packed(tied(grad_mixer, *across).reshape(-1, 128), grad_ffn.reshape(-1, 128), kept[3], held[3], extras)
    sums = all_sum(grid, flat, across + [put_mats.terms[0][0]], along)
    counts = [model // 128] * 2 + [6 * PAIR * width, 2]
    starts = [sum(counts[:i]) for i in range(4)]
    found = [sums[start : start + count].reshape(-1) for start, count in zip(starts, counts)]
    puts[1].ready(more=(puts[0],))
    puts[1].third()
    both = puts[1].result()
    held_columns = 3 * wide + 128
    second, first = both[:, :held_columns], both[:, held_columns:]
    share_beta = first[:, 3 * wide : 3 * wide + HEADS] + second[:, 3 * wide : 3 * wide + HEADS]
    parts = [part[:, : 3 * wide].reshape(share, 3, wide) for part in (first, second)]
    share_qkv = jnp.stack(parts, axis=2).reshape(share, 3 * model)
    grad_taps = found[2].reshape(HEADS // PAIR, 3, PAIR, width, depth)
    grad_taps = jnp.transpose(grad_taps, (3, 1, 0, 2, 4)).reshape(width, 3 * model)
    share_gateup = put_gateup.result(*puts[1].sent)
    share_mats = put_mats.result(*puts[1].sent)
    me = lax.axis_index(BOTH)

    def mine(array, count):
        return lax.dynamic_slice_in_dim(array, me * count, count, axis=-1)

    return (
        result.astype(BF16),
        grad_input,
        mine(found[0], share),
        share_qkv,
        mine(grad_taps, tap_share),
        share_beta,
        found[3][3 : 3 + depth],
        share_mats[:share],
        mine(found[1], share),
        share_gateup,
        share_mats[share:],
        jnp.sqrt(found[3][:3] / (result.size * peers)),
    )


def solution(mesh):
    both = P(BOTH)
    rows = P(BOTH, None)
    tokens = P("dp", "cp", None)
    taps = P(None, BOTH)
    in_specs = (tokens, both, rows, taps, rows, P(), rows, both, rows, rows, tokens)
    out_specs = (tokens, tokens, both, rows, taps, rows, P(), rows, both, rows, rows, P())
    return jax.shard_map(
        per_device, mesh=mesh, in_specs=in_specs, out_specs=out_specs, check_vma=False
    )
```
